32 devices in a mesh: energy: 8 (over y, x, core), slab: 4 (over z).
Axes of the slice: x: 2, y: 2, z: 4, core: 2. Of those that a mesh axis runs over, the one named last changes fastest.
Arguments:
- free_green: float32 [8, 8, 2, 256, 256], P('energy', 'slab'), may hold values from -2 to 2
- self_energy: float32 [8, 8, 2, 256, 256], P('energy', 'slab'), may hold values from -0.375 to 0.375
- coupling: float32 [8, 2, 256, 256], P('slab'), may hold values from -0.375 to 0.375
- pattern: int32 [8, 16, 16], P('slab'), may hold values 0 or 1
- offsets: int32 [4], replicated, may hold values from 1 to 7
- emission: float32 [4], replicated, may hold values from 0.2 to 1
- absorption: float32 [4], replicated, may hold values from 0.1 to 0.6
Outputs:
- retarded: float32 [8, 8, 2, 256, 256], P('energy', 'slab')
- scattering: float32 [8, 8, 2, 256, 256], P('energy', 'slab')
The draws below stay inside these ranges and needn't reach their ends.
All inputs are finite; a program needn't handle non-finite values. No bound on the sum of `pattern` on one device may be relied on, other than what follows from the above.
Results may differ from the reference program's by a relative error of at most 0.0003.
Values sent between devices are 32-bit elements; how exact they have to be, the bound alone decides.
No kernel may reach another device: no remote copies, remote signals or barrier semaphores. Data moves between devices by JAX's collectives and lax.ppermute only.
A program may use at most 64 MiB of HBM per device.

```python
import math
import jax
import jax.numpy as jnp
from jax import lax

NO = 256
NMODE = 4
NE = 8
NS = 8
NB = 16


def draw_free_green(key, part):
    key = jax.random.fold_in(key, 11)
    key_spread, key_real, key_imag = jax.random.split(key, 3)
    spread = 0.4 / math.sqrt(NO)
    full_shape = (NE, NS, 2, NO, NO)
    scatter_part = jnp.clip(jax.random.normal(key_spread, full_shape, jnp.float32), -4.0, 4.0) * spread
    diag_real = jax.random.uniform(key_real, (NE, NS, 1, NO, 1), jnp.float32, -0.6, 0.6)
    diag_imag = jax.random.uniform(key_imag, (NE, NS, 1, NO, 1), jnp.float32, -1.0, -0.4)
    identity = jnp.eye(NO, dtype=jnp.float32)
    diagonal = jnp.concatenate([diag_real, diag_imag], axis=2) * identity
    return scatter_part + diagonal


def place_ends(values, own_key, smallest, top_value):
    index_at = [jax.random.randint(jax.random.fold_in(own_key, axis), (), 0, length) for axis, length in enumerate(values.shape)]
    longest = values.shape.index(max(values.shape))
    neighbour = index_at[:longest] + [(index_at[longest] + 1) % values.shape[longest]] + index_at[longest + 1:]
    return values.at[tuple(index_at)].set(smallest).at[tuple(neighbour)].set(top_value)


def shard_levels(own_key, dims, cuts, smallest, high):
    def one(axis_at, shards_of):
        draws = jax.random.uniform(jax.random.fold_in(jax.random.fold_in(own_key, 6), axis_at), (shards_of,), jnp.float32, smallest / len(cuts), high / len(cuts))
        return jnp.repeat(jnp.exp(draws), dims[axis_at] // shards_of).reshape((-1,) + (1,) * (len(dims) - axis_at - 1))

    level = one(*cuts[0])
    for cut in cuts[1:]:
        level = level * one(*cut)
    return level


def gaussian(stream_key, extent, scale, limit, shards=(), kind=jnp.bfloat16):
    result = scale * jax.random.normal(stream_key, extent, jnp.float32)
    if shards:
        result = result * shard_levels(stream_key, extent, shards, -0.22, 0.18)
    return jnp.clip(result, -limit, limit).astype(kind)


def setup_inputs(seed: int = 0) -> dict:
    keys = jax.random.split(jax.random.key(seed), 8)
    return {
        "free_green": draw_free_green(jax.random.fold_in(keys[7], 71), 0),
        "self_energy": gaussian(keys[1], (NE, NS, 2, NO, NO), NO ** -0.5, 0.375, ((0, 8), (1, 4)), jnp.float32),
        "coupling": gaussian(keys[2], (NS, 2, NO, NO), NO ** -0.5, 0.375, ((0, 4),), jnp.float32),
        "pattern": place_ends((jax.random.randint(keys[3], (NS, NB, NB), 0, 2) < 1).astype(jnp.int32), jax.random.fold_in(keys[3], 1), 0, 1),
        "offsets": place_ends(jax.random.randint(keys[4], (NMODE,), 1, NE), jax.random.fold_in(keys[4], 1), 1, NE - 1).astype(jnp.int32),
        "emission": jnp.clip(jax.random.uniform(keys[5], (NMODE,), jnp.float32, 0.2, 1.0), 0.2, 1.0),
        "absorption": jnp.clip(jax.random.uniform(keys[6], (NMODE,), jnp.float32, 0.1, 0.6), 0.1, 0.6),
    }


def precise_product(left_matrix, right_matrix):
    return jnp.matmul(left_matrix, right_matrix, precision=lax.Precision.HIGHEST)


def complex_product(left_pair, right_pair):
    real_part = precise_product(left_pair[..., 0, :, :], right_pair[..., 0, :, :]) - precise_product(left_pair[..., 1, :, :], right_pair[..., 1, :, :])
    imag_part = precise_product(left_pair[..., 0, :, :], right_pair[..., 1, :, :]) + precise_product(left_pair[..., 1, :, :], right_pair[..., 0, :, :])
    return jnp.stack([real_part, imag_part], axis=-3)


def adjoint(pair):
    return jnp.stack([jnp.swapaxes(pair[..., 0, :, :], -1, -2), -jnp.swapaxes(pair[..., 1, :, :], -1, -2)], axis=-3)


def expand_pattern(coupling, pattern):
    number = pattern.shape[0]
    blocks = pattern.shape[1]
    orbitals = coupling.shape[-1]
    tile_size = orbitals // blocks
    tile_mask = jnp.broadcast_to(pattern[:, :, None, :, None], (number, blocks, tile_size, blocks, tile_size))
    tile_mask = tile_mask.reshape(number, orbitals, orbitals).astype(jnp.float32)
    return coupling * tile_mask[:, None, :, :]


def mode_weights(targets, sources, offsets, emission, absorption):
    spacing = sources[None, :, None] - targets[:, None, None]
    emitted = jnp.where(spacing == -offsets[None, None, :], emission[None, None, :], jnp.zeros_like(emission)[None, None, :])
    absorbed = jnp.where(spacing == offsets[None, None, :], absorption[None, None, :], jnp.zeros_like(absorption)[None, None, :])
    return jnp.sum(emitted + absorbed, axis=-1)


def reference(free_green, self_energy, coupling, pattern, offsets, emission, absorption):
    couple = expand_pattern(coupling, pattern)
    slab_count = free_green.shape[1]
    energy_count = free_green.shape[0]
    carried = jnp.zeros_like(free_green[:, 0])
    left_list = []
    for slab_index in range(slab_count):
        isolated = free_green[:, slab_index]
        coupler = couple[slab_index][None]
        forward = complex_product(isolated, coupler)
        backward = complex_product(adjoint(coupler), isolated)
        source = isolated + complex_product(complex_product(isolated, self_energy[:, slab_index]), isolated)
        carried = complex_product(complex_product(forward, carried), backward) + source
        left_list.append(carried)
    right_list = [left_list[-1]] * slab_count
    carried = left_list[-1]
    for slab_index in range(slab_count - 2, -1, -1):
        local_green = left_list[slab_index]
        coupler = couple[slab_index + 1][None]
        lower = complex_product(local_green, adjoint(coupler))
        upper = complex_product(coupler, local_green)
        carried = complex_product(complex_product(lower, carried), upper) + local_green
        right_list[slab_index] = carried
    retarded = jnp.stack(right_list, axis=1)
    everyone = jnp.arange(energy_count, dtype=jnp.int32)
    rates = mode_weights(everyone, everyone, offsets, emission, absorption)
    scattering = jnp.einsum("ef,fsxab->esxab", rates, retarded, precision=lax.Precision.HIGHEST)
    return retarded, scattering
```

```python
import functools

import jax
import jax.numpy as jnp
from jax import lax
from jax.experimental import pallas as pl
from jax.experimental.pallas import tpu as pltpu
from jax.sharding import PartitionSpec as P

F32 = jnp.float32
HALF = jnp.bfloat16
ANY = pl.BlockSpec(memory_space=pl.ANY)
VMEM = pl.BlockSpec(memory_space=pltpu.VMEM)
PARAMS = pltpu.CompilerParams(vmem_limit_bytes=40 * 2**20)


def split(value):
    high = value.astype(HALF)
    return high, (value - high.astype(F32)).astype(HALF)


def dot(left, right, transposed):
    dims = (((1,), (1 if transposed else 0,)), ((), ()))
    return lax.dot_general(left, right, dims, preferred_element_type=F32)


def put(matrix, block):
    size = block.shape[0]
    for level, part in enumerate(split(block)):
        real, imag = part[:, :size], part[:, size:]
        matrix[level, :size, :size] = real
        matrix[level, :size, size:] = imag
        matrix[level, size:, :size] = -imag
        matrix[level, size:, size:] = real


def times_split(high, low, matrix, transposed=False):
    return (
        dot(high, matrix[0], transposed)
        + dot(low, matrix[0], transposed)
        + dot(high, matrix[1], transposed)
    )


def times(block, matrix, transposed=False):
    high, low = split(block)
    return times_split(high, low, matrix, transposed)


def row_form(pair):
    return jnp.concatenate([pair[0], pair[1]], axis=1)


def adjoint_row(pair):
    return jnp.concatenate([jnp.transpose(pair[0]), -jnp.transpose(pair[1])], axis=1)


def expand(pattern, size):
    blocks = pattern.shape[0]
    tile = size // blocks
    rows = lax.broadcasted_iota(jnp.int32, (size, blocks), 0)
    first = lax.broadcasted_iota(jnp.int32, (size, blocks), 1) * tile
    member = jnp.where((rows >= first) & (rows < first + tile), 1.0, 0.0).astype(HALF)
    tall = dot(member, pattern.astype(F32).astype(HALF), False)
    return dot(tall.astype(HALF), member, True)


def couple(coupling, pattern, which, tiles=None):
    mask = expand(pattern[which if tiles is None else tiles], coupling.shape[-1])
    return [coupling[which, 0] * mask, coupling[which, 1] * mask]


def parity():
    return lax.rem(lax.axis_index("energy"), 2)


def source_kernel(green, sigma, coupling, pattern, out, source, coupler_half, m_a, m_b, m_c, m_d):
    first = row_form(green[0])
    put(m_a, row_form(sigma[0]))
    put(m_b, first)
    made = first + times(times(first, m_a), m_b)
    source[...] = made
    put(m_c, made)
    coupler = row_form(couple(coupling, pattern, 1))
    put(m_d, coupler)
    inner = row_form(sigma[1]) + times(times(coupler, m_c), m_d, True)
    put(m_a, inner)
    second = row_form(green[1])
    put(m_b, second)
    out[...] = second + times(times(second, m_a), m_b)
    opening = couple(coupling, pattern, 0)
    coupler_half[...] = jnp.where(parity() == 0, opening[0], opening[1])


def map_kernel(green, coupling, pattern, lead, tail, forward, backward, m_a, m_b, m_c, m_d):
    @pl.when(lax.axis_index("slab") > 0)
    def _():
        opening = couple(coupling, pattern, 0)
        coupler = row_form(couple(coupling, pattern, 1))
        first, second = row_form(green[0]), row_form(green[1])
        put(m_a, row_form(opening))
        ahead = times(first, m_a)
        forward[...] = ahead
        put(m_b, coupler)
        put(m_c, ahead)
        high, low = split(times(times(second, m_b), m_c))
        lead[0] = high
        lead[1] = low
        put(m_a, first)
        behind = times(adjoint_row(opening), m_a)
        backward[...] = behind
        put(m_d, second)
        put(tail, times(times(behind, m_b, True), m_d))


def fetch(choices, target, sem):
    for chosen, origin in choices:
        @pl.when(chosen)
        def _(origin=origin):
            pltpu.make_async_copy(origin, target, sem).start()


def wait_for(origin, target, sem):
    pltpu.make_async_copy(origin, target, sem).wait()


def shape(rows, columns, dtype=F32, *lead):
    return jax.ShapeDtypeStruct(lead + (rows, columns), dtype)


def matrices(number, size):
    return [pltpu.VMEM((2, 2 * size, 2 * size), HALF)] * number


def prepare_kernel(step, count, merged, *refs):
    turns = list(range(step, step + count - 2))
    listed = len(turns)
    arrived, wholes = refs[:listed], refs[listed : 2 * listed]
    refs = refs[2 * listed :]
    start_whole, source, forward, backward, coupling, pattern, following = refs[:7]
    refs = refs[7 + (5 if merged else 0) :]
    results, scratch = refs[:5], refs[5:]
    x_v, whole_v, source_v, forward_v, backward_v = scratch[:5]
    kept, sems = scratch[5:10], scratch[10]
    m_a, m_b, m_c, m_d = scratch[11:]
    place = lax.axis_index("slab")

    @pl.when((parity() == step) & (place < count - 1))
    def _():
        inner = place > 0
        fetch([(place == turn - step + 1, ref) for turn, ref in zip(turns, arrived)], x_v, sems.at[0])
        fetch(
            [(place == 0, start_whole)]
            + [(place == turn - step + 1, ref) for turn, ref in zip(turns, wholes)],
            whole_v,
            sems.at[1],
        )
        fetch([(place >= 0, source)], source_v, sems.at[2])
        fetch([(inner, forward)], forward_v, sems.at[3])
        fetch([(inner, backward)], backward_v, sems.at[4])
        wait_for(source, source_v, sems.at[2])

        @pl.when(inner)
        def _():
            wait_for(source, x_v, sems.at[0])
            wait_for(source, forward_v, sems.at[3])
            wait_for(source, backward_v, sems.at[4])
            put(m_a, x_v[...])
            put(m_b, backward_v[...])
            source_v[...] += times(times(forward_v[...], m_a), m_b)

        wait_for(source, whole_v, sems.at[1])
        lead, tail, constant, last_lead, last_tail = kept
        first, last = source_v[...], whole_v[...]
        coupler = row_form(couple(coupling, pattern, 1))
        through, joined = right_terms(first, last, coupler, m_a, m_b, m_c, m_d)
        constant[...] = joined
        next_coupler = row_form(following)
        put(m_a, next_coupler)
        lead[0], lead[1] = split(times(through, m_a, True))
        last_lead[0], last_lead[1] = split(times(last, m_a, True))
        behind = times(next_coupler, m_c)
        put(last_tail, behind)
        put(tail, times(behind, m_d))
        copies = [
            pltpu.make_async_copy(kept[index], results[index], sems.at[index])
            for index in range(5)
        ]
        for copy in copies:
            copy.start()
        for copy in copies:
            copy.wait()


def right_terms(first, last, coupler, m_coupler, m_first, m_last, m_upper):
    put(m_coupler, coupler)
    put(m_last, last)
    through = times(times(first, m_coupler, True), m_last)
    put(m_first, first)
    put(m_upper, times(coupler, m_first))
    return through, first + times(through, m_upper)


def relay_kernel(step, count, lefts, rights, *refs):
    refs = list(refs)
    place = lax.axis_index("slab")
    turn = step - parity()
    is_left = (turn >= 0) & (turn <= count - 2) & (place == turn + 1)
    is_right = (turn >= count - 1) & (place == 2 * count - 3 - turn)
    closing = lefts and step >= count - 2
    arrived = refs.pop(0)
    left_map = [refs.pop(0) for _ in range(3)] if lefts else None
    right_map = [refs.pop(0) for _ in range(3)] if rights else None
    if closing:
        forward, backward, source, coupling, pattern = [refs.pop(0) for _ in range(5)]
    out = refs.pop(0)
    if closing:
        end = refs.pop(0)
    x_v, lead_v, tail_v, constant_v, out_v, sems, m_x = refs[:7]
    refs = refs[7:]
    maps = ([(is_left, left_map)] if lefts else []) + ([(is_right, right_map)] if rights else [])
    active = is_left if not rights else is_right if not lefts else is_left | is_right

    if step == 0:

        @pl.when(place == 0)
        def _():
            copy = pltpu.make_async_copy(left_map[2], out, sems.at[0])
            copy.start()
            copy.wait()

    @pl.when(active)
    def _():
        fetch([(place >= 0, arrived)], x_v, sems.at[0])
        for index, target in enumerate((lead_v, tail_v, constant_v)):
            fetch([(chosen, refs_of[index]) for chosen, refs_of in maps], target, sems.at[1 + index])
        wait_for(arrived, x_v, sems.at[0])
        put(m_x, x_v[...])
        wait_for(maps[0][1][0], lead_v, sems.at[1])
        through = times_split(lead_v[0], lead_v[1], m_x)
        wait_for(maps[0][1][1], tail_v, sems.at[2])
        through = times(through, tail_v)
        wait_for(maps[0][1][2], constant_v, sems.at[3])
        out_v[...] = constant_v[...] + through
        if closing:
            forward_v, backward_v, source_v, coupling_v, m_a, m_b, m_c = refs

            @pl.when(is_left & (place == count - 1))
            def _():
                pltpu.make_async_copy(out_v, end, sems.at[0]).start()
                pltpu.make_async_copy(forward, forward_v, sems.at[1]).start()
                pltpu.make_async_copy(backward, backward_v, sems.at[2]).start()
                pltpu.make_async_copy(source, source_v, sems.at[3]).start()
                pltpu.make_async_copy(coupling.at[1], coupling_v.at[0], sems.at[4]).start()
                wait_for(backward, backward_v, sems.at[2])
                put(m_a, backward_v[...])
                wait_for(forward, forward_v, sems.at[1])
                wait_for(source, source_v, sems.at[3])
                first = source_v[...] + times(times(forward_v[...], m_x), m_a)
                wait_for(coupling.at[1], coupling_v.at[0], sems.at[4])
                coupler = row_form(couple(coupling_v, pattern, 0, 1))
                _, joined = right_terms(first, out_v[...], coupler, m_a, m_b, m_c, m_x)
                wait_for(out_v, end, sems.at[0])
                out_v[...] = joined

        copy = pltpu.make_async_copy(out_v, out, sems.at[0])
        copy.start()
        copy.wait()


def finish_kernel(count, *refs):
    refs = list(refs)
    arrived = [refs.pop(0) for _ in range(count)]
    outs = [refs.pop(0) for _ in range(count)]
    ends = [refs.pop(0) for _ in range(2)]
    lead, tail, constant, last_lead, last_tail, whole_start = [refs.pop(0) for _ in range(6)]
    wholes = [refs.pop(0) for _ in range(count - 1)]
    retarded = refs.pop(0)
    x_v, lead_v, tail_v, constant_v, out_v, last_lead_v, last_tail_v, whole_v, sems, m_x = refs
    place = lax.axis_index("slab")
    core = parity()
    size = x_v.shape[0]
    is_last = place == count - 1
    at = jnp.where(is_last, count - 2 + core, 2 * count - 3 - place + core)
    late = (place == 0) & (core == 1)

    @pl.when(jnp.logical_not(is_last))
    def _():
        fetch([(at == count - 1 + i, ref) for i, ref in enumerate(arrived)], x_v, sems.at[0])
        fetch([(place >= 0, last_lead)], last_lead_v, sems.at[1])
        fetch([(place >= 0, last_tail)], last_tail_v, sems.at[2])
        fetch(
            [(place == 0, whole_start)]
            + [((place > 0) & (place - 1 + core == i), ref) for i, ref in enumerate(wholes)],
            whole_v,
            sems.at[3],
        )

    fetch([(at == count - 2 + i, ref) for i, ref in enumerate(outs)], out_v, sems.at[4])
    fetch([(is_last & (core == i), ref) for i, ref in enumerate(ends)], whole_v, sems.at[3])

    @pl.when(late)
    def _():
        fetch([(place >= 0, lead)], lead_v, sems.at[4])
        fetch([(place >= 0, tail)], tail_v, sems.at[5])
        fetch([(place >= 0, constant)], constant_v, sems.at[6])

    @pl.when(jnp.logical_not(is_last))
    def _():
        wait_for(arrived[0], x_v, sems.at[0])
        put(m_x, x_v[...])

    @pl.when(late)
    def _():
        wait_for(lead, lead_v, sems.at[4])
        through = times_split(lead_v[0], lead_v[1], m_x)
        wait_for(tail, tail_v, sems.at[5])
        through = times(through, tail_v)
        wait_for(constant, constant_v, sems.at[6])
        out_v[...] = constant_v[...] + through

    @pl.when(jnp.logical_not(late))
    def _():
        wait_for(outs[0], out_v, sems.at[4])

    wait_for(outs[0], whole_v, sems.at[3])

    @pl.when(jnp.logical_not(is_last))
    def _():
        wait_for(last_lead, last_lead_v, sems.at[1])
        through = times_split(last_lead_v[0], last_lead_v[1], m_x)
        wait_for(last_tail, last_tail_v, sems.at[2])
        whole_v[...] += times(through, last_tail_v)

    for slab, block in enumerate((out_v, whole_v)):
        for part in range(2):
            retarded[slab, part] = block[:, part * size : (part + 1) * size]


def call(kernel, outs, scratch, args, specs=None, out_specs=None, aliases=None, flops=0, name=None):
    made = pl.pallas_call(
        kernel,
        out_shape=outs,
        in_specs=specs or [VMEM] * len(args),
        out_specs=out_specs or [VMEM] * len(outs),
        scratch_shapes=scratch,
        input_output_aliases=aliases or {},
        compiler_params=PARAMS,
        cost_estimate=pl.CostEstimate(flops=flops, bytes_accessed=4 * 2**20, transcendentals=0),
        name=name,
    )(*args)
    return list(made)


def mode_weights(targets, sources, offsets, emission, absorption):
    spacing = sources[None, :, None] - targets[:, None, None]
    emitted = jnp.where(
        spacing == -offsets[None, None, :],
        emission[None, None, :],
        jnp.zeros_like(emission)[None, None, :],
    )
    absorbed = jnp.where(
        spacing == offsets[None, None, :],
        absorption[None, None, :],
        jnp.zeros_like(absorption)[None, None, :],
    )
    return jnp.sum(emitted + absorbed, axis=-1)


def relay_pairs(step, energies, count):
    pairs = []
    for energy in range(energies):
        turn = step - energy % 2
        if 0 <= turn <= count - 2:
            ends = (turn, turn + 1)
        elif count - 1 <= turn <= 2 * count - 3:
            ends = (2 * count - 2 - turn, 2 * count - 3 - turn)
        else:
            continue
        pairs.append(tuple(energy * count + end for end in ends))
    return pairs


def shards(energies, count, free_green, self_energy, coupling, pattern, offsets, emission, absorption):
    size = free_green.shape[-1]
    green, sigma = free_green[0], self_energy[0]
    row = shape(size, 2 * size)
    lead = shape(size, 2 * size, HALF, 2)
    tail = shape(2 * size, 2 * size, HALF, 2)
    row_v = pltpu.VMEM(row.shape, F32)
    lead_v = pltpu.VMEM(lead.shape, HALF)
    product = 24 * size**3

    whole, source, coupler_half = call(
        source_kernel,
        [row, row, shape(size, size)],
        matrices(4, size),
        (green, sigma, coupling, pattern),
        flops=6 * product,
        name="source",
    )
    arrived, outs, ends = [], [whole], []

    def relay(step, value):
        return lax.ppermute(value, ("energy", "slab"), relay_pairs(step, energies, count))

    arrived.append(relay(0, whole))
    half = lax.ppermute(coupler_half, "slab", [(i, i - 1) for i in range(1, count)])
    left_lead, left_tail, forward, backward = call(
        map_kernel,
        [lead, tail, row, row],
        matrices(4, size),
        (green, coupling, pattern),
        flops=6 * product,
        name="left_maps",
    )
    left_map = (left_lead, left_tail, whole)
    right_map = None
    following = None
    for step in range(2 * count - 2):
        lefts, rights = step <= count - 1, step >= count - 1
        closing = lefts and step >= count - 2
        args = [arrived[step]]
        if lefts:
            args += left_map
        if rights:
            args += right_map[:3]
        if closing:
            args += [forward, backward, source, coupling, pattern]
        specs = [ANY] * len(args)
        if closing:
            specs[-1] = VMEM
        if step == 0:
            args.append(half)
            specs.append(ANY)

        def kernel(*refs, step=step, lefts=lefts, rights=rights, skip=len(args)):
            if step == 0:
                refs = refs[: skip - 1] + refs[skip:]
            relay_kernel(step, count, lefts, rights, *refs)

        scratch = [row_v, lead_v, *matrices(1, size), row_v, row_v, pltpu.SemaphoreType.DMA((5,))]
        scratch += matrices(1, size)
        if closing:
            scratch += [row_v, row_v, row_v, pltpu.VMEM((1, 2, size, size), F32), *matrices(3, size)]
        made = call(
            kernel,
            [row] * (2 if closing else 1),
            scratch,
            args,
            specs,
            [ANY] * (2 if closing else 1),
            flops=2 * product,
            name="relay",
        )
        outs.append(made[0])
        if closing:
            ends.append(made[1])
        arrived.append(relay(step + 1, made[0]))
        if step == 0:
            swapped = lax.ppermute(half, "energy", [(i, i ^ 1) for i in range(energies)])
            first_core = parity() == 0
            following = jnp.stack(
                [jnp.where(first_core, half, swapped), jnp.where(first_core, swapped, half)]
            )
        if step in (count - 3, count - 2):
            core = step - (count - 3)
            turns = range(core, core + count - 2)
            args = [arrived[turn] for turn in turns] + [outs[turn + 1] for turn in turns]
            args += [whole, source, forward, backward, coupling, pattern, following]
            specs = [ANY] * (len(args) - 3) + [VMEM] * 3
            aliases = {}
            if right_map is not None:
                aliases = {len(args) + index: index for index in range(5)}
                args += right_map
                specs += [ANY] * 5
            kept = [lead_v, *matrices(1, size), row_v, lead_v, *matrices(1, size)]
            right_map = call(
                functools.partial(prepare_kernel, core, count, core == 1),
                [lead, tail, row, lead, tail],
                [row_v] * 5 + kept + [pltpu.SemaphoreType.DMA((5,))] + matrices(4, size),
                args,
                specs,
                [ANY] * 5,
                aliases,
                flops=10 * product,
                name="right_maps",
            )
    args = arrived[count - 1 :] + outs[count - 1 :] + ends + right_map + [whole] + outs[1:count]
    scratch = [row_v, lead_v, *matrices(1, size), row_v, row_v]
    scratch += [lead_v, *matrices(1, size), row_v, pltpu.SemaphoreType.DMA((7,)), *matrices(1, size)]
    (retarded,) = call(
        functools.partial(finish_kernel, count),
        [shape(size, size, F32, 2, 2)],
        scratch,
        args,
        [ANY] * len(args),
        flops=4 * product,
        name="retarded",
    )
    retarded = retarded[None]
    everyone = jnp.arange(energies, dtype=jnp.int32)
    weights = mode_weights(everyone, everyone, offsets, emission, absorption)
    mixed = jnp.einsum(
        "ef,fsxab->esxab",
        weights,
        lax.all_to_all(retarded, "energy", split_axis=3, concat_axis=0, tiled=True),
        precision=lax.Precision.HIGHEST,
    )
    scattering = lax.all_to_all(mixed, "energy", split_axis=0, concat_axis=3, tiled=True)
    return (retarded, scattering)


def solution(mesh):
    blocks = P("energy", "slab", None, None, None)
    in_specs = (blocks, blocks, P("slab", None, None, None), P("slab", None, None), P(), P(), P())
    body = functools.partial(shards, mesh.shape["energy"], mesh.shape["slab"])
    return jax.shard_map(
        body, mesh=mesh, in_specs=in_specs, out_specs=(blocks, blocks), check_vma=False
    )
```

```python
import functools

import jax
import jax.numpy as jnp
from jax import lax
from jax.experimental import pallas as pl
from jax.experimental.pallas import tpu as pltpu
from jax.sharding import PartitionSpec as P

F32 = jnp.float32
HALF = jnp.bfloat16
HBM = pl.BlockSpec(memory_space=pltpu.HBM)
VMEM = pl.BlockSpec(memory_space=pltpu.VMEM)


def split(value):
    high = value.astype(HALF)
    return high, (value - high.astype(F32)).astype(HALF)


def dot(left, right, transposed):
    dims = (((1,), (1 if transposed else 0,)), ((), ()))
    return lax.dot_general(left, right, dims, preferred_element_type=F32)


def put(matrix, block):
    size = block.shape[0]
    for level, part in enumerate(split(block)):
        real, imag = part[:, :size], part[:, size:]
        matrix[level, :size, :size] = real
        matrix[level, :size, size:] = imag
        matrix[level, size:, :size] = -imag
        matrix[level, size:, size:] = real


def times_split(high, low, matrix, transposed=False):
    return (
        dot(high, matrix[0], transposed)
        + dot(low, matrix[0], transposed)
        + dot(high, matrix[1], transposed)
    )


def times(block, matrix, transposed=False):
    high, low = split(block)
    return times_split(high, low, matrix, transposed)


def row_form(pair):
    return jnp.concatenate([pair[0], pair[1]], axis=1)


def adjoint_row(pair):
    return jnp.concatenate([jnp.transpose(pair[0]), -jnp.transpose(pair[1])], axis=1)


def expand(pattern, size):
    blocks = pattern.shape[0]
    tile = size // blocks
    rows = lax.broadcasted_iota(jnp.int32, (size, blocks), 0)
    first = lax.broadcasted_iota(jnp.int32, (size, blocks), 1) * tile
    member = jnp.where((rows >= first) & (rows < first + tile), 1.0, 0.0).astype(HALF)
    tall = dot(member, pattern.astype(F32).astype(HALF), False)
    return dot(tall.astype(HALF), member, True)


def couple(coupling, pattern):
    mask = expand(pattern[...], coupling.shape[-1])
    return jnp.concatenate([coupling[0] * mask, coupling[1] * mask], axis=1)


def parity():
    return lax.rem(lax.axis_index("energy"), 2)


def shape(rows, columns, dtype=F32, *lead):
    return jax.ShapeDtypeStruct(lead + (rows, columns), dtype)


def matrices(number, size):
    return [pltpu.VMEM((2, 2 * size, 2 * size), HALF)] * number


def call(kernel, outs, scratch, args, specs=None, flops=0, name=None, limit=40):
    made = pl.pallas_call(
        kernel,
        out_shape=outs,
        in_specs=specs or [VMEM] * len(args),
        out_specs=[VMEM] * len(outs),
        scratch_shapes=scratch,
        compiler_params=pltpu.CompilerParams(vmem_limit_bytes=limit * 2**20),
        cost_estimate=pl.CostEstimate(flops=flops, bytes_accessed=2**20, transcendentals=0),
        name=name,
    )(*args)
    return list(made)


class Loads:
    def __init__(self, args, targets, sems, slabs=(0, 1)):
        order = [(0, 0), (1, 0), (3, 1), (2, 1), (1, 1), (0, 1), (3, 0), (2, 0)]
        self.copies = {
            (which, slab): pltpu.make_async_copy(
                args[which].at[slab], targets[which].at[slab], sems.at[index]
            )
            for index, (which, slab) in enumerate(order)
            if which < 2 or slab in slabs
        }
        self.targets = targets
        for copy in self.copies.values():
            copy.start()

    def get(self, which, slab):
        self.copies[which, slab].wait()
        return self.targets[which].at[slab]

    def green(self, slab):
        return row_form(self.get(0, slab))

    def sigma(self, slab):
        return row_form(self.get(1, slab))

    def coupler(self, slab):
        tiles = self.get(3, slab)
        return couple(self.get(2, slab), tiles)


def load_scratch(size, blocks):
    return [
        pltpu.VMEM((2, 2, size, size), F32),
        pltpu.VMEM((2, 2, size, size), F32),
        pltpu.VMEM((2, 2, size, size), F32),
        pltpu.VMEM((2, blocks, blocks), jnp.int32),
        pltpu.SemaphoreType.DMA((8,)),
    ]


def left_sources(loads, whole, source, coupler_out, m_a, m_b, m_c):
    first = loads.green(0)
    put(m_b, first)
    put(m_a, loads.sigma(0))
    made = first + times(times(first, m_a), m_b)
    if source is not None:
        source[...] = made
    put(m_a, made)
    coupler = loads.coupler(1)
    if coupler_out is not None:
        coupler_out[...] = coupler
    put(m_c, coupler)
    inner = loads.sigma(1) + times(times(coupler, m_a), m_c, True)
    put(m_a, inner)
    second = loads.green(1)
    put(m_b, second)
    whole[...] = second + times(times(second, m_a), m_b)
    return first, second


def source_kernel(green, sigma, coupling, pattern, whole, *scratch):
    @pl.when(lax.axis_index("slab") == 0)
    def _():
        loads = Loads((green, sigma, coupling, pattern), scratch[:4], scratch[4], (1,))
        left_sources(loads, whole, None, None, *scratch[5:])


def map_kernel(
    green, sigma, coupling, pattern,
    whole, source, coupler, opening, lead, tail, forward, backward, *scratch,
):
    m_a, m_b, m_c = scratch[5:]
    loads = Loads((green, sigma, coupling, pattern), scratch[:4], scratch[4])
    first, second = left_sources(loads, whole, source, coupler, m_a, m_b, m_c)
    before = loads.coupler(0)

    @pl.when(lax.axis_index("slab") > 0)
    def _():
        opening[...] = before
        put(m_a, before)
        ahead = times(first, m_a)
        forward[...] = ahead
        put(m_a, ahead)
        lead[0], lead[1] = split(times(times(second, m_c), m_a))
        put(m_a, first)
        size = before.shape[0]
        behind = times(adjoint_row((before[:, :size], before[:, size:])), m_a)
        backward[...] = behind
        put(tail, times(times(behind, m_c, True), m_b))


def right_terms(first, last, coupler, m_coupler, m_first, m_last, m_upper):
    put(m_coupler, coupler)
    put(m_last, last)
    through = times(times(first, m_coupler, True), m_last)
    put(m_first, first)
    put(m_upper, times(coupler, m_first))
    return through, first + times(through, m_upper)


def prepare_kernel(count, *refs):
    arrived, wholes = refs[: count - 1], refs[count - 1 : 2 * count - 2]
    refs = refs[2 * count - 2 :]
    start_whole, source, forward, backward, coupler, following = refs[:6]
    lead, tail, constant, last_lead, last_tail = refs[6:11]
    first_v, last_v, m_a, m_b, m_c, m_d = refs[11:]
    place = lax.axis_index("slab")

    @pl.when(place == 0)
    def _():
        first_v[...] = source[...]
        last_v[...] = start_whole[...]

    for turn in range(count - 1):
        @pl.when((place > 0) & (place == turn + 1 - parity()))
        def _(turn=turn):
            last_v[...] = wholes[turn][...]
            put(m_a, arrived[turn][...])

    @pl.when((place > 0) & (place < count - 1))
    def _():
        put(m_b, backward[...])
        first_v[...] = source[...] + times(times(forward[...], m_a), m_b)

    @pl.when(place < count - 1)
    def _():
        first, last = first_v[...], last_v[...]
        through, joined = right_terms(first, last, coupler[...], m_a, m_b, m_c, m_d)
        constant[...] = joined
        next_coupler = following[...]
        put(m_a, next_coupler)
        lead[0], lead[1] = split(times(through, m_a, True))
        last_lead[0], last_lead[1] = split(times(last, m_a, True))
        behind = times(next_coupler, m_c)
        put(last_tail, behind)
        put(tail, times(behind, m_d))


def apply_map(mapping, m_x):
    lead, tail, constant = mapping
    return constant[...] + times(times_split(lead[0], lead[1], m_x), tail)


def relay_kernel(step, count, lefts, rights, *refs):
    refs = list(refs)
    place = lax.axis_index("slab")
    turn = step - parity()
    is_left = (turn >= 0) & (turn <= count - 2) & (place == turn + 1)
    is_right = (turn >= count - 1) & (place == 2 * count - 3 - turn)
    closing = lefts and step >= count - 2
    arrived = refs.pop(0)
    left_map = [refs.pop(0) for _ in range(3)] if lefts else None
    right_map = [refs.pop(0) for _ in range(3)] if rights else None
    if closing:
        forward, backward, source, coupler = [refs.pop(0) for _ in range(4)]
    out = refs.pop(0)
    if closing:
        end, m_x, m_a, m_b, m_c = refs
    else:
        (m_x,) = refs

    if step == 0:
        @pl.when(place == 0)
        def _():
            out[...] = left_map[2][...]

    if lefts:
        @pl.when(is_left)
        def _():
            put(m_x, arrived[...])
            out[...] = apply_map(left_map, m_x)

    if closing:
        @pl.when(is_left & (place == count - 1))
        def _():
            last = out[...]
            end[...] = last
            put(m_a, backward[...])
            first = source[...] + times(times(forward[...], m_x), m_a)
            _, joined = right_terms(first, last, coupler[...], m_a, m_b, m_c, m_x)
            out[...] = joined

    if rights:
        @pl.when(is_right)
        def _():
            put(m_x, arrived[...])
            out[...] = apply_map(right_map, m_x)


def finish_kernel(count, *refs):
    refs = list(refs)
    arrived = [refs.pop(0) for _ in range(count)]
    outs = [refs.pop(0) for _ in range(count)]
    ends = [refs.pop(0) for _ in range(2)]
    right_map = [refs.pop(0) for _ in range(3)]
    last_lead, last_tail, whole_start = [refs.pop(0) for _ in range(3)]
    wholes = [refs.pop(0) for _ in range(count - 1)]
    retarded, out_v, whole_v, m_x = refs
    place = lax.axis_index("slab")
    core = parity()
    size = out_v.shape[0]
    is_last = place == count - 1
    at = jnp.where(is_last, count - 2 + core, 2 * count - 3 - place + core)
    late = (place == 0) & (core == 1)

    for index in range(count):
        @pl.when(at == count - 1 + index)
        def _(index=index):
            put(m_x, arrived[index][...])

        @pl.when(at == count - 2 + index)
        def _(index=index):
            out_v[...] = outs[index][...]

    for index in range(2):
        @pl.when(is_last & (core == index))
        def _(index=index):
            whole_v[...] = ends[index][...]

    @pl.when(late)
    def _():
        out_v[...] = apply_map(right_map, m_x)

    @pl.when(place == 0)
    def _():
        whole_v[...] = apply_map((last_lead, last_tail, whole_start), m_x)

    for index in range(count - 1):
        @pl.when((place > 0) & jnp.logical_not(is_last) & (place - 1 + core == index))
        def _(index=index):
            whole_v[...] = apply_map((last_lead, last_tail, wholes[index]), m_x)

    for slab, block in enumerate((out_v, whole_v)):
        for part in range(2):
            retarded[slab, part] = block[:, part * size : (part + 1) * size]


def mode_weights(targets, sources, offsets, emission, absorption):
    spacing = sources[None, :, None] - targets[:, None, None]
    emitted = jnp.where(
        spacing == -offsets[None, None, :],
        emission[None, None, :],
        jnp.zeros_like(emission)[None, None, :],
    )
    absorbed = jnp.where(
        spacing == offsets[None, None, :],
        absorption[None, None, :],
        jnp.zeros_like(absorption)[None, None, :],
    )
    return jnp.sum(emitted + absorbed, axis=-1)


def relay_pairs(step, energies, count):
    pairs = []
    for energy in range(energies):
        turn = step - energy % 2
        if 0 <= turn <= count - 2:
            ends = (turn, turn + 1)
        elif count - 1 <= turn <= 2 * count - 3:
            ends = (2 * count - 2 - turn, 2 * count - 3 - turn)
        else:
            continue
        pairs.append(tuple(energy * count + end for end in ends))
    return pairs


def shards(energies, count, free_green, self_energy, coupling, pattern, offsets, emission, absorption):
    size, blocks = free_green.shape[-1], pattern.shape[-1]
    args = (free_green[0], self_energy[0], coupling, pattern)
    row = shape(size, 2 * size)
    lead = shape(size, 2 * size, HALF, 2)
    tail = shape(2 * size, 2 * size, HALF, 2)
    row_v = pltpu.VMEM(row.shape, F32)
    product = 24 * size**3
    loading = load_scratch(size, blocks) + matrices(3, size)

    def relay(step, value):
        return lax.ppermute(value, ("energy", "slab"), relay_pairs(step, energies, count))

    begun = call(
        source_kernel,
        [row],
        loading,
        args,
        [HBM] * 4,
        flops=6 * product,
        name="source",
        limit=58,
    )
    arrived, outs, ends = [relay(0, begun[0])], [], []
    whole, source, coupler, opening, left_lead, left_tail, forward, backward = call(
        map_kernel,
        [row] * 4 + [lead, tail, row, row],
        loading,
        args,
        [HBM] * 4,
        flops=12 * product,
        name="left_maps",
        limit=42,
    )
    left_map = [left_lead, left_tail, whole]
    right_map = following = None
    for step in range(2 * count - 2):
        lefts, rights = step <= count - 1, step >= count - 1
        closing = lefts and step >= count - 2
        args = [arrived[step]]
        if lefts:
            args += left_map
        if rights:
            args += right_map[:3]
        if closing:
            args += [forward, backward, source, coupler]
        made = call(
            functools.partial(relay_kernel, step, count, lefts, rights),
            [row] * (2 if closing else 1),
            matrices(4 if closing else 1, size),
            args,
            flops=2 * product,
            name="relay",
        )
        outs.append(made[0])
        ends += made[1:]
        arrived.append(relay(step + 1, made[0]))
        if step == 0:
            following = lax.ppermute(opening, "slab", [(i, i - 1) for i in range(1, count)])
        if step == count - 2:
            args = arrived[: count - 1] + outs[: count - 1]
            args += [whole, source, forward, backward, coupler, following]
            right_map = call(
                functools.partial(prepare_kernel, count),
                [lead, tail, row, lead, tail],
                [row_v] * 2 + matrices(4, size),
                args,
                flops=10 * product,
                name="right_maps",
            )
    args = arrived[count - 1 :] + outs[count - 2 :] + ends + right_map + [whole] + outs[: count - 1]
    (retarded,) = call(
        functools.partial(finish_kernel, count),
        [shape(size, size, F32, 2, 2)],
        [row_v] * 2 + matrices(1, size),
        args,
        flops=4 * product,
        name="retarded",
    )
    retarded = retarded[None]
    everyone = jnp.arange(energies, dtype=jnp.int32)
    weights = mode_weights(everyone, everyone, offsets, emission, absorption)
    mixed = jnp.einsum(
        "ef,fsxab->esxab",
        weights,
        lax.all_to_all(retarded, "energy", split_axis=3, concat_axis=0, tiled=True),
        precision=lax.Precision.HIGHEST,
    )
    scattering = lax.all_to_all(mixed, "energy", split_axis=0, concat_axis=3, tiled=True)
    return (retarded, scattering)


def solution(mesh):
    blocks = P("energy", "slab", None, None, None)
    in_specs = (blocks, blocks, P("slab", None, None, None), P("slab", None, None), P(), P(), P())
    body = functools.partial(shards, mesh.shape["energy"], mesh.shape["slab"])
    return jax.shard_map(
        body, mesh=mesh, in_specs=in_specs, out_specs=(blocks, blocks), check_vma=False
    )
```

```python
import functools

import jax
import jax.numpy as jnp
from jax import lax
from jax.experimental import pallas as pl
from jax.experimental.pallas import tpu as pltpu
from jax.sharding import PartitionSpec as P

F32 = jnp.float32
HALF = jnp.bfloat16
HBM = pl.BlockSpec(memory_space=pltpu.HBM)
VMEM = pl.BlockSpec(memory_space=pltpu.VMEM)


def split(value):
    high = value.astype(HALF)
    return high, (value - high.astype(F32)).astype(HALF)


def dot(left, right, transposed):
    dims = (((1,), (1 if transposed else 0,)), ((), ()))
    return lax.dot_general(left, right, dims, preferred_element_type=F32)


def put(matrix, block):
    size = block.shape[0]
    for level, part in enumerate(split(block)):
        real, imag = part[:, :size], part[:, size:]
        matrix[level, :size, :size] = real
        matrix[level, :size, size:] = imag
        matrix[level, size:, :size] = -imag
        matrix[level, size:, size:] = real


def times_split(high, low, matrix, transposed=False):
    return (
        dot(high, matrix[0], transposed)
        + dot(low, matrix[0], transposed)
        + dot(high, matrix[1], transposed)
    )


def times(block, matrix, transposed=False):
    high, low = split(block)
    return times_split(high, low, matrix, transposed)


def row_form(pair):
    return jnp.concatenate([pair[0], pair[1]], axis=1)


def adjoint_row(pair):
    return jnp.concatenate([jnp.transpose(pair[0]), -jnp.transpose(pair[1])], axis=1)


def expand(pattern, size):
    blocks = pattern.shape[0]
    tile = size // blocks
    rows = lax.broadcasted_iota(jnp.int32, (size, blocks), 0)
    first = lax.broadcasted_iota(jnp.int32, (size, blocks), 1) * tile
    member = jnp.where((rows >= first) & (rows < first + tile), 1.0, 0.0).astype(HALF)
    tall = dot(member, pattern.astype(F32).astype(HALF), False)
    return dot(tall.astype(HALF), member, True)


def couple(coupling, pattern):
    mask = expand(pattern[...], coupling.shape[-1])
    return jnp.concatenate([coupling[0] * mask, coupling[1] * mask], axis=1)


def parity():
    return lax.rem(lax.axis_index("energy"), 2)


def shape(rows, columns, dtype=F32, *lead):
    return jax.ShapeDtypeStruct(lead + (rows, columns), dtype)


def matrices(number, size):
    return [pltpu.VMEM((2, 2 * size, 2 * size), HALF)] * number


def call(kernel, outs, scratch, args, specs=None, flops=0, name=None, limit=40):
    made = pl.pallas_call(
        kernel,
        out_shape=outs,
        in_specs=specs or [VMEM] * len(args),
        out_specs=[VMEM] * len(outs),
        scratch_shapes=scratch,
        compiler_params=pltpu.CompilerParams(vmem_limit_bytes=limit * 2**20),
        cost_estimate=pl.CostEstimate(flops=flops, bytes_accessed=2**20, transcendentals=0),
        name=name,
    )(*args)
    return list(made)


class Loads:
    def __init__(self, args, targets, sems, couplers=(0, 1), blocks=True):
        order = [(0, 0), (1, 0), (3, 1), (2, 1), (1, 1), (0, 1), (3, 0), (2, 0)]
        self.copies = {
            (which, slab): pltpu.make_async_copy(
                args[which].at[slab], targets[which].at[slab], sems.at[index]
            )
            for index, (which, slab) in enumerate(order)
            if (blocks if which < 2 else slab in couplers)
        }
        self.targets = targets
        for copy in self.copies.values():
            copy.start()

    def get(self, which, slab):
        self.copies[which, slab].wait()
        return self.targets[which].at[slab]

    def green(self, slab):
        return row_form(self.get(0, slab))

    def sigma(self, slab):
        return row_form(self.get(1, slab))

    def coupler(self, slab):
        tiles = self.get(3, slab)
        return couple(self.get(2, slab), tiles)


def load_scratch(size, blocks):
    return [
        pltpu.VMEM((2, 2, size, size), F32),
        pltpu.VMEM((2, 2, size, size), F32),
        pltpu.VMEM((2, 2, size, size), F32),
        pltpu.VMEM((2, blocks, blocks), jnp.int32),
        pltpu.SemaphoreType.DMA((8,)),
    ]


def left_sources(loads, whole, source, coupler_out, m_a, m_b, m_c):
    first = loads.green(0)
    put(m_b, first)
    put(m_a, loads.sigma(0))
    made = first + times(times(first, m_a), m_b)
    if source is not None:
        source[...] = made
    put(m_a, made)
    coupler = loads.coupler(1)
    if coupler_out is not None:
        coupler_out[...] = coupler
    put(m_c, coupler)
    inner = loads.sigma(1) + times(times(coupler, m_a), m_c, True)
    put(m_a, inner)
    second = loads.green(1)
    put(m_b, second)
    whole[...] = second + times(times(second, m_a), m_b)
    return first, second


def source_kernel(green, sigma, coupling, pattern, whole, *scratch):
    @pl.when(lax.axis_index("slab") == 0)
    def _():
        loads = Loads((green, sigma, coupling, pattern), scratch[:4], scratch[4], (1,))
        left_sources(loads, whole, None, None, *scratch[5:])

    @pl.when((lax.axis_index("slab") > 0) & (parity() == 1))
    def _():
        loads = Loads((green, sigma, coupling, pattern), scratch[:4], scratch[4], (0,), False)
        whole[...] = loads.coupler(0)


def map_kernel(
    green, sigma, coupling, pattern,
    whole, source, coupler, opening, lead, tail, forward, backward, *scratch,
):
    m_a, m_b, m_c = scratch[5:]
    loads = Loads((green, sigma, coupling, pattern), scratch[:4], scratch[4])
    first, second = left_sources(loads, whole, source, coupler, m_a, m_b, m_c)
    before = loads.coupler(0)

    @pl.when(lax.axis_index("slab") > 0)
    def _():
        opening[...] = before
        put(m_a, before)
        ahead = times(first, m_a)
        forward[...] = ahead
        put(m_a, ahead)
        lead[0], lead[1] = split(times(times(second, m_c), m_a))
        put(m_a, first)
        size = before.shape[0]
        behind = times(adjoint_row((before[:, :size], before[:, size:])), m_a)
        backward[...] = behind
        put(tail, times(times(behind, m_c, True), m_b))


def right_terms(first, last, coupler, m_coupler, m_first, m_last, m_upper):
    put(m_coupler, coupler)
    put(m_last, last)
    through = times(times(first, m_coupler, True), m_last)
    put(m_first, first)
    put(m_upper, times(coupler, m_first))
    return through, first + times(through, m_upper)


def prepare_kernel(count, *refs):
    arrived, wholes = refs[: count - 1], refs[count - 1 : 2 * count - 2]
    refs = refs[2 * count - 2 :]
    start_whole, source, forward, backward, coupler = refs[:5]
    followings = refs[5:7]
    lead, tail, constant, last_lead, last_tail = refs[7:12]
    first_v, last_v, m_a, m_b, m_c, m_d = refs[12:]
    place = lax.axis_index("slab")

    @pl.when(place == 0)
    def _():
        first_v[...] = source[...]
        last_v[...] = start_whole[...]

    for turn in range(count - 1):
        @pl.when((place > 0) & (place == turn + 1 - parity()))
        def _(turn=turn):
            last_v[...] = wholes[turn][...]
            put(m_a, arrived[turn][...])

    @pl.when((place > 0) & (place < count - 1))
    def _():
        put(m_b, backward[...])
        first_v[...] = source[...] + times(times(forward[...], m_a), m_b)

    @pl.when(place < count - 1)
    def _():
        first, last = first_v[...], last_v[...]
        through, joined = right_terms(first, last, coupler[...], m_a, m_b, m_c, m_d)
        constant[...] = joined
        next_coupler = jnp.where(parity() == 0, followings[0][...], followings[1][...])
        put(m_a, next_coupler)
        lead[0], lead[1] = split(times(through, m_a, True))
        last_lead[0], last_lead[1] = split(times(last, m_a, True))
        behind = times(next_coupler, m_c)
        put(last_tail, behind)
        put(tail, times(behind, m_d))


def apply_map(mapping, m_x):
    lead, tail, constant = mapping
    return constant[...] + times(times_split(lead[0], lead[1], m_x), tail)


def relay_kernel(step, count, lefts, rights, *refs):
    refs = list(refs)
    place = lax.axis_index("slab")
    turn = step - parity()
    is_left = (turn >= 0) & (turn <= count - 2) & (place == turn + 1)
    is_right = (turn >= count - 1) & (place == 2 * count - 3 - turn)
    closing = lefts and step >= count - 2
    arrived = refs.pop(0)
    left_map = [refs.pop(0) for _ in range(3)] if lefts else None
    right_map = [refs.pop(0) for _ in range(3)] if rights else None
    if closing:
        forward, backward, source, coupler = [refs.pop(0) for _ in range(4)]
    out = refs.pop(0)
    if closing:
        end, m_x, m_a, m_b, m_c = refs
    else:
        (m_x,) = refs

    if step == 0:
        @pl.when(place == 0)
        def _():
            out[...] = left_map[2][...]

    if lefts:
        @pl.when(is_left)
        def _():
            put(m_x, arrived[...])
            out[...] = apply_map(left_map, m_x)

    if closing:
        @pl.when(is_left & (place == count - 1))
        def _():
            last = out[...]
            end[...] = last
            put(m_a, backward[...])
            first = source[...] + times(times(forward[...], m_x), m_a)
            _, joined = right_terms(first, last, coupler[...], m_a, m_b, m_c, m_x)
            out[...] = joined

    if rights:
        @pl.when(is_right)
        def _():
            put(m_x, arrived[...])
            out[...] = apply_map(right_map, m_x)


def finish_kernel(count, *refs):
    refs = list(refs)
    arrived = [refs.pop(0) for _ in range(count)]
    outs = [refs.pop(0) for _ in range(count)]
    ends = [refs.pop(0) for _ in range(2)]
    right_map = [refs.pop(0) for _ in range(3)]
    last_lead, last_tail, whole_start = [refs.pop(0) for _ in range(3)]
    wholes = [refs.pop(0) for _ in range(count - 1)]
    retarded, out_v, whole_v, m_x = refs
    place = lax.axis_index("slab")
    core = parity()
    size = out_v.shape[0]
    is_last = place == count - 1
    at = jnp.where(is_last, count - 2 + core, 2 * count - 3 - place + core)
    late = (place == 0) & (core == 1)

    for index in range(count):
        @pl.when(at == count - 1 + index)
        def _(index=index):
            put(m_x, arrived[index][...])

        @pl.when(at == count - 2 + index)
        def _(index=index):
            out_v[...] = outs[index][...]

    for index in range(2):
        @pl.when(is_last & (core == index))
        def _(index=index):
            whole_v[...] = ends[index][...]

    @pl.when(late)
    def _():
        out_v[...] = apply_map(right_map, m_x)

    @pl.when(place == 0)
    def _():
        whole_v[...] = apply_map((last_lead, last_tail, whole_start), m_x)

    for index in range(count - 1):
        @pl.when((place > 0) & jnp.logical_not(is_last) & (place - 1 + core == index))
        def _(index=index):
            whole_v[...] = apply_map((last_lead, last_tail, wholes[index]), m_x)

    for slab, block in enumerate((out_v, whole_v)):
        for part in range(2):
            retarded[slab, part] = block[:, part * size : (part + 1) * size]


def mode_weights(targets, sources, offsets, emission, absorption):
    spacing = sources[None, :, None] - targets[:, None, None]
    emitted = jnp.where(
        spacing == -offsets[None, None, :],
        emission[None, None, :],
        jnp.zeros_like(emission)[None, None, :],
    )
    absorbed = jnp.where(
        spacing == offsets[None, None, :],
        absorption[None, None, :],
        jnp.zeros_like(absorption)[None, None, :],
    )
    return jnp.sum(emitted + absorbed, axis=-1)


def relay_pairs(step, energies, count):
    pairs = []
    for energy in range(energies):
        turn = step - energy % 2
        if turn < 0:
            pairs += [(energy * count + i, energy * count + i - 1) for i in range(1, count)]
            continue
        if turn <= count - 2:
            ends = (turn, turn + 1)
        elif count - 1 <= turn <= 2 * count - 3:
            ends = (2 * count - 2 - turn, 2 * count - 3 - turn)
        else:
            continue
        pairs.append(tuple(energy * count + end for end in ends))
    return pairs


def shards(energies, count, free_green, self_energy, coupling, pattern, offsets, emission, absorption):
    size, blocks = free_green.shape[-1], pattern.shape[-1]
    args = (free_green[0], self_energy[0], coupling, pattern)
    row = shape(size, 2 * size)
    lead = shape(size, 2 * size, HALF, 2)
    tail = shape(2 * size, 2 * size, HALF, 2)
    row_v = pltpu.VMEM(row.shape, F32)
    product = 24 * size**3
    loading = load_scratch(size, blocks) + matrices(3, size)

    def relay(step, value):
        return lax.ppermute(value, ("energy", "slab"), relay_pairs(step, energies, count))

    begun = call(
        source_kernel,
        [row],
        loading,
        args,
        [HBM] * 4,
        flops=6 * product,
        name="source",
        limit=58,
    )
    arrived, outs, ends = [relay(0, begun[0])], [], []
    whole, source, coupler, opening, left_lead, left_tail, forward, backward = call(
        map_kernel,
        [row] * 4 + [lead, tail, row, row],
        loading,
        args,
        [HBM] * 4,
        flops=12 * product,
        name="left_maps",
        limit=42,
    )
    left_map = [left_lead, left_tail, whole]
    right_map = following = None
    for step in range(2 * count - 2):
        lefts, rights = step <= count - 1, step >= count - 1
        closing = lefts and step >= count - 2
        args = [arrived[step]]
        if lefts:
            args += left_map
        if rights:
            args += right_map[:3]
        if closing:
            args += [forward, backward, source, coupler]
        made = call(
            functools.partial(relay_kernel, step, count, lefts, rights),
            [row] * (2 if closing else 1),
            matrices(4 if closing else 1, size),
            args,
            flops=2 * product,
            name="relay",
        )
        outs.append(made[0])
        ends += made[1:]
        arrived.append(relay(step + 1, made[0]))
        if step == 0:
            down = [
                (energy * count + i, energy * count + i - 1)
                for energy in range(0, energies, 2)
                for i in range(1, count)
            ]
            following = lax.ppermute(opening, ("energy", "slab"), down)
        if step == count - 2:
            args = arrived[: count - 1] + outs[: count - 1]
            args += [whole, source, forward, backward, coupler, following, arrived[0]]
            right_map = call(
                functools.partial(prepare_kernel, count),
                [lead, tail, row, lead, tail],
                [row_v] * 2 + matrices(4, size),
                args,
                flops=10 * product,
                name="right_maps",
            )
    args = arrived[count - 1 :] + outs[count - 2 :] + ends + right_map + [whole] + outs[: count - 1]
    (retarded,) = call(
        functools.partial(finish_kernel, count),
        [shape(size, size, F32, 2, 2)],
        [row_v] * 2 + matrices(1, size),
        args,
        flops=4 * product,
        name="retarded",
    )
    retarded = retarded[None]
    everyone = jnp.arange(energies, dtype=jnp.int32)
    weights = mode_weights(everyone, everyone, offsets, emission, absorption)
    mixed = jnp.einsum(
        "ef,fsxab->esxab",
        weights,
        lax.all_to_all(retarded, "energy", split_axis=3, concat_axis=0, tiled=True),
        precision=lax.Precision.HIGHEST,
    )
    scattering = lax.all_to_all(mixed, "energy", split_axis=0, concat_axis=3, tiled=True)
    return (retarded, scattering)


def solution(mesh):
    blocks = P("energy", "slab", None, None, None)
    in_specs = (blocks, blocks, P("slab", None, None, None), P("slab", None, None), P(), P(), P())
    body = functools.partial(shards, mesh.shape["energy"], mesh.shape["slab"])
    return jax.shard_map(
        body, mesh=mesh, in_specs=in_specs, out_specs=(blocks, blocks), check_vma=False
    )
```

```python
import functools

import jax
import jax.numpy as jnp
from jax import lax
from jax.experimental import pallas as pl
from jax.experimental.pallas import tpu as pltpu
from jax.sharding import PartitionSpec as P

F32 = jnp.float32
HALF = jnp.bfloat16
HBM = pl.BlockSpec(memory_space=pltpu.HBM)
VMEM = pl.BlockSpec(memory_space=pltpu.VMEM)
SMEM = pl.BlockSpec(memory_space=pltpu.SMEM)


def split(value):
    high = value.astype(HALF)
    return high, (value - high.astype(F32)).astype(HALF)


def dot(left, right, transposed):
    dims = (((1,), (1 if transposed else 0,)), ((), ()))
    return lax.dot_general(left, right, dims, preferred_element_type=F32)


def put(matrix, block):
    size = block.shape[0]
    for level, part in enumerate(split(block)):
        real, imag = part[:, :size], part[:, size:]
        matrix[level, :size, :size] = real
        matrix[level, :size, size:] = imag
        matrix[level, size:, :size] = -imag
        matrix[level, size:, size:] = real


def times_split(high, low, matrix, transposed=False):
    return (
        dot(high, matrix[0], transposed)
        + dot(low, matrix[0], transposed)
        + dot(high, matrix[1], transposed)
    )


def times(block, matrix, transposed=False):
    high, low = split(block)
    return times_split(high, low, matrix, transposed)


def row_form(pair):
    return jnp.concatenate([pair[0], pair[1]], axis=1)


def adjoint_row(pair):
    return jnp.concatenate([jnp.transpose(pair[0]), -jnp.transpose(pair[1])], axis=1)


def expand(pattern, size):
    blocks = pattern.shape[0]
    tile = size // blocks
    rows = lax.broadcasted_iota(jnp.int32, (size, blocks), 0)
    first = lax.broadcasted_iota(jnp.int32, (size, blocks), 1) * tile
    member = jnp.where((rows >= first) & (rows < first + tile), 1.0, 0.0).astype(HALF)
    tall = dot(member, pattern.astype(F32).astype(HALF), False)
    return dot(tall.astype(HALF), member, True)


def couple(coupling, pattern):
    mask = expand(pattern[...], coupling.shape[-1])
    return jnp.concatenate([coupling[0] * mask, coupling[1] * mask], axis=1)


def parity():
    return lax.rem(lax.axis_index("energy"), 2)


def shape(rows, columns, dtype=F32, *lead):
    return jax.ShapeDtypeStruct(lead + (rows, columns), dtype)


def matrices(number, size):
    return [pltpu.VMEM((2, 2 * size, 2 * size), HALF)] * number


def call(kernel, outs, scratch, args, specs=None, flops=0, name=None, limit=40):
    made = pl.pallas_call(
        kernel,
        out_shape=outs,
        in_specs=specs or [VMEM] * len(args),
        out_specs=[VMEM] * len(outs),
        scratch_shapes=scratch,
        compiler_params=pltpu.CompilerParams(vmem_limit_bytes=limit * 2**20),
        cost_estimate=pl.CostEstimate(flops=flops, bytes_accessed=2**20, transcendentals=0),
        name=name,
    )(*args)
    return list(made)


class Loads:
    def __init__(self, args, targets, sems, couplers=(0, 1), blocks=True):
        order = [(0, 0), (1, 0), (3, 1), (2, 1), (1, 1), (0, 1), (3, 0), (2, 0)]
        self.copies = {
            (which, slab): pltpu.make_async_copy(
                args[which].at[slab], targets[which].at[slab], sems.at[index]
            )
            for index, (which, slab) in enumerate(order)
            if (blocks if which < 2 else slab in couplers)
        }
        self.targets = targets
        for copy in self.copies.values():
            copy.start()

    def get(self, which, slab):
        self.copies[which, slab].wait()
        return self.targets[which].at[slab]

    def green(self, slab):
        return row_form(self.get(0, slab))

    def sigma(self, slab):
        return row_form(self.get(1, slab))

    def coupler(self, slab):
        tiles = self.get(3, slab)
        return couple(self.get(2, slab), tiles)


def load_scratch(size, blocks):
    return [
        pltpu.VMEM((2, 2, size, size), F32),
        pltpu.VMEM((2, 2, size, size), F32),
        pltpu.VMEM((2, 2, size, size), F32),
        pltpu.VMEM((2, blocks, blocks), jnp.int32),
        pltpu.SemaphoreType.DMA((8,)),
    ]


def left_sources(loads, whole, source, coupler_out, m_a, m_b, m_c):
    first = loads.green(0)
    put(m_b, first)
    put(m_a, loads.sigma(0))
    made = first + times(times(first, m_a), m_b)
    if source is not None:
        source[...] = made
    put(m_a, made)
    coupler = loads.coupler(1)
    if coupler_out is not None:
        coupler_out[...] = coupler
    put(m_c, coupler)
    inner = loads.sigma(1) + times(times(coupler, m_a), m_c, True)
    put(m_a, inner)
    second = loads.green(1)
    put(m_b, second)
    whole[...] = second + times(times(second, m_a), m_b)
    return first, second


def source_kernel(green, sigma, coupling, pattern, whole, *scratch):
    @pl.when(lax.axis_index("slab") == 0)
    def _():
        loads = Loads((green, sigma, coupling, pattern), scratch[:4], scratch[4], (1,))
        left_sources(loads, whole, None, None, *scratch[5:])

    @pl.when((lax.axis_index("slab") > 0) & (parity() == 1))
    def _():
        loads = Loads((green, sigma, coupling, pattern), scratch[:4], scratch[4], (0,), False)
        whole[...] = loads.coupler(0)


def map_kernel(
    green, sigma, coupling, pattern,
    whole, source, coupler, opening, lead, tail, forward, backward, *scratch,
):
    m_a, m_b, m_c = scratch[5:]
    loads = Loads((green, sigma, coupling, pattern), scratch[:4], scratch[4])
    first, second = left_sources(loads, whole, source, coupler, m_a, m_b, m_c)
    before = loads.coupler(0)

    @pl.when(lax.axis_index("slab") > 0)
    def _():
        opening[...] = before
        put(m_a, before)
        ahead = times(first, m_a)
        forward[...] = ahead
        put(m_a, ahead)
        lead[0], lead[1] = split(times(times(second, m_c), m_a))
        put(m_a, first)
        size = before.shape[0]
        behind = times(adjoint_row((before[:, :size], before[:, size:])), m_a)
        backward[...] = behind
        put(tail, times(times(behind, m_c, True), m_b))


def right_terms(first, last, coupler, m_coupler, m_first, m_last, m_upper):
    put(m_coupler, coupler)
    put(m_last, last)
    through = times(times(first, m_coupler, True), m_last)
    put(m_first, first)
    put(m_upper, times(coupler, m_first))
    return through, first + times(through, m_upper)


def prepare_kernel(count, *refs):
    arrived, wholes = refs[: count - 1], refs[count - 1 : 2 * count - 2]
    refs = refs[2 * count - 2 :]
    start_whole, source, forward, backward, coupler = refs[:5]
    followings = refs[5:7]
    lead, tail, constant, last_lead, last_tail = refs[7:12]
    first_v, last_v, m_a, m_b, m_c, m_d = refs[12:]
    place = lax.axis_index("slab")

    @pl.when(place == 0)
    def _():
        first_v[...] = source[...]
        last_v[...] = start_whole[...]

    for turn in range(count - 1):
        @pl.when((place > 0) & (place == turn + 1 - parity()))
        def _(turn=turn):
            last_v[...] = wholes[turn][...]
            put(m_a, arrived[turn][...])

    @pl.when((place > 0) & (place < count - 1))
    def _():
        put(m_b, backward[...])
        first_v[...] = source[...] + times(times(forward[...], m_a), m_b)

    @pl.when(place < count - 1)
    def _():
        first, last = first_v[...], last_v[...]
        through, joined = right_terms(first, last, coupler[...], m_a, m_b, m_c, m_d)
        constant[...] = joined
        next_coupler = jnp.where(parity() == 0, followings[0][...], followings[1][...])
        put(m_a, next_coupler)
        lead[0], lead[1] = split(times(through, m_a, True))
        last_lead[0], last_lead[1] = split(times(last, m_a, True))
        behind = times(next_coupler, m_c)
        put(last_tail, behind)
        put(tail, times(behind, m_d))


def apply_map(mapping, m_x):
    lead, tail, constant = mapping
    return constant[...] + times(times_split(lead[0], lead[1], m_x), tail)


def relay_kernel(step, count, lefts, rights, *refs):
    refs = list(refs)
    place = lax.axis_index("slab")
    turn = step - parity()
    is_left = (turn >= 0) & (turn <= count - 2) & (place == turn + 1)
    is_right = (turn >= count - 1) & (place == 2 * count - 3 - turn)
    closing = lefts and step >= count - 2
    arrived = refs.pop(0)
    left_map = [refs.pop(0) for _ in range(3)] if lefts else None
    right_map = [refs.pop(0) for _ in range(3)] if rights else None
    if closing:
        forward, backward, source, coupler = [refs.pop(0) for _ in range(4)]
    out = refs.pop(0)
    if closing:
        end, m_x, m_a, m_b, m_c = refs
    else:
        (m_x,) = refs

    if step == 0:
        @pl.when(place == 0)
        def _():
            out[...] = left_map[2][...]

    if lefts:
        @pl.when(is_left)
        def _():
            put(m_x, arrived[...])
            out[...] = apply_map(left_map, m_x)

    if closing:
        @pl.when(is_left & (place == count - 1))
        def _():
            last = out[...]
            end[...] = last
            put(m_a, backward[...])
            first = source[...] + times(times(forward[...], m_x), m_a)
            _, joined = right_terms(first, last, coupler[...], m_a, m_b, m_c, m_x)
            out[...] = joined

    if rights:
        @pl.when(is_right)
        def _():
            put(m_x, arrived[...])
            out[...] = apply_map(right_map, m_x)


def finish_kernel(count, *refs):
    refs = list(refs)
    arrived = [refs.pop(0) for _ in range(count)]
    outs = [refs.pop(0) for _ in range(count)]
    ends = [refs.pop(0) for _ in range(2)]
    right_map = [refs.pop(0) for _ in range(3)]
    last_lead, last_tail, whole_start = [refs.pop(0) for _ in range(3)]
    wholes = [refs.pop(0) for _ in range(count - 1)]
    retarded = refs.pop(0)
    out_v, whole_v, m_x = refs[-3:]
    parcels = refs[:-3]
    place = lax.axis_index("slab")
    core = parity()
    size = out_v.shape[0]
    is_last = place == count - 1
    at = jnp.where(is_last, count - 2 + core, 2 * count - 3 - place + core)
    late = (place == 0) & (core == 1)

    for index in range(count):
        @pl.when(at == count - 1 + index)
        def _(index=index):
            put(m_x, arrived[index][...])

        @pl.when(at == count - 2 + index)
        def _(index=index):
            out_v[...] = outs[index][...]

    for index in range(2):
        @pl.when(is_last & (core == index))
        def _(index=index):
            whole_v[...] = ends[index][...]

    @pl.when(late)
    def _():
        out_v[...] = apply_map(right_map, m_x)

    @pl.when(place == 0)
    def _():
        whole_v[...] = apply_map((last_lead, last_tail, whole_start), m_x)

    for index in range(count - 1):
        @pl.when((place > 0) & jnp.logical_not(is_last) & (place - 1 + core == index))
        def _(index=index):
            whole_v[...] = apply_map((last_lead, last_tail, wholes[index]), m_x)

    for slab, block in enumerate((out_v, whole_v)):
        for part in range(2):
            retarded[slab, part] = block[:, part * size : (part + 1) * size]
    for mask, parcel in enumerate(parcels):
        for slab, block in enumerate((out_v, whole_v)):
            parcel[slab] = block[share(mask, parcel.shape[1]), :]


def share(mask, rows):
    chip = lax.shift_right_logical(lax.axis_index("energy"), 1)
    return pl.ds(pl.multiple_of(lax.bitwise_xor(chip, mask) * rows, rows), rows)


def mix_kernel(chips, weights, *refs):
    parcels, (mine, other) = refs[:chips], refs[chips:]
    energy = lax.axis_index("energy")
    core = lax.rem(energy, 2)
    sources = [lax.bitwise_xor(energy, 2 * mask) for mask in range(chips)]
    for mask in range(chips):
        for target, out in ((sources[mask], mine), (sources[mask] + 1 - 2 * core, other)):
            total = weights[target, sources[0]] * parcels[0][...]
            for index in range(1, chips):
                total += weights[target, sources[index]] * parcels[index][...]
            out[mask] = total


def sum_kernel(chips, mine, other, *outs):
    for mask in range(chips):
        outs[mask][...] = mine[mask] + other[mask]


def place_kernel(chips, *refs):
    parcels, scattering = refs[:chips], refs[chips]
    size = scattering.shape[-1]
    for mask, parcel in enumerate(parcels):
        where = share(mask, parcel.shape[1])
        for slab in range(2):
            for part in range(2):
                scattering[slab, part, where, :] = parcel[
                    slab, :, part * size : (part + 1) * size
                ]


def mode_weights(targets, sources, offsets, emission, absorption):
    spacing = sources[None, :, None] - targets[:, None, None]
    emitted = jnp.where(
        spacing == -offsets[None, None, :],
        emission[None, None, :],
        jnp.zeros_like(emission)[None, None, :],
    )
    absorbed = jnp.where(
        spacing == offsets[None, None, :],
        absorption[None, None, :],
        jnp.zeros_like(absorption)[None, None, :],
    )
    return jnp.sum(emitted + absorbed, axis=-1)


def relay_pairs(step, energies, count):
    pairs = []
    for energy in range(energies):
        turn = step - energy % 2
        if turn < 0:
            pairs += [(energy * count + i, energy * count + i - 1) for i in range(1, count)]
            continue
        if turn <= count - 2:
            ends = (turn, turn + 1)
        elif count - 1 <= turn <= 2 * count - 3:
            ends = (2 * count - 2 - turn, 2 * count - 3 - turn)
        else:
            continue
        pairs.append(tuple(energy * count + end for end in ends))
    return pairs


def shards(energies, count, free_green, self_energy, coupling, pattern, offsets, emission, absorption):
    size, blocks = free_green.shape[-1], pattern.shape[-1]
    args = (free_green[0], self_energy[0], coupling, pattern)
    row = shape(size, 2 * size)
    lead = shape(size, 2 * size, HALF, 2)
    tail = shape(2 * size, 2 * size, HALF, 2)
    row_v = pltpu.VMEM(row.shape, F32)
    product = 24 * size**3
    loading = load_scratch(size, blocks) + matrices(3, size)

    def relay(step, value):
        return lax.ppermute(value, ("energy", "slab"), relay_pairs(step, energies, count))

    begun = call(
        source_kernel,
        [row],
        loading,
        args,
        [HBM] * 4,
        flops=6 * product,
        name="source",
        limit=58,
    )
    arrived, outs, ends = [relay(0, begun[0])], [], []
    whole, source, coupler, opening, left_lead, left_tail, forward, backward = call(
        map_kernel,
        [row] * 4 + [lead, tail, row, row],
        loading,
        args,
        [HBM] * 4,
        flops=12 * product,
        name="left_maps",
        limit=42,
    )
    left_map = [left_lead, left_tail, whole]
    right_map = following = None
    for step in range(2 * count - 2):
        lefts, rights = step <= count - 1, step >= count - 1
        closing = lefts and step >= count - 2
        args = [arrived[step]]
        if lefts:
            args += left_map
        if rights:
            args += right_map[:3]
        if closing:
            args += [forward, backward, source, coupler]
        made = call(
            functools.partial(relay_kernel, step, count, lefts, rights),
            [row] * (2 if closing else 1),
            matrices(4 if closing else 1, size),
            args,
            flops=2 * product,
            name="relay",
        )
        outs.append(made[0])
        ends += made[1:]
        arrived.append(relay(step + 1, made[0]))
        if step == 0:
            down = [
                (energy * count + i, energy * count + i - 1)
                for energy in range(0, energies, 2)
                for i in range(1, count)
            ]
            following = lax.ppermute(opening, ("energy", "slab"), down)
        if step == count - 2:
            args = arrived[: count - 1] + outs[: count - 1]
            args += [whole, source, forward, backward, coupler, following, arrived[0]]
            right_map = call(
                functools.partial(prepare_kernel, count),
                [lead, tail, row, lead, tail],
                [row_v] * 2 + matrices(4, size),
                args,
                flops=10 * product,
                name="right_maps",
            )
    args = arrived[count - 1 :] + outs[count - 2 :] + ends + right_map + [whole] + outs[: count - 1]
    chips = energies // 2
    parcel = shape(size // chips, 2 * size, F32, 2)
    retarded, *parcels = call(
        functools.partial(finish_kernel, count),
        [shape(size, size, F32, 2, 2)] + [parcel] * chips,
        [row_v] * 2 + matrices(1, size),
        args,
        flops=4 * product,
        name="retarded",
    )

    def exchange(values):
        return values[:1] + [
            lax.ppermute(value, "energy", [(i, i ^ (2 * mask)) for i in range(energies)])
            for mask, value in enumerate(values)
            if mask
        ]

    everyone = jnp.arange(energies, dtype=jnp.int32)
    weights = mode_weights(everyone, everyone, offsets, emission, absorption)
    partial = shape(size // chips, 2 * size, F32, chips, 2)
    mine, other = call(
        functools.partial(mix_kernel, chips),
        [partial] * 2,
        [],
        [weights] + exchange(parcels),
        [SMEM] + [VMEM] * chips,
        flops=product // 4,
        name="mix",
    )
    other = lax.ppermute(other, "energy", [(i, i ^ 1) for i in range(energies)])
    parcels = call(
        functools.partial(sum_kernel, chips), [parcel] * chips, [], [mine, other], name="sum"
    )
    (scattering,) = call(
        functools.partial(place_kernel, chips),
        [shape(size, size, F32, 2, 2)],
        [],
        exchange(parcels),
        name="scattering",
    )
    return (retarded[None], scattering[None])


def solution(mesh):
    blocks = P("energy", "slab", None, None, None)
    in_specs = (blocks, blocks, P("slab", None, None, None), P("slab", None, None), P(), P(), P())
    body = functools.partial(shards, mesh.shape["energy"], mesh.shape["slab"])
    return jax.shard_map(
        body, mesh=mesh, in_specs=in_specs, out_specs=(blocks, blocks), check_vma=False
    )
```

```python
import functools

import jax
import jax.numpy as jnp
from jax import lax
from jax.experimental import pallas as pl
from jax.experimental.pallas import tpu as pltpu
from jax.sharding import PartitionSpec as P

F32 = jnp.float32
HALF = jnp.bfloat16
HBM = pl.BlockSpec(memory_space=pltpu.HBM)
VMEM = pl.BlockSpec(memory_space=pltpu.VMEM)
SMEM = pl.BlockSpec(memory_space=pltpu.SMEM)


def split(value):
    high = value.astype(HALF)
    return high, (value - high.astype(F32)).astype(HALF)


def dot(left, right, transposed):
    dims = (((1,), (1 if transposed else 0,)), ((), ()))
    return lax.dot_general(left, right, dims, preferred_element_type=F32)


def parts_of(block, adjoint=False):
    size = block.shape[0]
    real, imag = block[:, :size], block[:, size:]
    return real, imag, (real - imag if adjoint else real + imag)


def put(matrix, block, adjoint=False):
    for index, part in enumerate(parts_of(block, adjoint)):
        matrix[0, index], matrix[1, index] = split(part)


def times_split(left, matrix, transposed=False):
    products = []
    for index, (high, low) in enumerate(left):
        size = high.shape[0]
        both = dot(jnp.concatenate([high, low], axis=0), matrix[0, index], transposed)
        products.append(both[:size] + both[size:] + dot(high, matrix[1, index], transposed))
    first, second, third = products
    if transposed:
        return jnp.concatenate([first + second, third - first + second], axis=1)
    return jnp.concatenate([first - second, third - first - second], axis=1)


def times(block, matrix, transposed=False):
    return times_split([split(part) for part in parts_of(block)], matrix, transposed)


def row_form(pair):
    return jnp.concatenate([pair[0], pair[1]], axis=1)


def adjoint_row(pair):
    return jnp.concatenate([jnp.transpose(pair[0]), -jnp.transpose(pair[1])], axis=1)


def expand(pattern, size):
    blocks = pattern.shape[0]
    tile = size // blocks
    rows = lax.broadcasted_iota(jnp.int32, (size, blocks), 0)
    first = lax.broadcasted_iota(jnp.int32, (size, blocks), 1) * tile
    member = jnp.where((rows >= first) & (rows < first + tile), 1.0, 0.0).astype(HALF)
    tall = dot(member, pattern.astype(F32).astype(HALF), False)
    return dot(tall.astype(HALF), member, True)


def couple(coupling, pattern):
    mask = expand(pattern[...], coupling.shape[-1])
    return jnp.concatenate([coupling[0] * mask, coupling[1] * mask], axis=1)


def parity():
    return lax.rem(lax.axis_index("energy"), 2)


def shape(rows, columns, dtype=F32, *lead):
    return jax.ShapeDtypeStruct(lead + (rows, columns), dtype)


def matrices(number, size):
    return [pltpu.VMEM((2, 3, size, size), HALF)] * number


def call(kernel, outs, scratch, args, specs=None, flops=0, name=None, limit=40):
    made = pl.pallas_call(
        kernel,
        out_shape=outs,
        in_specs=specs or [VMEM] * len(args),
        out_specs=[VMEM] * len(outs),
        scratch_shapes=scratch,
        compiler_params=pltpu.CompilerParams(vmem_limit_bytes=limit * 2**20),
        cost_estimate=pl.CostEstimate(flops=flops, bytes_accessed=2**20, transcendentals=0),
        name=name,
    )(*args)
    return list(made)


class Loads:
    def __init__(self, args, targets, sems, couplers=(0, 1), blocks=True):
        order = [(0, 0), (1, 0), (3, 1), (2, 1), (1, 1), (0, 1), (3, 0), (2, 0)]
        self.copies = {
            (which, slab): pltpu.make_async_copy(
                args[which].at[slab], targets[which].at[slab], sems.at[index]
            )
            for index, (which, slab) in enumerate(order)
            if (blocks if which < 2 else slab in couplers)
        }
        self.targets = targets
        for copy in self.copies.values():
            copy.start()

    def get(self, which, slab):
        self.copies[which, slab].wait()
        return self.targets[which].at[slab]

    def green(self, slab):
        return row_form(self.get(0, slab))

    def sigma(self, slab):
        return row_form(self.get(1, slab))

    def coupler(self, slab):
        tiles = self.get(3, slab)
        return couple(self.get(2, slab), tiles)


def load_scratch(size, blocks):
    return [
        pltpu.VMEM((2, 2, size, size), F32),
        pltpu.VMEM((2, 2, size, size), F32),
        pltpu.VMEM((2, 2, size, size), F32),
        pltpu.VMEM((2, blocks, blocks), jnp.int32),
        pltpu.SemaphoreType.DMA((8,)),
    ]


def left_sources(loads, whole, source, coupler_out, m_a, m_b, m_c):
    first = loads.green(0)
    put(m_b, first)
    put(m_a, loads.sigma(0))
    made = first + times(times(first, m_a), m_b)
    if source is not None:
        source[...] = made
    put(m_a, made)
    coupler = loads.coupler(1)
    if coupler_out is not None:
        coupler_out[...] = coupler
    put(m_c, coupler, True)
    inner = loads.sigma(1) + times(times(coupler, m_a), m_c, True)
    put(m_a, inner)
    second = loads.green(1)
    put(m_b, second)
    whole[...] = second + times(times(second, m_a), m_b)
    return first, second


def source_kernel(green, sigma, coupling, pattern, whole, *scratch):
    @pl.when(lax.axis_index("slab") == 0)
    def _():
        loads = Loads((green, sigma, coupling, pattern), scratch[:4], scratch[4], (1,))
        left_sources(loads, whole, None, None, *scratch[5:])

    @pl.when((lax.axis_index("slab") > 0) & (parity() == 1))
    def _():
        loads = Loads((green, sigma, coupling, pattern), scratch[:4], scratch[4], (0,), False)
        whole[...] = loads.coupler(0)


def map_kernel(
    green, sigma, coupling, pattern,
    whole, source, coupler, opening, lead, tail, forward, backward, *scratch,
):
    m_a, m_b, m_c = scratch[5:]
    loads = Loads((green, sigma, coupling, pattern), scratch[:4], scratch[4])
    first, second = left_sources(loads, whole, source, coupler, m_a, m_b, m_c)
    before = loads.coupler(0)

    @pl.when(lax.axis_index("slab") > 0)
    def _():
        opening[...] = before
        put(m_a, first)
        size = before.shape[0]
        behind = times(adjoint_row((before[:, :size], before[:, size:])), m_a)
        backward[...] = behind
        put(tail, times(times(behind, m_c, True), m_b))
        put(m_a, before)
        ahead = times(first, m_a)
        forward[...] = ahead
        put(m_a, ahead)
        put(m_c, coupler[...])
        put(lead, times(times(second, m_c), m_a))


def right_terms(first, last, coupler, m_coupler, m_first, m_last, m_upper):
    put(m_coupler, coupler, True)
    put(m_last, last)
    through = times(times(first, m_coupler, True), m_last)
    put(m_first, first)
    put(m_upper, times(coupler, m_first))
    return through, first + times(through, m_upper)


def prepare_kernel(count, *refs):
    arrived, wholes = refs[: count - 1], refs[count - 1 : 2 * count - 2]
    refs = refs[2 * count - 2 :]
    start_whole, source, forward, backward, coupler = refs[:5]
    followings = refs[5:7]
    lead, tail, constant, last_lead, last_tail = refs[7:12]
    first_v, last_v, m_a, m_b, m_c, m_d = refs[12:]
    place = lax.axis_index("slab")

    @pl.when(place == 0)
    def _():
        first_v[...] = source[...]
        last_v[...] = start_whole[...]

    for turn in range(count - 1):
        @pl.when((place > 0) & (place == turn + 1 - parity()))
        def _(turn=turn):
            last_v[...] = wholes[turn][...]
            put(m_a, arrived[turn][...])

    @pl.when((place > 0) & (place < count - 1))
    def _():
        put(m_b, backward[...])
        first_v[...] = source[...] + times(times(forward[...], m_a), m_b)

    @pl.when(place < count - 1)
    def _():
        first, last = first_v[...], last_v[...]
        through, joined = right_terms(first, last, coupler[...], m_a, m_b, m_c, m_d)
        constant[...] = joined
        next_coupler = jnp.where(parity() == 0, followings[0][...], followings[1][...])
        put(m_a, next_coupler, True)
        put(lead, times(through, m_a, True))
        put(last_lead, times(last, m_a, True))
        behind = times(next_coupler, m_c)
        put(last_tail, behind)
        put(tail, times(behind, m_d))


def apply_map(mapping, m_x):
    lead, tail, constant = mapping
    ahead = [(lead[0, index], lead[1, index]) for index in range(3)]
    return constant[...] + times(times_split(ahead, m_x), tail)


def relay_kernel(step, count, lefts, rights, *refs):
    refs = list(refs)
    place = lax.axis_index("slab")
    turn = step - parity()
    is_left = (turn >= 0) & (turn <= count - 2) & (place == turn + 1)
    is_right = (turn >= count - 1) & (place == 2 * count - 3 - turn)
    closing = lefts and step >= count - 2
    arrived = refs.pop(0)
    left_map = [refs.pop(0) for _ in range(3)] if lefts else None
    right_map = [refs.pop(0) for _ in range(3)] if rights else None
    if closing:
        forward, backward, source, coupler = [refs.pop(0) for _ in range(4)]
    out = refs.pop(0)
    if closing:
        end, m_x, m_a, m_b, m_c = refs
    else:
        (m_x,) = refs

    if step == 0:
        @pl.when(place == 0)
        def _():
            out[...] = left_map[2][...]

    if lefts:
        @pl.when(is_left)
        def _():
            put(m_x, arrived[...])
            out[...] = apply_map(left_map, m_x)

    if closing:
        @pl.when(is_left & (place == count - 1))
        def _():
            last = out[...]
            end[...] = last
            put(m_a, backward[...])
            first = source[...] + times(times(forward[...], m_x), m_a)
            _, joined = right_terms(first, last, coupler[...], m_a, m_b, m_c, m_x)
            out[...] = joined

    if rights:
        @pl.when(is_right)
        def _():
            put(m_x, arrived[...])
            out[...] = apply_map(right_map, m_x)


def finish_kernel(count, *refs):
    refs = list(refs)
    arrived = [refs.pop(0) for _ in range(count)]
    outs = [refs.pop(0) for _ in range(count)]
    ends = [refs.pop(0) for _ in range(2)]
    right_map = [refs.pop(0) for _ in range(3)]
    last_lead, last_tail, whole_start = [refs.pop(0) for _ in range(3)]
    wholes = [refs.pop(0) for _ in range(count - 1)]
    retarded = refs.pop(0)
    out_v, whole_v, m_x = refs[-3:]
    parcels = refs[:-3]
    place = lax.axis_index("slab")
    core = parity()
    size = out_v.shape[0]
    is_last = place == count - 1
    at = jnp.where(is_last, count - 2 + core, 2 * count - 3 - place + core)
    late = (place == 0) & (core == 1)

    for index in range(count):
        @pl.when(at == count - 1 + index)
        def _(index=index):
            put(m_x, arrived[index][...])

        @pl.when(at == count - 2 + index)
        def _(index=index):
            out_v[...] = outs[index][...]

    for index in range(2):
        @pl.when(is_last & (core == index))
        def _(index=index):
            whole_v[...] = ends[index][...]

    @pl.when(late)
    def _():
        out_v[...] = apply_map(right_map, m_x)

    @pl.when(place == 0)
    def _():
        whole_v[...] = apply_map((last_lead, last_tail, whole_start), m_x)

    for index in range(count - 1):
        @pl.when((place > 0) & jnp.logical_not(is_last) & (place - 1 + core == index))
        def _(index=index):
            whole_v[...] = apply_map((last_lead, last_tail, wholes[index]), m_x)

    for slab, block in enumerate((out_v, whole_v)):
        for part in range(2):
            retarded[slab, part] = block[:, part * size : (part + 1) * size]
    for mask, parcel in enumerate(parcels):
        for slab, block in enumerate((out_v, whole_v)):
            parcel[slab] = block[share(mask, parcel.shape[1]), :]


def share(mask, rows):
    chip = lax.shift_right_logical(lax.axis_index("energy"), 1)
    return pl.ds(pl.multiple_of(lax.bitwise_xor(chip, mask) * rows, rows), rows)


def mix_kernel(chips, weights, *refs):
    parcels, (mine, other) = refs[:chips], refs[chips:]
    energy = lax.axis_index("energy")
    core = lax.rem(energy, 2)
    sources = [lax.bitwise_xor(energy, 2 * mask) for mask in range(chips)]
    for mask in range(chips):
        for target, out in ((sources[mask], mine), (sources[mask] + 1 - 2 * core, other)):
            total = weights[target, sources[0]] * parcels[0][...]
            for index in range(1, chips):
                total += weights[target, sources[index]] * parcels[index][...]
            out[mask] = total


def sum_kernel(chips, mine, other, *outs):
    for mask in range(chips):
        outs[mask][...] = mine[mask] + other[mask]


def place_kernel(chips, *refs):
    parcels, scattering = refs[:chips], refs[chips]
    size = scattering.shape[-1]
    for mask, parcel in enumerate(parcels):
        where = share(mask, parcel.shape[1])
        for slab in range(2):
            for part in range(2):
                scattering[slab, part, where, :] = parcel[
                    slab, :, part * size : (part + 1) * size
                ]


def mode_weights(targets, sources, offsets, emission, absorption):
    spacing = sources[None, :, None] - targets[:, None, None]
    emitted = jnp.where(
        spacing == -offsets[None, None, :],
        emission[None, None, :],
        jnp.zeros_like(emission)[None, None, :],
    )
    absorbed = jnp.where(
        spacing == offsets[None, None, :],
        absorption[None, None, :],
        jnp.zeros_like(absorption)[None, None, :],
    )
    return jnp.sum(emitted + absorbed, axis=-1)


def relay_pairs(step, energies, count):
    pairs = []
    for energy in range(energies):
        turn = step - energy % 2
        if turn < 0:
            pairs += [(energy * count + i, energy * count + i - 1) for i in range(1, count)]
            continue
        if turn <= count - 2:
            ends = (turn, turn + 1)
        elif count - 1 <= turn <= 2 * count - 3:
            ends = (2 * count - 2 - turn, 2 * count - 3 - turn)
        else:
            continue
        pairs.append(tuple(energy * count + end for end in ends))
    return pairs


def shards(energies, count, free_green, self_energy, coupling, pattern, offsets, emission, absorption):
    size, blocks = free_green.shape[-1], pattern.shape[-1]
    args = (free_green[0], self_energy[0], coupling, pattern)
    row = shape(size, 2 * size)
    factor = shape(size, size, HALF, 2, 3)
    row_v = pltpu.VMEM(row.shape, F32)
    product = 24 * size**3
    loading = load_scratch(size, blocks) + matrices(3, size)

    def relay(step, value):
        return lax.ppermute(value, ("energy", "slab"), relay_pairs(step, energies, count))

    begun = call(
        source_kernel,
        [row],
        loading,
        args,
        [HBM] * 4,
        flops=6 * product,
        name="source",
        limit=58,
    )
    arrived, outs, ends = [relay(0, begun[0])], [], []
    whole, source, coupler, opening, left_lead, left_tail, forward, backward = call(
        map_kernel,
        [row] * 4 + [factor, factor, row, row],
        loading,
        args,
        [HBM] * 4,
        flops=12 * product,
        name="left_maps",
        limit=42,
    )
    left_map = [left_lead, left_tail, whole]
    right_map = following = None
    for step in range(2 * count - 2):
        lefts, rights = step <= count - 1, step >= count - 1
        closing = lefts and step >= count - 2
        args = [arrived[step]]
        if lefts:
            args += left_map
        if rights:
            args += right_map[:3]
        if closing:
            args += [forward, backward, source, coupler]
        made = call(
            functools.partial(relay_kernel, step, count, lefts, rights),
            [row] * (2 if closing else 1),
            matrices(4 if closing else 1, size),
            args,
            flops=2 * product,
            name="relay",
        )
        outs.append(made[0])
        ends += made[1:]
        arrived.append(relay(step + 1, made[0]))
        if step == 0:
            down = [
                (energy * count + i, energy * count + i - 1)
                for energy in range(0, energies, 2)
                for i in range(1, count)
            ]
            following = lax.ppermute(opening, ("energy", "slab"), down)
        if step == count - 2:
            args = arrived[: count - 1] + outs[: count - 1]
            args += [whole, source, forward, backward, coupler, following, arrived[0]]
            right_map = call(
                functools.partial(prepare_kernel, count),
                [factor, factor, row, factor, factor],
                [row_v] * 2 + matrices(4, size),
                args,
                flops=10 * product,
                name="right_maps",
            )
    args = arrived[count - 1 :] + outs[count - 2 :] + ends + right_map + [whole] + outs[: count - 1]
    chips = energies // 2
    parcel = shape(size // chips, 2 * size, F32, 2)
    retarded, *parcels = call(
        functools.partial(finish_kernel, count),
        [shape(size, size, F32, 2, 2)] + [parcel] * chips,
        [row_v] * 2 + matrices(1, size),
        args,
        flops=4 * product,
        name="retarded",
    )

    def exchange(values):
        return values[:1] + [
            lax.ppermute(value, "energy", [(i, i ^ (2 * mask)) for i in range(energies)])
            for mask, value in enumerate(values)
            if mask
        ]

    everyone = jnp.arange(energies, dtype=jnp.int32)
    weights = mode_weights(everyone, everyone, offsets, emission, absorption)
    partial = shape(size // chips, 2 * size, F32, chips, 2)
    mine, other = call(
        functools.partial(mix_kernel, chips),
        [partial] * 2,
        [],
        [weights] + exchange(parcels),
        [SMEM] + [VMEM] * chips,
        flops=product // 4,
        name="mix",
    )
    other = lax.ppermute(other, "energy", [(i, i ^ 1) for i in range(energies)])
    parcels = call(
        functools.partial(sum_kernel, chips), [parcel] * chips, [], [mine, other], name="sum"
    )
    (scattering,) = call(
        functools.partial(place_kernel, chips),
        [shape(size, size, F32, 2, 2)],
        [],
        exchange(parcels),
        name="scattering",
    )
    return (retarded[None], scattering[None])


def solution(mesh):
    blocks = P("energy", "slab", None, None, None)
    in_specs = (blocks, blocks, P("slab", None, None, None), P("slab", None, None), P(), P(), P())
    body = functools.partial(shards, mesh.shape["energy"], mesh.shape["slab"])
    return jax.shard_map(
        body, mesh=mesh, in_specs=in_specs, out_specs=(blocks, blocks), check_vma=False
    )
```

```python
import functools

import jax
import jax.numpy as jnp
from jax import lax
from jax.experimental import pallas as pl
from jax.experimental.pallas import tpu as pltpu
from jax.sharding import PartitionSpec as P

F32 = jnp.float32
HALF = jnp.bfloat16
HBM = pl.BlockSpec(memory_space=pltpu.HBM)
VMEM = pl.BlockSpec(memory_space=pltpu.VMEM)
SMEM = pl.BlockSpec(memory_space=pltpu.SMEM)


def split(value):
    high = value.astype(HALF)
    return high, (value - high.astype(F32)).astype(HALF)


def dot(left, right, transposed):
    dims = (((1,), (1 if transposed else 0,)), ((), ()))
    return lax.dot_general(left, right, dims, preferred_element_type=F32)


def parts_of(block, adjoint=False):
    size = block.shape[0]
    real, imag = block[:, :size], block[:, size:]
    return real, imag, (real - imag if adjoint else real + imag)


def put(matrix, block, adjoint=False):
    for index, part in enumerate(parts_of(block, adjoint)):
        matrix[0, index], matrix[1, index] = split(part)


def times_split(left, matrix, transposed=False):
    products = []
    for index, (high, low) in enumerate(left):
        size = high.shape[0]
        both = dot(jnp.concatenate([high, low], axis=0), matrix[0, index], transposed)
        products.append(both[:size] + both[size:] + dot(high, matrix[1, index], transposed))
    first, second, third = products
    if transposed:
        return jnp.concatenate([first + second, third - first + second], axis=1)
    return jnp.concatenate([first - second, third - first - second], axis=1)


def times(block, matrix, transposed=False):
    return times_split([split(part) for part in parts_of(block)], matrix, transposed)


def row_form(pair):
    return jnp.concatenate([pair[0], pair[1]], axis=1)


def adjoint_row(pair):
    return jnp.concatenate([jnp.transpose(pair[0]), -jnp.transpose(pair[1])], axis=1)


def expand(pattern, size):
    blocks = pattern.shape[0]
    tile = size // blocks
    rows = lax.broadcasted_iota(jnp.int32, (size, blocks), 0)
    first = lax.broadcasted_iota(jnp.int32, (size, blocks), 1) * tile
    member = jnp.where((rows >= first) & (rows < first + tile), 1.0, 0.0).astype(HALF)
    tall = dot(member, pattern.astype(F32).astype(HALF), False)
    return dot(tall.astype(HALF), member, True)


def couple(coupling, pattern):
    mask = expand(pattern[...], coupling.shape[-1])
    return jnp.concatenate([coupling[0] * mask, coupling[1] * mask], axis=1)


def parity():
    return lax.rem(lax.axis_index("energy"), 2)


def shape(rows, columns, dtype=F32, *lead):
    return jax.ShapeDtypeStruct(lead + (rows, columns), dtype)


def matrices(number, size):
    return [pltpu.VMEM((2, 3, size, size), HALF)] * number


def call(kernel, outs, scratch, args, specs=None, flops=0, name=None, limit=40):
    made = pl.pallas_call(
        kernel,
        out_shape=outs,
        in_specs=specs or [VMEM] * len(args),
        out_specs=[VMEM] * len(outs),
        scratch_shapes=scratch,
        compiler_params=pltpu.CompilerParams(vmem_limit_bytes=limit * 2**20),
        cost_estimate=pl.CostEstimate(flops=flops, bytes_accessed=2**20, transcendentals=0),
        name=name,
    )(*args)
    return list(made)


class Loads:
    def __init__(self, args, targets, sems, couplers=(0, 1), blocks=True):
        order = [(0, 0), (1, 0), (3, 1), (2, 1), (1, 1), (0, 1), (3, 0), (2, 0)]
        self.copies = {
            (which, slab): pltpu.make_async_copy(
                args[which].at[slab], targets[which].at[slab], sems.at[index]
            )
            for index, (which, slab) in enumerate(order)
            if (blocks if which < 2 else slab in couplers)
        }
        self.targets = targets
        for copy in self.copies.values():
            copy.start()

    def get(self, which, slab):
        self.copies[which, slab].wait()
        return self.targets[which].at[slab]

    def green(self, slab):
        return row_form(self.get(0, slab))

    def sigma(self, slab):
        return row_form(self.get(1, slab))

    def coupler(self, slab):
        tiles = self.get(3, slab)
        return couple(self.get(2, slab), tiles)


def load_scratch(size, blocks):
    return [
        pltpu.VMEM((2, 2, size, size), F32),
        pltpu.VMEM((2, 2, size, size), F32),
        pltpu.VMEM((2, 2, size, size), F32),
        pltpu.VMEM((2, blocks, blocks), jnp.int32),
        pltpu.SemaphoreType.DMA((8,)),
    ]


def left_sources(loads, whole, source, coupler_out, m_a, m_b, m_c):
    first = loads.green(0)
    put(m_b, first)
    put(m_a, loads.sigma(0))
    made = first + times(times(first, m_a), m_b)
    if source is not None:
        source[...] = made
    put(m_a, made)
    coupler = loads.coupler(1)
    if coupler_out is not None:
        coupler_out[...] = coupler
    put(m_c, coupler, True)
    inner = loads.sigma(1) + times(times(coupler, m_a), m_c, True)
    put(m_a, inner)
    second = loads.green(1)
    put(m_b, second)
    whole[...] = second + times(times(second, m_a), m_b)
    return first, second


def source_kernel(green, sigma, coupling, pattern, whole, *scratch):
    @pl.when(lax.axis_index("slab") == 0)
    def _():
        loads = Loads((green, sigma, coupling, pattern), scratch[:4], scratch[4], (1,))
        left_sources(loads, whole, None, None, *scratch[5:])

    @pl.when((lax.axis_index("slab") > 0) & (parity() == 1))
    def _():
        loads = Loads((green, sigma, coupling, pattern), scratch[:4], scratch[4], (0,), False)
        whole[...] = loads.coupler(0)


def map_kernel(
    green, sigma, coupling, pattern,
    whole, source, coupler, opening, lead, tail, forward, backward, *scratch,
):
    m_a, m_b, m_c = scratch[5:]
    loads = Loads((green, sigma, coupling, pattern), scratch[:4], scratch[4])
    first, second = left_sources(loads, whole, source, coupler, m_a, m_b, m_c)
    before = loads.coupler(0)

    @pl.when(lax.axis_index("slab") > 0)
    def _():
        opening[...] = before
        put(m_a, first)
        size = before.shape[0]
        behind = times(adjoint_row((before[:, :size], before[:, size:])), m_a)
        backward[...] = behind
        put(tail, times(times(behind, m_c, True), m_b))
        put(m_a, before)
        ahead = times(first, m_a)
        forward[...] = ahead
        put(m_a, ahead)
        put(m_c, coupler[...])
        put(lead, times(times(second, m_c), m_a))


def right_terms(first, last, coupler, m_coupler, m_first, m_last, m_upper):
    put(m_coupler, coupler, True)
    put(m_last, last)
    through = times(times(first, m_coupler, True), m_last)
    put(m_first, first)
    put(m_upper, times(coupler, m_first))
    return through, first + times(through, m_upper)


def prepare_kernel(count, *refs):
    arrived, wholes = refs[: count - 1], refs[count - 1 : 2 * count - 2]
    refs = refs[2 * count - 2 :]
    start_whole, source, forward, backward, coupler = refs[:5]
    followings = refs[5:7]
    lead, tail, constant, last_lead, last_tail = refs[7:12]
    first_v, last_v, m_a, m_b, m_c, m_d = refs[12:]
    place = lax.axis_index("slab")

    @pl.when(place == 0)
    def _():
        first_v[...] = source[...]
        last_v[...] = start_whole[...]

    for turn in range(count - 1):
        @pl.when((place > 0) & (place == turn + 1 - parity()))
        def _(turn=turn):
            last_v[...] = wholes[turn][...]
            put(m_a, arrived[turn][...])

    @pl.when((place > 0) & (place < count - 1))
    def _():
        put(m_b, backward[...])
        first_v[...] = source[...] + times(times(forward[...], m_a), m_b)

    @pl.when(place < count - 1)
    def _():
        first, last = first_v[...], last_v[...]
        through, joined = right_terms(first, last, coupler[...], m_a, m_b, m_c, m_d)
        constant[...] = joined
        next_coupler = jnp.where(parity() == 0, followings[0][...], followings[1][...])
        put(m_a, next_coupler, True)
        put(lead, times(through, m_a, True))
        put(last_lead, times(last, m_a, True))
        behind = times(next_coupler, m_c)
        put(last_tail, behind)
        put(tail, times(behind, m_d))


def apply_map(mapping, m_x):
    lead, tail, constant = mapping
    ahead = [(lead[0, index], lead[1, index]) for index in range(3)]
    return constant[...] + times(times_split(ahead, m_x), tail)


def relay_kernel(step, count, lefts, rights, *refs):
    refs = list(refs)
    place = lax.axis_index("slab")
    turn = step - parity()
    is_left = (turn >= 0) & (turn <= count - 2) & (place == turn + 1)
    is_right = (turn >= count - 1) & (place == 2 * count - 3 - turn)
    closing = lefts and step >= count - 2
    arrived = refs.pop(0)
    left_map = [refs.pop(0) for _ in range(3)] if lefts else None
    right_map = [refs.pop(0) for _ in range(3)] if rights else None
    if closing:
        forward, backward, source, coupler = [refs.pop(0) for _ in range(4)]
    out = refs.pop(0)
    if closing:
        end, m_x, m_a, m_b, m_c = refs
    else:
        (m_x,) = refs

    if step == 0:
        @pl.when(place == 0)
        def _():
            out[...] = left_map[2][...]

    if lefts:
        @pl.when(is_left)
        def _():
            put(m_x, arrived[...])
            out[...] = apply_map(left_map, m_x)

    if closing:
        @pl.when(is_left & (place == count - 1))
        def _():
            last = out[...]
            end[...] = last
            put(m_a, backward[...])
            first = source[...] + times(times(forward[...], m_x), m_a)
            _, joined = right_terms(first, last, coupler[...], m_a, m_b, m_c, m_x)
            out[...] = joined

    if rights:
        @pl.when(is_right)
        def _():
            put(m_x, arrived[...])
            out[...] = apply_map(right_map, m_x)


def last_kernel(count, *refs):
    refs = list(refs)
    arrived = [refs.pop(0) for _ in range(count)]
    ends = [refs.pop(0) for _ in range(2)]
    last_lead, last_tail, whole_start = [refs.pop(0) for _ in range(3)]
    wholes = [refs.pop(0) for _ in range(count - 1)]
    block, *parcels, m_x = refs
    place = lax.axis_index("slab")
    core = parity()
    is_last = place == count - 1

    for index in range(count):
        @pl.when(jnp.logical_not(is_last) & (2 * count - 3 - place + core == count - 1 + index))
        def _(index=index):
            put(m_x, arrived[index][...])

    for index in range(2):
        @pl.when(is_last & (core == index))
        def _(index=index):
            block[...] = ends[index][...]

    @pl.when(place == 0)
    def _():
        block[...] = apply_map((last_lead, last_tail, whole_start), m_x)

    for index in range(count - 1):
        @pl.when((place > 0) & jnp.logical_not(is_last) & (place - 1 + core == index))
        def _(index=index):
            block[...] = apply_map((last_lead, last_tail, wholes[index]), m_x)

    pack(block, parcels)


def first_kernel(count, *refs):
    refs = list(refs)
    arrived = refs.pop(0)
    outs = [refs.pop(0) for _ in range(count)]
    right_map = [refs.pop(0) for _ in range(3)]
    refs.pop(0)
    block, *parcels, m_x = refs
    place = lax.axis_index("slab")
    core = parity()
    at = jnp.where(place == count - 1, count - 2 + core, 2 * count - 3 - place + core)

    for index in range(count):
        @pl.when(at == count - 2 + index)
        def _(index=index):
            block[...] = outs[index][...]

    @pl.when((place == 0) & (core == 1))
    def _():
        put(m_x, arrived[...])
        block[...] = apply_map(right_map, m_x)

    pack(block, parcels)


def pack(block, parcels):
    for mask, parcel in enumerate(parcels):
        parcel[...] = block[share(mask, parcel.shape[0]), :]


def unpack_kernel(*refs):
    blocks, out = refs[:2], refs[2]
    size = out.shape[-1]
    for slab, block in enumerate(blocks):
        for part in range(2):
            out[slab, part] = block[:, part * size : (part + 1) * size]


def share(mask, rows):
    chip = lax.shift_right_logical(lax.axis_index("energy"), 1)
    return pl.ds(pl.multiple_of(lax.bitwise_xor(chip, mask) * rows, rows), rows)


def mix_kernel(chips, weights, *refs):
    parcels, (mine, other) = refs[:chips], refs[chips:]
    energy = lax.axis_index("energy")
    core = lax.rem(energy, 2)
    sources = [lax.bitwise_xor(energy, 2 * mask) for mask in range(chips)]
    for mask in range(chips):
        for target, out in ((sources[mask], mine), (sources[mask] + 1 - 2 * core, other)):
            total = weights[target, sources[0]] * parcels[0][...]
            for index in range(1, chips):
                total += weights[target, sources[index]] * parcels[index][...]
            out[mask] = total


def sum_kernel(chips, mine, other, *outs):
    for mask in range(chips):
        outs[mask][...] = mine[mask] + other[mask]


def place_kernel(chips, *refs):
    scattering = refs[2 * chips]
    size = scattering.shape[-1]
    for slab in range(2):
        for mask, parcel in enumerate(refs[slab * chips : (slab + 1) * chips]):
            where = share(mask, parcel.shape[0])
            for part in range(2):
                scattering[slab, part, where, :] = parcel[:, part * size : (part + 1) * size]


def mode_weights(targets, sources, offsets, emission, absorption):
    spacing = sources[None, :, None] - targets[:, None, None]
    emitted = jnp.where(
        spacing == -offsets[None, None, :],
        emission[None, None, :],
        jnp.zeros_like(emission)[None, None, :],
    )
    absorbed = jnp.where(
        spacing == offsets[None, None, :],
        absorption[None, None, :],
        jnp.zeros_like(absorption)[None, None, :],
    )
    return jnp.sum(emitted + absorbed, axis=-1)


def relay_pairs(step, energies, count):
    pairs = []
    for energy in range(energies):
        turn = step - energy % 2
        if turn < 0:
            pairs += [(energy * count + i, energy * count + i - 1) for i in range(1, count)]
            continue
        if turn <= count - 2:
            ends = (turn, turn + 1)
        elif count - 1 <= turn <= 2 * count - 3:
            ends = (2 * count - 2 - turn, 2 * count - 3 - turn)
        else:
            continue
        pairs.append(tuple(energy * count + end for end in ends))
    return pairs


def shards(energies, count, free_green, self_energy, coupling, pattern, offsets, emission, absorption):
    size, blocks = free_green.shape[-1], pattern.shape[-1]
    args = (free_green[0], self_energy[0], coupling, pattern)
    row = shape(size, 2 * size)
    factor = shape(size, size, HALF, 2, 3)
    row_v = pltpu.VMEM(row.shape, F32)
    product = 24 * size**3
    loading = load_scratch(size, blocks) + matrices(3, size)

    def relay(step, value):
        return lax.ppermute(value, ("energy", "slab"), relay_pairs(step, energies, count))

    begun = call(
        source_kernel,
        [row],
        loading,
        args,
        [HBM] * 4,
        flops=6 * product,
        name="source",
        limit=58,
    )
    arrived, outs, ends = [relay(0, begun[0])], [], []
    whole, source, coupler, opening, left_lead, left_tail, forward, backward = call(
        map_kernel,
        [row] * 4 + [factor, factor, row, row],
        loading,
        args,
        [HBM] * 4,
        flops=12 * product,
        name="left_maps",
        limit=42,
    )
    left_map = [left_lead, left_tail, whole]
    right_map = following = None
    for step in range(2 * count - 2):
        lefts, rights = step <= count - 1, step >= count - 1
        closing = lefts and step >= count - 2
        args = [arrived[step]]
        if lefts:
            args += left_map
        if rights:
            args += right_map[:3]
        if closing:
            args += [forward, backward, source, coupler]
        made = call(
            functools.partial(relay_kernel, step, count, lefts, rights),
            [row] * (2 if closing else 1),
            matrices(4 if closing else 1, size),
            args,
            flops=2 * product,
            name="relay",
        )
        outs.append(made[0])
        ends += made[1:]
        arrived.append(relay(step + 1, made[0]))
        if step == 0:
            down = [
                (energy * count + i, energy * count + i - 1)
                for energy in range(0, energies, 2)
                for i in range(1, count)
            ]
            following = lax.ppermute(opening, ("energy", "slab"), down)
        if step == count - 2:
            args = arrived[: count - 1] + outs[: count - 1]
            args += [whole, source, forward, backward, coupler, following, arrived[0]]
            right_map = call(
                functools.partial(prepare_kernel, count),
                [factor, factor, row, factor, factor],
                [row_v] * 2 + matrices(4, size),
                args,
                flops=10 * product,
                name="right_maps",
            )
    chips = energies // 2
    parcel = shape(size // chips, 2 * size)
    blocks, parcels = [None, None], [None, None]
    args = arrived[count - 1 :] + ends + right_map[3:] + [whole] + outs[: count - 1]
    blocks[1], *parcels[1] = call(
        functools.partial(last_kernel, count),
        [row] + [parcel] * chips,
        matrices(1, size),
        args,
        flops=2 * product,
        name="second_slab",
    )
    args = arrived[-1:] + outs[count - 2 :] + right_map[:3] + blocks[1:]
    blocks[0], *parcels[0] = call(
        functools.partial(first_kernel, count),
        [row] + [parcel] * chips,
        matrices(1, size),
        args,
        flops=2 * product,
        name="first_slab",
    )
    (retarded,) = call(
        unpack_kernel, [shape(size, size, F32, 2, 2)], [], blocks, name="retarded"
    )

    def exchange(values):
        return values[:1] + [
            lax.ppermute(value, "energy", [(i, i ^ (2 * mask)) for i in range(energies)])
            for mask, value in enumerate(values)
            if mask
        ]

    everyone = jnp.arange(energies, dtype=jnp.int32)
    weights = mode_weights(everyone, everyone, offsets, emission, absorption)
    partial = shape(size // chips, 2 * size, F32, chips)
    sums = [None, None]
    for slab in (1, 0):
        mine, other = call(
            functools.partial(mix_kernel, chips),
            [partial] * 2,
            [],
            [weights] + exchange(parcels[slab]),
            [SMEM] + [VMEM] * chips,
            flops=product // 8,
            name="mix",
        )
        other = lax.ppermute(other, "energy", [(i, i ^ 1) for i in range(energies)])
        sums[slab] = call(
            functools.partial(sum_kernel, chips), [parcel] * chips, [], [mine, other], name="sum"
        )
    returned = [exchange(sums[slab]) for slab in (1, 0)][::-1]
    (scattering,) = call(
        functools.partial(place_kernel, chips),
        [shape(size, size, F32, 2, 2)],
        [],
        returned[0] + returned[1],
        name="scattering",
    )
    return (retarded[None], scattering[None])


def solution(mesh):
    blocks = P("energy", "slab", None, None, None)
    in_specs = (blocks, blocks, P("slab", None, None, None), P("slab", None, None), P(), P(), P())
    body = functools.partial(shards, mesh.shape["energy"], mesh.shape["slab"])
    return jax.shard_map(
        body, mesh=mesh, in_specs=in_specs, out_specs=(blocks, blocks), check_vma=False
    )
```

```python
import functools

import jax
import jax.numpy as jnp
from jax import lax
from jax.experimental import pallas as pl
from jax.experimental.pallas import tpu as pltpu
from jax.sharding import PartitionSpec as P

F32 = jnp.float32
HALF = jnp.bfloat16
HBM = pl.BlockSpec(memory_space=pltpu.HBM)
VMEM = pl.BlockSpec(memory_space=pltpu.VMEM)
SMEM = pl.BlockSpec(memory_space=pltpu.SMEM)
LEADING = 0


def split(value):
    high = value.astype(HALF)
    return high, (value - high.astype(F32)).astype(HALF)


def dot(left, right, transposed):
    dims = (((1,), (1 if transposed else 0,)), ((), ()))
    return lax.dot_general(left, right, dims, preferred_element_type=F32)


def parts_of(block, adjoint=False):
    size = block.shape[0]
    real, imag = block[:, :size], block[:, size:]
    return real, imag, (real - imag if adjoint else real + imag)


def put(matrix, block, adjoint=False):
    for index, part in enumerate(parts_of(block, adjoint)):
        matrix[0, index], matrix[1, index] = split(part)


def times_split(left, matrix, transposed=False):
    products = []
    for index, (high, low) in enumerate(left):
        size = high.shape[0]
        both = dot(jnp.concatenate([high, low], axis=0), matrix[0, index], transposed)
        products.append(both[:size] + both[size:] + dot(high, matrix[1, index], transposed))
    first, second, third = products
    if transposed:
        return jnp.concatenate([first + second, third - first + second], axis=1)
    return jnp.concatenate([first - second, third - first - second], axis=1)


def times(block, matrix, transposed=False):
    return times_split([split(part) for part in parts_of(block)], matrix, transposed)


def row_form(pair):
    return jnp.concatenate([pair[0], pair[1]], axis=1)


def adjoint_row(pair):
    return jnp.concatenate([jnp.transpose(pair[0]), -jnp.transpose(pair[1])], axis=1)


def expand(pattern, size):
    blocks = pattern.shape[0]
    tile = size // blocks
    rows = lax.broadcasted_iota(jnp.int32, (size, blocks), 0)
    first = lax.broadcasted_iota(jnp.int32, (size, blocks), 1) * tile
    member = jnp.where((rows >= first) & (rows < first + tile), 1.0, 0.0).astype(HALF)
    tall = dot(member, pattern.astype(F32).astype(HALF), False)
    return dot(tall.astype(HALF), member, True)


def couple(coupling, pattern):
    mask = expand(pattern[...], coupling.shape[-1])
    return jnp.concatenate([coupling[0] * mask, coupling[1] * mask], axis=1)


def trailing():
    return lax.rem(lax.axis_index("energy") + LEADING, 2)


def shape(rows, columns, dtype=F32, *lead):
    return jax.ShapeDtypeStruct(lead + (rows, columns), dtype)


def matrices(number, size):
    return [pltpu.VMEM((2, 3, size, size), HALF)] * number


def call(kernel, outs, scratch, args, specs=None, flops=0, name=None, limit=40):
    made = pl.pallas_call(
        kernel,
        out_shape=outs,
        in_specs=specs or [VMEM] * len(args),
        out_specs=[VMEM] * len(outs),
        scratch_shapes=scratch,
        compiler_params=pltpu.CompilerParams(vmem_limit_bytes=limit * 2**20),
        cost_estimate=pl.CostEstimate(flops=flops, bytes_accessed=2**20, transcendentals=0),
        name=name,
    )(*args)
    return list(made)


class Loads:
    def __init__(self, args, targets, sems, couplers=(0, 1), blocks=True):
        order = [(0, 0), (1, 0), (3, 1), (2, 1), (1, 1), (0, 1), (3, 0), (2, 0)]
        self.copies = {
            (which, slab): pltpu.make_async_copy(
                args[which].at[slab], targets[which].at[slab], sems.at[index]
            )
            for index, (which, slab) in enumerate(order)
            if (blocks if which < 2 else slab in couplers)
        }
        self.targets = targets
        for copy in self.copies.values():
            copy.start()

    def get(self, which, slab):
        self.copies[which, slab].wait()
        return self.targets[which].at[slab]

    def green(self, slab):
        return row_form(self.get(0, slab))

    def sigma(self, slab):
        return row_form(self.get(1, slab))

    def coupler(self, slab):
        tiles = self.get(3, slab)
        return couple(self.get(2, slab), tiles)


def load_scratch(size, blocks):
    return [
        pltpu.VMEM((2, 2, size, size), F32),
        pltpu.VMEM((2, 2, size, size), F32),
        pltpu.VMEM((2, 2, size, size), F32),
        pltpu.VMEM((2, blocks, blocks), jnp.int32),
        pltpu.SemaphoreType.DMA((8,)),
    ]


def left_sources(loads, whole, source, coupler_out, m_a, m_b, m_c):
    first = loads.green(0)
    put(m_b, first)
    put(m_a, loads.sigma(0))
    made = first + times(times(first, m_a), m_b)
    if source is not None:
        source[...] = made
    put(m_a, made)
    coupler = loads.coupler(1)
    if coupler_out is not None:
        coupler_out[...] = coupler
    put(m_c, coupler, True)
    inner = loads.sigma(1) + times(times(coupler, m_a), m_c, True)
    put(m_a, inner)
    second = loads.green(1)
    put(m_b, second)
    whole[...] = second + times(times(second, m_a), m_b)
    return first, second


def source_kernel(green, sigma, coupling, pattern, whole, gate, *scratch):
    @pl.when(lax.axis_index("slab") == 0)
    def _():
        loads = Loads((green, sigma, coupling, pattern), scratch[:4], scratch[4], (1,))
        left_sources(loads, whole, None, None, *scratch[5:])

    @pl.when((lax.axis_index("slab") > 0) & (trailing() == 1))
    def _():
        loads = Loads((green, sigma, coupling, pattern), scratch[:4], scratch[4], (0,), False)
        gate[...] = loads.coupler(0)[: gate.shape[0]]


def map_kernel(
    green, sigma, coupling, pattern,
    whole, source, coupler, upper, lower, lead, tail, forward, backward, *scratch,
):
    m_a, m_b, m_c = scratch[5:]
    loads = Loads((green, sigma, coupling, pattern), scratch[:4], scratch[4])
    first, second = left_sources(loads, whole, source, coupler, m_a, m_b, m_c)
    before = loads.coupler(0)

    @pl.when(lax.axis_index("slab") > 0)
    def _():
        upper[...] = before[: upper.shape[0]]
        lower[...] = before[upper.shape[0] :]
        put(m_a, first)
        size = before.shape[0]
        behind = times(adjoint_row((before[:, :size], before[:, size:])), m_a)
        backward[...] = behind
        put(tail, times(times(behind, m_c, True), m_b))
        put(m_a, before)
        ahead = times(first, m_a)
        forward[...] = ahead
        put(m_a, ahead)
        put(m_c, coupler[...])
        put(lead, times(times(second, m_c), m_a))


def right_terms(first, last, coupler, m_coupler, m_first, m_last, m_upper):
    put(m_coupler, coupler, True)
    put(m_last, last)
    through = times(times(first, m_coupler, True), m_last)
    put(m_first, first)
    put(m_upper, times(coupler, m_first))
    return through, first + times(through, m_upper)


def prepare_kernel(count, *refs):
    arrived, wholes = refs[: count - 1], refs[count - 1 : 2 * count - 2]
    refs = refs[2 * count - 2 :]
    start_whole, source, forward, backward, coupler = refs[:5]
    gate, upper, lower = refs[5:8]
    lead, tail, constant, last_lead, last_tail = refs[8:13]
    first_v, last_v, m_a, m_b, m_c, m_d = refs[13:]
    place = lax.axis_index("slab")

    @pl.when(place == 0)
    def _():
        first_v[...] = source[...]
        last_v[...] = start_whole[...]

    for turn in range(count - 1):
        @pl.when((place > 0) & (place == turn + 1 - trailing()))
        def _(turn=turn):
            last_v[...] = wholes[turn][...]
            put(m_a, arrived[turn][...])

    @pl.when((place > 0) & (place < count - 1))
    def _():
        put(m_b, backward[...])
        first_v[...] = source[...] + times(times(forward[...], m_a), m_b)

    @pl.when(place < count - 1)
    def _():
        first, last = first_v[...], last_v[...]
        through, joined = right_terms(first, last, coupler[...], m_a, m_b, m_c, m_d)
        constant[...] = joined
        above = jnp.where(trailing() == 0, upper[...], gate[...])
        next_coupler = jnp.concatenate([above, lower[...]], axis=0)
        put(m_a, next_coupler, True)
        put(lead, times(through, m_a, True))
        put(last_lead, times(last, m_a, True))
        behind = times(next_coupler, m_c)
        put(last_tail, behind)
        put(tail, times(behind, m_d))


def apply_map(mapping, m_x):
    lead, tail, constant = mapping
    ahead = [(lead[0, index], lead[1, index]) for index in range(3)]
    return constant[...] + times(times_split(ahead, m_x), tail)


def relay_kernel(step, count, lefts, rights, *refs):
    refs = list(refs)
    place = lax.axis_index("slab")
    turn = step - trailing()
    is_left = (turn >= 0) & (turn <= count - 2) & (place == turn + 1)
    is_right = (turn >= count - 1) & (place == 2 * count - 3 - turn)
    closing = lefts and step >= count - 2
    arrived = refs.pop(0)
    left_map = [refs.pop(0) for _ in range(3)] if lefts else None
    right_map = [refs.pop(0) for _ in range(3)] if rights else None
    if closing:
        forward, backward, source, coupler = [refs.pop(0) for _ in range(4)]
    if step == 0:
        refs.pop(0)
    out = refs.pop(0)
    if closing:
        end, m_x, m_a, m_b, m_c = refs
    else:
        (m_x,) = refs

    if step == 0:
        @pl.when(place == 0)
        def _():
            out[...] = left_map[2][...]

    if lefts:
        @pl.when(is_left)
        def _():
            put(m_x, arrived[...])
            out[...] = apply_map(left_map, m_x)

    if closing:
        @pl.when(is_left & (place == count - 1))
        def _():
            last = out[...]
            end[...] = last
            put(m_a, backward[...])
            first = source[...] + times(times(forward[...], m_x), m_a)
            _, joined = right_terms(first, last, coupler[...], m_a, m_b, m_c, m_x)
            out[...] = joined

    if rights:
        @pl.when(is_right)
        def _():
            put(m_x, arrived[...])
            out[...] = apply_map(right_map, m_x)


def last_kernel(count, *refs):
    refs = list(refs)
    arrived = [refs.pop(0) for _ in range(count)]
    ends = [refs.pop(0) for _ in range(2)]
    last_lead, last_tail, whole_start = [refs.pop(0) for _ in range(3)]
    wholes = [refs.pop(0) for _ in range(count - 1)]
    block, *parcels, m_x = refs
    place = lax.axis_index("slab")
    core = trailing()
    is_last = place == count - 1

    for index in range(count):
        @pl.when(jnp.logical_not(is_last) & (2 * count - 3 - place + core == count - 1 + index))
        def _(index=index):
            put(m_x, arrived[index][...])

    for index in range(2):
        @pl.when(is_last & (core == index))
        def _(index=index):
            block[...] = ends[index][...]

    @pl.when(place == 0)
    def _():
        block[...] = apply_map((last_lead, last_tail, whole_start), m_x)

    for index in range(count - 1):
        @pl.when((place > 0) & jnp.logical_not(is_last) & (place - 1 + core == index))
        def _(index=index):
            block[...] = apply_map((last_lead, last_tail, wholes[index]), m_x)

    pack(block, parcels)


def first_kernel(count, *refs):
    refs = list(refs)
    arrived = refs.pop(0)
    outs = [refs.pop(0) for _ in range(count)]
    right_map = [refs.pop(0) for _ in range(3)]
    refs.pop(0)
    block, *parcels, m_x = refs
    place = lax.axis_index("slab")
    core = trailing()
    at = jnp.where(place == count - 1, count - 2 + core, 2 * count - 3 - place + core)

    for index in range(count):
        @pl.when(at == count - 2 + index)
        def _(index=index):
            block[...] = outs[index][...]

    @pl.when((place == 0) & (core == 1))
    def _():
        put(m_x, arrived[...])
        block[...] = apply_map(right_map, m_x)

    pack(block, parcels)


def pack(block, parcels):
    for mask, parcel in enumerate(parcels):
        parcel[...] = block[share(mask, parcel.shape[0]), :]


def unpack_kernel(*refs):
    blocks, out = refs[:2], refs[2]
    size = out.shape[-1]
    for slab, block in enumerate(blocks):
        for part in range(2):
            out[slab, part] = block[:, part * size : (part + 1) * size]


def share(mask, rows):
    chip = lax.shift_right_logical(lax.axis_index("energy"), 1)
    return pl.ds(pl.multiple_of(lax.bitwise_xor(chip, mask) * rows, rows), rows)


def mix_kernel(chips, weights, *refs):
    parcels, (mine, other) = refs[:chips], refs[chips:]
    energy = lax.axis_index("energy")
    core = lax.rem(energy, 2)
    sources = [lax.bitwise_xor(energy, 2 * mask) for mask in range(chips)]
    for mask in range(chips):
        for target, out in ((sources[mask], mine), (sources[mask] + 1 - 2 * core, other)):
            total = weights[target, sources[0]] * parcels[0][...]
            for index in range(1, chips):
                total += weights[target, sources[index]] * parcels[index][...]
            out[mask] = total


def sum_kernel(chips, mine, other, *outs):
    for mask in range(chips):
        outs[mask][...] = mine[mask] + other[mask]


def place_kernel(chips, *refs):
    scattering = refs[2 * chips]
    size = scattering.shape[-1]
    for slab in range(2):
        for mask, parcel in enumerate(refs[slab * chips : (slab + 1) * chips]):
            where = share(mask, parcel.shape[0])
            for part in range(2):
                scattering[slab, part, where, :] = parcel[:, part * size : (part + 1) * size]


def mode_weights(targets, sources, offsets, emission, absorption):
    spacing = sources[None, :, None] - targets[:, None, None]
    emitted = jnp.where(
        spacing == -offsets[None, None, :],
        emission[None, None, :],
        jnp.zeros_like(emission)[None, None, :],
    )
    absorbed = jnp.where(
        spacing == offsets[None, None, :],
        absorption[None, None, :],
        jnp.zeros_like(absorption)[None, None, :],
    )
    return jnp.sum(emitted + absorbed, axis=-1)


def relay_pairs(step, energies, count):
    pairs = []
    for energy in range(energies):
        turn = step - (energy + LEADING) % 2
        if 0 <= turn <= count - 2:
            ends = (turn, turn + 1)
        elif count - 1 <= turn <= 2 * count - 3:
            ends = (2 * count - 2 - turn, 2 * count - 3 - turn)
        else:
            continue
        pairs.append(tuple(energy * count + end for end in ends))
    return pairs


def shards(energies, count, free_green, self_energy, coupling, pattern, offsets, emission, absorption):
    size, blocks = free_green.shape[-1], pattern.shape[-1]
    args = (free_green[0], self_energy[0], coupling, pattern)
    row = shape(size, 2 * size)
    half = shape(size // 2, 2 * size)
    factor = shape(size, size, HALF, 2, 3)
    row_v = pltpu.VMEM(row.shape, F32)
    product = 24 * size**3
    loading = load_scratch(size, blocks) + matrices(3, size)

    def relay(step, value):
        return lax.ppermute(value, ("energy", "slab"), relay_pairs(step, energies, count))

    def lower_place(value, cores):
        pairs = [
            (energy * count + i, energy * count + i - 1)
            for energy in range(energies)
            for i in range(1, count)
            if (energy + LEADING) % 2 in cores
        ]
        return lax.ppermute(value, ("energy", "slab"), pairs)

    begun = call(
        source_kernel,
        [row, half],
        loading,
        args,
        [HBM] * 4,
        flops=6 * product,
        name="source",
        limit=61,
    )
    arrived, outs, ends = [relay(0, begun[0])], [], []
    gate = lower_place(begun[1], [1])
    whole, source, coupler, upper, lower, left_lead, left_tail, forward, backward = call(
        map_kernel,
        [row] * 3 + [half] * 2 + [factor, factor, row, row],
        loading,
        args,
        [HBM] * 4,
        flops=12 * product,
        name="left_maps",
        limit=49,
    )
    left_map = [left_lead, left_tail, whole]
    right_map = None
    for step in range(2 * count - 2):
        lefts, rights = step <= count - 1, step >= count - 1
        closing = lefts and step >= count - 2
        args = [arrived[step]]
        if lefts:
            args += left_map
        if rights:
            args += right_map[:3]
        if closing:
            args += [forward, backward, source, coupler]
        if step == 0:
            args.append(gate)
        made = call(
            functools.partial(relay_kernel, step, count, lefts, rights),
            [row] * (2 if closing else 1),
            matrices(4 if closing else 1, size),
            args,
            flops=2 * product,
            name="relay",
        )
        outs.append(made[0])
        ends += made[1:]
        arrived.append(relay(step + 1, made[0]))
        if step == 0:
            lower = lower_place(lower, [0, 1])
            upper = lower_place(upper, [0])
        if step == count - 2:
            args = arrived[: count - 1] + outs[: count - 1]
            args += [whole, source, forward, backward, coupler, gate, upper, lower]
            right_map = call(
                functools.partial(prepare_kernel, count),
                [factor, factor, row, factor, factor],
                [row_v] * 2 + matrices(4, size),
                args,
                flops=10 * product,
                name="right_maps",
            )
    chips = energies // 2
    parcel = shape(size // chips, 2 * size)
    blocks, parcels = [None, None], [None, None]
    args = arrived[count - 1 :] + ends + right_map[3:] + [whole] + outs[: count - 1]
    blocks[1], *parcels[1] = call(
        functools.partial(last_kernel, count),
        [row] + [parcel] * chips,
        matrices(1, size),
        args,
        flops=2 * product,
        name="second_slab",
    )
    args = arrived[-1:] + outs[count - 2 :] + right_map[:3] + blocks[1:]
    blocks[0], *parcels[0] = call(
        functools.partial(first_kernel, count),
        [row] + [parcel] * chips,
        matrices(1, size),
        args,
        flops=2 * product,
        name="first_slab",
    )
    (retarded,) = call(
        unpack_kernel, [shape(size, size, F32, 2, 2)], [], blocks, name="retarded"
    )

    def exchange(values):
        return values[:1] + [
            lax.ppermute(value, "energy", [(i, i ^ (2 * mask)) for i in range(energies)])
            for mask, value in enumerate(values)
            if mask
        ]

    everyone = jnp.arange(energies, dtype=jnp.int32)
    weights = mode_weights(everyone, everyone, offsets, emission, absorption)
    partial = shape(size // chips, 2 * size, F32, chips)
    sums = [None, None]
    for slab in (1, 0):
        mine, other = call(
            functools.partial(mix_kernel, chips),
            [partial] * 2,
            [],
            [weights] + exchange(parcels[slab]),
            [SMEM] + [VMEM] * chips,
            flops=product // 8,
            name="mix",
        )
        other = lax.ppermute(other, "energy", [(i, i ^ 1) for i in range(energies)])
        sums[slab] = call(
            functools.partial(sum_kernel, chips), [parcel] * chips, [], [mine, other], name="sum"
        )
    returned = [exchange(sums[slab]) for slab in (1, 0)][::-1]
    (scattering,) = call(
        functools.partial(place_kernel, chips),
        [shape(size, size, F32, 2, 2)],
        [],
        returned[0] + returned[1],
        name="scattering",
    )
    return (retarded[None], scattering[None])


def solution(mesh):
    blocks = P("energy", "slab", None, None, None)
    in_specs = (blocks, blocks, P("slab", None, None, None), P("slab", None, None), P(), P(), P())
    body = functools.partial(shards, mesh.shape["energy"], mesh.shape["slab"])
    return jax.shard_map(
        body, mesh=mesh, in_specs=in_specs, out_specs=(blocks, blocks), check_vma=False
    )
```

```python
import functools

import jax
import jax.numpy as jnp
from jax import lax
from jax.experimental import pallas as pl
from jax.experimental.pallas import tpu as pltpu
from jax.sharding import PartitionSpec as P

F32 = jnp.float32
HALF = jnp.bfloat16
HBM = pl.BlockSpec(memory_space=pltpu.HBM)
VMEM = pl.BlockSpec(memory_space=pltpu.VMEM)
SMEM = pl.BlockSpec(memory_space=pltpu.SMEM)
LEADING = 1


def split(value):
    high = value.astype(HALF)
    return high, (value - high.astype(F32)).astype(HALF)


def dot(left, right, transposed):
    dims = (((1,), (1 if transposed else 0,)), ((), ()))
    return lax.dot_general(left, right, dims, preferred_element_type=F32)


def parts_of(block, adjoint=False):
    size = block.shape[1] // 2
    real, imag = block[:, :size], block[:, size:]
    return real, imag, (real - imag if adjoint else real + imag)


def put(matrix, block, adjoint=False):
    for index, part in enumerate(parts_of(block, adjoint)):
        matrix[0, index], matrix[1, index] = split(part)


def times_split(left, matrix, transposed=False):
    products = []
    for index, (high, low) in enumerate(left):
        size = high.shape[0]
        both = dot(jnp.concatenate([high, low], axis=0), matrix[0, index], transposed)
        products.append(both[:size] + both[size:] + dot(high, matrix[1, index], transposed))
    first, second, third = products
    if transposed:
        return jnp.concatenate([first + second, third - first + second], axis=1)
    return jnp.concatenate([first - second, third - first - second], axis=1)


def times(block, matrix, transposed=False):
    return times_split([split(part) for part in parts_of(block)], matrix, transposed)


def row_form(pair):
    return jnp.concatenate([pair[0], pair[1]], axis=1)


def adjoint_row(pair):
    return jnp.concatenate([jnp.transpose(pair[0]), -jnp.transpose(pair[1])], axis=1)


def expand(pattern, size):
    blocks = pattern.shape[0]
    tile = size // blocks
    rows = lax.broadcasted_iota(jnp.int32, (size, blocks), 0)
    first = lax.broadcasted_iota(jnp.int32, (size, blocks), 1) * tile
    member = jnp.where((rows >= first) & (rows < first + tile), 1.0, 0.0).astype(HALF)
    tall = dot(member, pattern.astype(F32).astype(HALF), False)
    return dot(tall.astype(HALF), member, True)


def couple(coupling, pattern):
    mask = expand(pattern[...], coupling.shape[-1])
    return jnp.concatenate([coupling[0] * mask, coupling[1] * mask], axis=1)


def trailing():
    return lax.rem(lax.axis_index("energy") + LEADING, 2)


def shape(rows, columns, dtype=F32, *lead):
    return jax.ShapeDtypeStruct(lead + (rows, columns), dtype)


def matrices(number, size):
    return [pltpu.VMEM((2, 3, size, size), HALF)] * number


def call(kernel, outs, scratch, args, specs=None, out_specs=None, flops=0, name=None, limit=40):
    made = pl.pallas_call(
        kernel,
        out_shape=outs,
        in_specs=specs or [VMEM] * len(args),
        out_specs=out_specs or [VMEM] * len(outs),
        scratch_shapes=scratch,
        compiler_params=pltpu.CompilerParams(vmem_limit_bytes=limit * 2**20),
        cost_estimate=pl.CostEstimate(flops=flops, bytes_accessed=2**20, transcendentals=0),
        name=name,
    )(*args)
    return list(made)


class Loads:
    def __init__(self, args, targets, sems, couplers=(0, 1), blocks=True):
        order = [(0, 0), (1, 0), (3, 1), (2, 1), (1, 1), (0, 1), (3, 0), (2, 0)]
        self.copies = {
            (which, slab): pltpu.make_async_copy(
                args[which].at[slab], targets[which].at[slab], sems.at[index]
            )
            for index, (which, slab) in enumerate(order)
            if (blocks if which < 2 else slab in couplers)
        }
        self.targets = targets
        for copy in self.copies.values():
            copy.start()

    def get(self, which, slab):
        self.copies[which, slab].wait()
        return self.targets[which].at[slab]

    def green(self, slab):
        return row_form(self.get(0, slab))

    def sigma(self, slab):
        return row_form(self.get(1, slab))

    def coupler(self, slab):
        tiles = self.get(3, slab)
        return couple(self.get(2, slab), tiles)


def load_scratch(size, blocks):
    return [
        pltpu.VMEM((2, 2, size, size), F32),
        pltpu.VMEM((2, 2, size, size), F32),
        pltpu.VMEM((2, 2, size, size), F32),
        pltpu.VMEM((2, blocks, blocks), jnp.int32),
        pltpu.SemaphoreType.DMA((8,)),
    ]


def left_sources(loads, source, coupler_out, m_a, m_b, m_c):
    first = loads.green(0)
    put(m_b, first)
    put(m_a, loads.sigma(0))
    made = first + times(times(first, m_a), m_b)
    if source is not None:
        source[...] = made
    put(m_a, made)
    coupler = loads.coupler(1)
    if coupler_out is not None:
        coupler_out[...] = coupler
    put(m_c, coupler, True)
    inner = loads.sigma(1) + times(times(coupler, m_a), m_c, True)
    put(m_a, inner)
    second = loads.green(1)
    put(m_b, second)
    return first, second, times(second, m_a)


def source_kernel(green, sigma, coupling, pattern, whole, gate, *scratch):
    *scratch, out_v, out_sems = scratch
    place, behind = lax.axis_index("slab"), trailing()

    @pl.when((place == 0) & (behind == 0))
    def _():
        loads = Loads((green, sigma, coupling, pattern), scratch[:4], scratch[4], (1,))
        _, second, through = left_sources(loads, None, None, *scratch[5:])
        rows = second.shape[0] // 2
        copies = []
        for index in range(2):
            where = slice(index * rows, (index + 1) * rows)
            out_v[where] = second[where] + times(through[where], scratch[6])
            copies.append(
                pltpu.make_async_copy(out_v.at[where], whole.at[where], out_sems.at[index])
            )
            copies[-1].start()
        for copy in copies:
            copy.wait()

    @pl.when((place > 0) & (behind == 1))
    def _():
        loads = Loads((green, sigma, coupling, pattern), scratch[:4], scratch[4], (0,), False)
        out_v[...] = loads.coupler(0)
        copy = pltpu.make_async_copy(out_v.at[: gate.shape[0]], gate, out_sems.at[0])
        copy.start()
        copy.wait()


def map_kernel(
    green, sigma, coupling, pattern,
    whole, source, coupler, upper, lower, lead, tail, forward, backward, *scratch,
):
    m_a, m_b, m_c = scratch[5:]
    loads = Loads((green, sigma, coupling, pattern), scratch[:4], scratch[4])
    first, second, through = left_sources(loads, source, coupler, m_a, m_b, m_c)
    whole[...] = second + times(through, m_b)
    before = loads.coupler(0)

    @pl.when(lax.axis_index("slab") > 0)
    def _():
        upper[...] = before[: upper.shape[0]]
        lower[...] = before[upper.shape[0] :]
        put(m_a, first)
        size = before.shape[0]
        behind = times(adjoint_row((before[:, :size], before[:, size:])), m_a)
        backward[...] = behind
        put(tail, times(times(behind, m_c, True), m_b))
        put(m_a, before)
        ahead = times(first, m_a)
        forward[...] = ahead
        put(m_a, ahead)
        put(m_c, coupler[...])
        put(lead, times(times(second, m_c), m_a))


def right_terms(first, last, coupler, m_coupler, m_first, m_last, m_upper):
    put(m_coupler, coupler, True)
    put(m_last, last)
    through = times(times(first, m_coupler, True), m_last)
    put(m_first, first)
    put(m_upper, times(coupler, m_first))
    return through, first + times(through, m_upper)


def prepare_kernel(count, *refs):
    arrived, wholes = refs[: count - 1], refs[count - 1 : 2 * count - 2]
    refs = refs[2 * count - 2 :]
    start_whole, source, forward, backward, coupler = refs[:5]
    gate, upper, lower = refs[5:8]
    lead, tail, constant, last_lead, last_tail = refs[8:13]
    first_v, last_v, m_a, m_b, m_c, m_d = refs[13:]
    place = lax.axis_index("slab")

    @pl.when(place == 0)
    def _():
        first_v[...] = source[...]
        last_v[...] = start_whole[...]

    for turn in range(count - 1):
        @pl.when((place > 0) & (place == turn + 1 - trailing()))
        def _(turn=turn):
            last_v[...] = wholes[turn][...]
            put(m_a, arrived[turn][...])

    @pl.when((place > 0) & (place < count - 1))
    def _():
        put(m_b, backward[...])
        first_v[...] = source[...] + times(times(forward[...], m_a), m_b)

    @pl.when(place < count - 1)
    def _():
        first, last = first_v[...], last_v[...]
        through, joined = right_terms(first, last, coupler[...], m_a, m_b, m_c, m_d)
        constant[...] = joined
        above = jnp.where(trailing() == 0, upper[...], gate[...])
        next_coupler = jnp.concatenate([above, lower[...]], axis=0)
        put(m_a, next_coupler, True)
        put(lead, times(through, m_a, True))
        put(last_lead, times(last, m_a, True))
        behind = times(next_coupler, m_c)
        put(last_tail, behind)
        put(tail, times(behind, m_d))


def apply_map(mapping, m_x):
    lead, tail, constant = mapping
    ahead = [(lead[0, index], lead[1, index]) for index in range(3)]
    return constant[...] + times(times_split(ahead, m_x), tail)


def relay_kernel(step, count, lefts, rights, *refs):
    refs = list(refs)
    place = lax.axis_index("slab")
    turn = step - trailing()
    is_left = (turn >= 0) & (turn <= count - 2) & (place == turn + 1)
    is_right = (turn >= count - 1) & (place == 2 * count - 3 - turn)
    closing = lefts and step >= count - 2
    arrived = refs.pop(0)
    left_map = [refs.pop(0) for _ in range(3)] if lefts else None
    right_map = [refs.pop(0) for _ in range(3)] if rights else None
    if closing:
        forward, backward, source, coupler = [refs.pop(0) for _ in range(4)]
    if step == 0:
        refs.pop(0)
    out = refs.pop(0)
    if closing:
        end, m_x, m_a, m_b, m_c = refs
    else:
        (m_x,) = refs

    if step == 0:
        @pl.when(place == 0)
        def _():
            out[...] = left_map[2][...]

    if lefts:
        @pl.when(is_left)
        def _():
            put(m_x, arrived[...])
            out[...] = apply_map(left_map, m_x)

    if closing:
        @pl.when(is_left & (place == count - 1))
        def _():
            last = out[...]
            end[...] = last
            put(m_a, backward[...])
            first = source[...] + times(times(forward[...], m_x), m_a)
            _, joined = right_terms(first, last, coupler[...], m_a, m_b, m_c, m_x)
            out[...] = joined

    if rights:
        @pl.when(is_right)
        def _():
            put(m_x, arrived[...])
            out[...] = apply_map(right_map, m_x)


def last_kernel(count, *refs):
    refs = list(refs)
    arrived = [refs.pop(0) for _ in range(count)]
    ends = [refs.pop(0) for _ in range(2)]
    last_lead, last_tail, whole_start = [refs.pop(0) for _ in range(3)]
    wholes = [refs.pop(0) for _ in range(count - 1)]
    block, *parcels, m_x = refs
    place = lax.axis_index("slab")
    core = trailing()
    is_last = place == count - 1

    for index in range(count):
        @pl.when(jnp.logical_not(is_last) & (2 * count - 3 - place + core == count - 1 + index))
        def _(index=index):
            put(m_x, arrived[index][...])

    for index in range(2):
        @pl.when(is_last & (core == index))
        def _(index=index):
            block[...] = ends[index][...]

    @pl.when(place == 0)
    def _():
        block[...] = apply_map((last_lead, last_tail, whole_start), m_x)

    for index in range(count - 1):
        @pl.when((place > 0) & jnp.logical_not(is_last) & (place - 1 + core == index))
        def _(index=index):
            block[...] = apply_map((last_lead, last_tail, wholes[index]), m_x)

    pack(block, parcels)


def first_kernel(count, *refs):
    refs = list(refs)
    arrived = refs.pop(0)
    outs = [refs.pop(0) for _ in range(count)]
    right_map = [refs.pop(0) for _ in range(3)]
    refs.pop(0)
    block, *parcels, m_x = refs
    place = lax.axis_index("slab")
    core = trailing()
    at = jnp.where(place == count - 1, count - 2 + core, 2 * count - 3 - place + core)

    for index in range(count):
        @pl.when(at == count - 2 + index)
        def _(index=index):
            block[...] = outs[index][...]

    @pl.when((place == 0) & (core == 1))
    def _():
        put(m_x, arrived[...])
        block[...] = apply_map(right_map, m_x)

    pack(block, parcels)


def pack(block, parcels):
    for mask, parcel in enumerate(parcels):
        parcel[...] = block[share(mask, parcel.shape[0]), :]


def unpack_kernel(*refs):
    blocks, out = refs[:2], refs[2]
    size = out.shape[-1]
    for slab, block in enumerate(blocks):
        for part in range(2):
            out[slab, part] = block[:, part * size : (part + 1) * size]


def share(mask, rows):
    chip = lax.shift_right_logical(lax.axis_index("energy"), 1)
    return pl.ds(pl.multiple_of(lax.bitwise_xor(chip, mask) * rows, rows), rows)


def mix_kernel(chips, weights, *refs):
    parcels, (mine, other) = refs[:chips], refs[chips:]
    energy = lax.axis_index("energy")
    core = lax.rem(energy, 2)
    sources = [lax.bitwise_xor(energy, 2 * mask) for mask in range(chips)]
    for mask in range(chips):
        for target, out in ((sources[mask], mine), (sources[mask] + 1 - 2 * core, other)):
            total = weights[target, sources[0]] * parcels[0][...]
            for index in range(1, chips):
                total += weights[target, sources[index]] * parcels[index][...]
            out[mask] = total


def sum_kernel(chips, mine, other, *outs):
    for mask in range(chips):
        outs[mask][...] = mine[mask] + other[mask]


def place_kernel(chips, *refs):
    scattering = refs[2 * chips]
    size = scattering.shape[-1]
    for slab in range(2):
        for mask, parcel in enumerate(refs[slab * chips : (slab + 1) * chips]):
            where = share(mask, parcel.shape[0])
            for part in range(2):
                scattering[slab, part, where, :] = parcel[:, part * size : (part + 1) * size]


def mode_weights(targets, sources, offsets, emission, absorption):
    spacing = sources[None, :, None] - targets[:, None, None]
    emitted = jnp.where(
        spacing == -offsets[None, None, :],
        emission[None, None, :],
        jnp.zeros_like(emission)[None, None, :],
    )
    absorbed = jnp.where(
        spacing == offsets[None, None, :],
        absorption[None, None, :],
        jnp.zeros_like(absorption)[None, None, :],
    )
    return jnp.sum(emitted + absorbed, axis=-1)


def relay_pairs(step, energies, count):
    pairs = []
    for energy in range(energies):
        turn = step - (energy + LEADING) % 2
        if 0 <= turn <= count - 2:
            ends = (turn, turn + 1)
        elif count - 1 <= turn <= 2 * count - 3:
            ends = (2 * count - 2 - turn, 2 * count - 3 - turn)
        else:
            continue
        pairs.append(tuple(energy * count + end for end in ends))
    return pairs


def shards(energies, count, free_green, self_energy, coupling, pattern, offsets, emission, absorption):
    size, blocks = free_green.shape[-1], pattern.shape[-1]
    args = (free_green[0], self_energy[0], coupling, pattern)
    row = shape(size, 2 * size)
    half = shape(size // 2, 2 * size)
    factor = shape(size, size, HALF, 2, 3)
    row_v = pltpu.VMEM(row.shape, F32)
    product = 24 * size**3
    loading = load_scratch(size, blocks) + matrices(3, size)

    def relay(step, value):
        return lax.ppermute(value, ("energy", "slab"), relay_pairs(step, energies, count))

    def lower_place(value, cores):
        pairs = [
            (energy * count + i, energy * count + i - 1)
            for energy in range(energies)
            for i in range(1, count)
            if (energy + LEADING) % 2 in cores
        ]
        return lax.ppermute(value, ("energy", "slab"), pairs)

    begun = call(
        source_kernel,
        [row, half],
        loading + [row_v, pltpu.SemaphoreType.DMA((2,))],
        args,
        [HBM] * 4,
        [HBM] * 2,
        flops=6 * product,
        name="source",
        limit=61,
    )
    arrived, outs, ends = [relay(0, begun[0])], [], []
    gate = lower_place(begun[1], [1])
    whole, source, coupler, upper, lower, left_lead, left_tail, forward, backward = call(
        map_kernel,
        [row] * 3 + [half] * 2 + [factor, factor, row, row],
        loading,
        args,
        [HBM] * 4,
        flops=12 * product,
        name="left_maps",
        limit=49,
    )
    left_map = [left_lead, left_tail, whole]
    right_map = None
    for step in range(2 * count - 2):
        lefts, rights = step <= count - 1, step >= count - 1
        closing = lefts and step >= count - 2
        args = [arrived[step]]
        if lefts:
            args += left_map
        if rights:
            args += right_map[:3]
        if closing:
            args += [forward, backward, source, coupler]
        if step == 0:
            args.append(gate)
        made = call(
            functools.partial(relay_kernel, step, count, lefts, rights),
            [row] * (2 if closing else 1),
            matrices(4 if closing else 1, size),
            args,
            flops=2 * product,
            name="relay",
        )
        outs.append(made[0])
        ends += made[1:]
        arrived.append(relay(step + 1, made[0]))
        if step == 0:
            lower = lower_place(lower, [0, 1])
            upper = lower_place(upper, [0])
        if step == count - 2:
            args = arrived[: count - 1] + outs[: count - 1]
            args += [whole, source, forward, backward, coupler, gate, upper, lower]
            right_map = call(
                functools.partial(prepare_kernel, count),
                [factor, factor, row, factor, factor],
                [row_v] * 2 + matrices(4, size),
                args,
                flops=10 * product,
                name="right_maps",
            )
    chips = energies // 2
    parcel = shape(size // chips, 2 * size)
    blocks, parcels = [None, None], [None, None]
    args = arrived[count - 1 :] + ends + right_map[3:] + [whole] + outs[: count - 1]
    blocks[1], *parcels[1] = call(
        functools.partial(last_kernel, count),
        [row] + [parcel] * chips,
        matrices(1, size),
        args,
        flops=2 * product,
        name="second_slab",
    )
    args = arrived[-1:] + outs[count - 2 :] + right_map[:3] + blocks[1:]
    blocks[0], *parcels[0] = call(
        functools.partial(first_kernel, count),
        [row] + [parcel] * chips,
        matrices(1, size),
        args,
        flops=2 * product,
        name="first_slab",
    )
    (retarded,) = call(
        unpack_kernel, [shape(size, size, F32, 2, 2)], [], blocks, name="retarded"
    )

    def exchange(values):
        return values[:1] + [
            lax.ppermute(value, "energy", [(i, i ^ (2 * mask)) for i in range(energies)])
            for mask, value in enumerate(values)
            if mask
        ]

    everyone = jnp.arange(energies, dtype=jnp.int32)
    weights = mode_weights(everyone, everyone, offsets, emission, absorption)
    partial = shape(size // chips, 2 * size, F32, chips)
    sums = [None, None]
    for slab in (1, 0):
        mine, other = call(
            functools.partial(mix_kernel, chips),
            [partial] * 2,
            [],
            [weights] + exchange(parcels[slab]),
            [SMEM] + [VMEM] * chips,
            flops=product // 8,
            name="mix",
        )
        other = lax.ppermute(other, "energy", [(i, i ^ 1) for i in range(energies)])
        sums[slab] = call(
            functools.partial(sum_kernel, chips), [parcel] * chips, [], [mine, other], name="sum"
        )
    returned = [exchange(sums[slab]) for slab in (1, 0)][::-1]
    (scattering,) = call(
        functools.partial(place_kernel, chips),
        [shape(size, size, F32, 2, 2)],
        [],
        returned[0] + returned[1],
        name="scattering",
    )
    return (retarded[None], scattering[None])


def solution(mesh):
    blocks = P("energy", "slab", None, None, None)
    in_specs = (blocks, blocks, P("slab", None, None, None), P("slab", None, None), P(), P(), P())
    body = functools.partial(shards, mesh.shape["energy"], mesh.shape["slab"])
    return jax.shard_map(
        body, mesh=mesh, in_specs=in_specs, out_specs=(blocks, blocks), check_vma=False
    )
```

```python
import functools

import jax
import jax.numpy as jnp
from jax import lax
from jax.experimental import pallas as pl
from jax.experimental.pallas import tpu as pltpu
from jax.sharding import PartitionSpec as P

F32 = jnp.float32
HALF = jnp.bfloat16
HBM = pl.BlockSpec(memory_space=pltpu.HBM)
VMEM = pl.BlockSpec(memory_space=pltpu.VMEM)
SMEM = pl.BlockSpec(memory_space=pltpu.SMEM)
LEADING = 0


def split(value):
    high = value.astype(HALF)
    return high, (value - high.astype(F32)).astype(HALF)


def dot(left, right, transposed):
    dims = (((1,), (1 if transposed else 0,)), ((), ()))
    return lax.dot_general(left, right, dims, preferred_element_type=F32)


def parts_of(block, adjoint=False):
    size = block.shape[1] // 2
    real, imag = block[:, :size], block[:, size:]
    return real, imag, (real - imag if adjoint else real + imag)


def put(matrix, block, adjoint=False):
    for index, part in enumerate(parts_of(block, adjoint)):
        matrix[0, index], matrix[1, index] = split(part)


def times_split(left, matrix, transposed=False):
    products = []
    for index, (high, low) in enumerate(left):
        size = high.shape[0]
        both = dot(jnp.concatenate([high, low], axis=0), matrix[0, index], transposed)
        products.append(both[:size] + both[size:] + dot(high, matrix[1, index], transposed))
    first, second, third = products
    if transposed:
        return jnp.concatenate([first + second, third - first + second], axis=1)
    return jnp.concatenate([first - second, third - first - second], axis=1)


def times(block, matrix, transposed=False):
    return times_split([split(part) for part in parts_of(block)], matrix, transposed)


def row_form(pair):
    return jnp.concatenate([pair[0], pair[1]], axis=1)


def adjoint_row(pair):
    return jnp.concatenate([jnp.transpose(pair[0]), -jnp.transpose(pair[1])], axis=1)


def expand(pattern, size):
    blocks = pattern.shape[0]
    tile = size // blocks
    rows = lax.broadcasted_iota(jnp.int32, (size, blocks), 0)
    first = lax.broadcasted_iota(jnp.int32, (size, blocks), 1) * tile
    member = jnp.where((rows >= first) & (rows < first + tile), 1.0, 0.0).astype(HALF)
    tall = dot(member, pattern.astype(F32).astype(HALF), False)
    return dot(tall.astype(HALF), member, True)


def couple(coupling, pattern):
    mask = expand(pattern[...], coupling.shape[-1])
    return jnp.concatenate([coupling[0] * mask, coupling[1] * mask], axis=1)


def trailing():
    return lax.rem(lax.axis_index("energy") + LEADING, 2)


def shape(rows, columns, dtype=F32, *lead):
    return jax.ShapeDtypeStruct(lead + (rows, columns), dtype)


def matrices(number, size):
    return [pltpu.VMEM((2, 3, size, size), HALF)] * number


def call(kernel, outs, scratch, args, specs=None, out_specs=None, flops=0, name=None, limit=40):
    made = pl.pallas_call(
        kernel,
        out_shape=outs,
        in_specs=specs or [VMEM] * len(args),
        out_specs=out_specs or [VMEM] * len(outs),
        scratch_shapes=scratch,
        compiler_params=pltpu.CompilerParams(vmem_limit_bytes=limit * 2**20),
        cost_estimate=pl.CostEstimate(flops=flops, bytes_accessed=2**20, transcendentals=0),
        name=name,
    )(*args)
    return list(made)


class Loads:
    def __init__(self, args, targets, sems, couplers=(0, 1), blocks=True):
        order = [(0, 0), (1, 0), (3, 1), (2, 1), (1, 1), (0, 1), (3, 0), (2, 0)]
        self.copies = {
            (which, slab): pltpu.make_async_copy(
                args[which].at[slab], targets[which].at[slab], sems.at[index]
            )
            for index, (which, slab) in enumerate(order)
            if (blocks if which < 2 else slab in couplers)
        }
        self.targets = targets
        for copy in self.copies.values():
            copy.start()

    def get(self, which, slab):
        self.copies[which, slab].wait()
        return self.targets[which].at[slab]

    def green(self, slab):
        return row_form(self.get(0, slab))

    def sigma(self, slab):
        return row_form(self.get(1, slab))

    def coupler(self, slab):
        tiles = self.get(3, slab)
        return couple(self.get(2, slab), tiles)


def load_scratch(size, blocks):
    return [
        pltpu.VMEM((2, 2, size, size), F32),
        pltpu.VMEM((2, 2, size, size), F32),
        pltpu.VMEM((2, 2, size, size), F32),
        pltpu.VMEM((2, blocks, blocks), jnp.int32),
        pltpu.SemaphoreType.DMA((8,)),
    ]


def left_sources(loads, source, coupler_out, m_a, m_b, m_c):
    first = loads.green(0)
    put(m_b, first)
    put(m_a, loads.sigma(0))
    made = first + times(times(first, m_a), m_b)
    if source is not None:
        source[...] = made
    put(m_a, made)
    coupler = loads.coupler(1)
    if coupler_out is not None:
        coupler_out[...] = coupler
    put(m_c, coupler, True)
    inner = loads.sigma(1) + times(times(coupler, m_a), m_c, True)
    put(m_a, inner)
    second = loads.green(1)
    put(m_b, second)
    return first, second, times(second, m_a)


def source_kernel(green, sigma, coupling, pattern, whole, gate, *scratch):
    *scratch, out_v, out_sems = scratch
    place, behind = lax.axis_index("slab"), trailing()

    @pl.when((place == 0) & (behind == 0))
    def _():
        loads = Loads((green, sigma, coupling, pattern), scratch[:4], scratch[4], (1,))
        _, second, through = left_sources(loads, None, None, *scratch[5:])
        rows = second.shape[0] // 2
        copies = []
        for index in range(2):
            where = slice(index * rows, (index + 1) * rows)
            out_v[where] = second[where] + times(through[where], scratch[6])
            copies.append(
                pltpu.make_async_copy(out_v.at[where], whole.at[where], out_sems.at[index])
            )
            copies[-1].start()
        for copy in copies:
            copy.wait()

    @pl.when((place > 0) & (behind == 1))
    def _():
        loads = Loads((green, sigma, coupling, pattern), scratch[:4], scratch[4], (0,), False)
        out_v[...] = loads.coupler(0)
        copy = pltpu.make_async_copy(out_v.at[: gate.shape[0]], gate, out_sems.at[0])
        copy.start()
        copy.wait()


def map_kernel(
    green, sigma, coupling, pattern,
    whole, source, coupler, upper, lower, lead, tail, forward, backward, *scratch,
):
    m_a, m_b, m_c = scratch[5:]
    loads = Loads((green, sigma, coupling, pattern), scratch[:4], scratch[4])
    first, second, through = left_sources(loads, source, coupler, m_a, m_b, m_c)
    whole[...] = second + times(through, m_b)
    before = loads.coupler(0)

    @pl.when(lax.axis_index("slab") > 0)
    def _():
        upper[...] = before[: upper.shape[0]]
        lower[...] = before[upper.shape[0] :]
        put(m_a, first)
        size = before.shape[0]
        behind = times(adjoint_row((before[:, :size], before[:, size:])), m_a)
        backward[...] = behind
        put(tail, times(times(behind, m_c, True), m_b))
        put(m_a, before)
        ahead = times(first, m_a)
        forward[...] = ahead
        put(m_a, ahead)
        put(m_c, coupler[...])
        put(lead, times(times(second, m_c), m_a))


def right_terms(first, last, coupler, m_coupler, m_first, m_last, m_upper):
    put(m_coupler, coupler, True)
    put(m_last, last)
    through = times(times(first, m_coupler, True), m_last)
    put(m_first, first)
    put(m_upper, times(coupler, m_first))
    return through, first + times(through, m_upper)


def prepare_kernel(count, *refs):
    arrived, wholes = refs[: count - 1], refs[count - 1 : 2 * count - 2]
    refs = refs[2 * count - 2 :]
    start_whole, source, forward, backward, coupler = refs[:5]
    gate, upper, lower = refs[5:8]
    lead, tail, constant, last_lead, last_tail = refs[8:13]
    first_v, last_v, m_a, m_b, m_c, m_d = refs[13:]
    place = lax.axis_index("slab")

    @pl.when(place == 0)
    def _():
        first_v[...] = source[...]
        last_v[...] = start_whole[...]

    for turn in range(count - 1):
        @pl.when((place > 0) & (place == turn + 1 - trailing()))
        def _(turn=turn):
            last_v[...] = wholes[turn][...]
            put(m_a, arrived[turn][...])

    @pl.when((place > 0) & (place < count - 1))
    def _():
        put(m_b, backward[...])
        first_v[...] = source[...] + times(times(forward[...], m_a), m_b)

    @pl.when(place < count - 1)
    def _():
        first, last = first_v[...], last_v[...]
        through, joined = right_terms(first, last, coupler[...], m_a, m_b, m_c, m_d)
        constant[...] = joined
        above = jnp.where(trailing() == 0, upper[...], gate[...])
        next_coupler = jnp.concatenate([above, lower[...]], axis=0)
        put(m_a, next_coupler, True)
        put(lead, times(through, m_a, True))
        put(last_lead, times(last, m_a, True))
        behind = times(next_coupler, m_c)
        put(last_tail, behind)
        put(tail, times(behind, m_d))


def apply_map(mapping, m_x):
    lead, tail, constant = mapping
    ahead = [(lead[0, index], lead[1, index]) for index in range(3)]
    return constant[...] + times(times_split(ahead, m_x), tail)


def relay_kernel(step, count, lefts, rights, *refs):
    refs = list(refs)
    place = lax.axis_index("slab")
    turn = step - trailing()
    is_left = (turn >= 0) & (turn <= count - 2) & (place == turn + 1)
    is_right = (turn >= count - 1) & (place == 2 * count - 3 - turn)
    closing = lefts and step >= count - 2
    arrived = refs.pop(0)
    left_map = [refs.pop(0) for _ in range(3)] if lefts else None
    right_map = [refs.pop(0) for _ in range(3)] if rights else None
    if closing:
        forward, backward, source, coupler = [refs.pop(0) for _ in range(4)]
    if step == 0:
        refs.pop(0)
    out = refs.pop(0)
    if closing:
        end, m_x, m_a, m_b, m_c = refs
    else:
        (m_x,) = refs

    if step == 0:
        @pl.when(place == 0)
        def _():
            out[...] = left_map[2][...]

    if lefts:
        @pl.when(is_left)
        def _():
            put(m_x, arrived[...])
            out[...] = apply_map(left_map, m_x)

    if closing:
        @pl.when(is_left & (place == count - 1))
        def _():
            last = out[...]
            end[...] = last
            put(m_a, backward[...])
            first = source[...] + times(times(forward[...], m_x), m_a)
            _, joined = right_terms(first, last, coupler[...], m_a, m_b, m_c, m_x)
            out[...] = joined

    if rights:
        @pl.when(is_right)
        def _():
            put(m_x, arrived[...])
            out[...] = apply_map(right_map, m_x)


def last_kernel(count, *refs):
    refs = list(refs)
    arrived = [refs.pop(0) for _ in range(count)]
    ends = [refs.pop(0) for _ in range(2)]
    last_lead, last_tail, whole_start = [refs.pop(0) for _ in range(3)]
    wholes = [refs.pop(0) for _ in range(count - 1)]
    block, *parcels, m_x = refs
    place = lax.axis_index("slab")
    core = trailing()
    is_last = place == count - 1

    for index in range(count):
        @pl.when(jnp.logical_not(is_last) & (2 * count - 3 - place + core == count - 1 + index))
        def _(index=index):
            put(m_x, arrived[index][...])

    for index in range(2):
        @pl.when(is_last & (core == index))
        def _(index=index):
            block[...] = ends[index][...]

    @pl.when(place == 0)
    def _():
        block[...] = apply_map((last_lead, last_tail, whole_start), m_x)

    for index in range(count - 1):
        @pl.when((place > 0) & jnp.logical_not(is_last) & (place - 1 + core == index))
        def _(index=index):
            block[...] = apply_map((last_lead, last_tail, wholes[index]), m_x)

    pack(block, parcels)


def first_kernel(count, *refs):
    refs = list(refs)
    arrived = refs.pop(0)
    outs = [refs.pop(0) for _ in range(count)]
    right_map = [refs.pop(0) for _ in range(3)]
    refs.pop(0)
    block, *parcels, m_x = refs
    place = lax.axis_index("slab")
    core = trailing()
    at = jnp.where(place == count - 1, count - 2 + core, 2 * count - 3 - place + core)

    for index in range(count):
        @pl.when(at == count - 2 + index)
        def _(index=index):
            block[...] = outs[index][...]

    @pl.when((place == 0) & (core == 1))
    def _():
        put(m_x, arrived[...])
        block[...] = apply_map(right_map, m_x)

    pack(block, parcels)


def pack(block, parcels):
    for mask, parcel in enumerate(parcels):
        parcel[...] = block[share(mask, parcel.shape[0]), :]


def unpack_kernel(*refs):
    blocks, out = refs[:2], refs[2]
    size = out.shape[-1]
    for slab, block in enumerate(blocks):
        for part in range(2):
            out[slab, part] = block[:, part * size : (part + 1) * size]


def share(mask, rows):
    chip = lax.shift_right_logical(lax.axis_index("energy"), 1)
    return pl.ds(pl.multiple_of(lax.bitwise_xor(chip, mask) * rows, rows), rows)


def mix_kernel(chips, weights, *refs):
    parcels, (mine, other) = refs[:chips], refs[chips:]
    energy = lax.axis_index("energy")
    core = lax.rem(energy, 2)
    sources = [lax.bitwise_xor(energy, 2 * mask) for mask in range(chips)]
    for mask in range(chips):
        for target, out in ((sources[mask], mine), (sources[mask] + 1 - 2 * core, other)):
            total = weights[target, sources[0]] * parcels[0][...]
            for index in range(1, chips):
                total += weights[target, sources[index]] * parcels[index][...]
            out[mask] = total


def sum_kernel(chips, mine, other, *outs):
    for mask in range(chips):
        outs[mask][...] = mine[mask] + other[mask]


def place_kernel(chips, *refs):
    scattering = refs[2 * chips]
    size = scattering.shape[-1]
    for slab in range(2):
        for mask, parcel in enumerate(refs[slab * chips : (slab + 1) * chips]):
            where = share(mask, parcel.shape[0])
            for part in range(2):
                scattering[slab, part, where, :] = parcel[:, part * size : (part + 1) * size]


def mode_weights(targets, sources, offsets, emission, absorption):
    spacing = sources[None, :, None] - targets[:, None, None]
    emitted = jnp.where(
        spacing == -offsets[None, None, :],
        emission[None, None, :],
        jnp.zeros_like(emission)[None, None, :],
    )
    absorbed = jnp.where(
        spacing == offsets[None, None, :],
        absorption[None, None, :],
        jnp.zeros_like(absorption)[None, None, :],
    )
    return jnp.sum(emitted + absorbed, axis=-1)


def relay_pairs(step, energies, count):
    pairs = []
    for energy in range(energies):
        turn = step - (energy + LEADING) % 2
        if 0 <= turn <= count - 2:
            ends = (turn, turn + 1)
        elif count - 1 <= turn <= 2 * count - 3:
            ends = (2 * count - 2 - turn, 2 * count - 3 - turn)
        else:
            continue
        pairs.append(tuple(energy * count + end for end in ends))
    return pairs


def shards(energies, count, free_green, self_energy, coupling, pattern, offsets, emission, absorption):
    size, blocks = free_green.shape[-1], pattern.shape[-1]
    args = (free_green[0], self_energy[0], coupling, pattern)
    row = shape(size, 2 * size)
    half = shape(size // 2, 2 * size)
    factor = shape(size, size, HALF, 2, 3)
    row_v = pltpu.VMEM(row.shape, F32)
    product = 24 * size**3
    loading = load_scratch(size, blocks) + matrices(3, size)

    def relay(step, value):
        return lax.ppermute(value, ("energy", "slab"), relay_pairs(step, energies, count))

    def lower_place(value, cores):
        pairs = [
            (energy * count + i, energy * count + i - 1)
            for energy in range(energies)
            for i in range(1, count)
            if (energy + LEADING) % 2 in cores
        ]
        return lax.ppermute(value, ("energy", "slab"), pairs)

    begun = call(
        source_kernel,
        [row, half],
        loading + [row_v, pltpu.SemaphoreType.DMA((2,))],
        args,
        [HBM] * 4,
        [HBM] * 2,
        flops=6 * product,
        name="source",
        limit=61,
    )
    arrived, outs, ends = [relay(0, begun[0])], [], []
    gate = lower_place(begun[1], [1])
    whole, source, coupler, upper, lower, left_lead, left_tail, forward, backward = call(
        map_kernel,
        [row] * 3 + [half] * 2 + [factor, factor, row, row],
        loading,
        args,
        [HBM] * 4,
        flops=12 * product,
        name="left_maps",
        limit=49,
    )
    left_map = [left_lead, left_tail, whole]
    right_map = None
    for step in range(2 * count - 2):
        lefts, rights = step <= count - 1, step >= count - 1
        closing = lefts and step >= count - 2
        args = [arrived[step]]
        if lefts:
            args += left_map
        if rights:
            args += right_map[:3]
        if closing:
            args += [forward, backward, source, coupler]
        if step == 0:
            args.append(gate)
        made = call(
            functools.partial(relay_kernel, step, count, lefts, rights),
            [row] * (2 if closing else 1),
            matrices(4 if closing else 1, size),
            args,
            flops=2 * product,
            name="relay",
        )
        outs.append(made[0])
        ends += made[1:]
        arrived.append(relay(step + 1, made[0]))
        if step == 0:
            lower = lower_place(lower, [0, 1])
            upper = lower_place(upper, [0])
        if step == count - 2:
            args = arrived[: count - 1] + outs[: count - 1]
            args += [whole, source, forward, backward, coupler, gate, upper, lower]
            right_map = call(
                functools.partial(prepare_kernel, count),
                [factor, factor, row, factor, factor],
                [row_v] * 2 + matrices(4, size),
                args,
                flops=10 * product,
                name="right_maps",
            )
    chips = energies // 2
    parcel = shape(size // chips, 2 * size)
    blocks, parcels = [None, None], [None, None]
    args = arrived[count - 1 :] + ends + right_map[3:] + [whole] + outs[: count - 1]
    blocks[1], *parcels[1] = call(
        functools.partial(last_kernel, count),
        [row] + [parcel] * chips,
        matrices(1, size),
        args,
        flops=2 * product,
        name="second_slab",
    )
    args = arrived[-1:] + outs[count - 2 :] + right_map[:3] + blocks[1:]
    blocks[0], *parcels[0] = call(
        functools.partial(first_kernel, count),
        [row] + [parcel] * chips,
        matrices(1, size),
        args,
        flops=2 * product,
        name="first_slab",
    )
    (retarded,) = call(
        unpack_kernel, [shape(size, size, F32, 2, 2)], [], blocks, name="retarded"
    )

    def exchange(values):
        return values[:1] + [
            lax.ppermute(value, "energy", [(i, i ^ (2 * mask)) for i in range(energies)])
            for mask, value in enumerate(values)
            if mask
        ]

    everyone = jnp.arange(energies, dtype=jnp.int32)
    weights = mode_weights(everyone, everyone, offsets, emission, absorption)
    partial = shape(size // chips, 2 * size, F32, chips)
    sums = [None, None]
    for slab in (1, 0):
        mine, other = call(
            functools.partial(mix_kernel, chips),
            [partial] * 2,
            [],
            [weights] + exchange(parcels[slab]),
            [SMEM] + [VMEM] * chips,
            flops=product // 8,
            name="mix",
        )
        other = lax.ppermute(other, "energy", [(i, i ^ 1) for i in range(energies)])
        sums[slab] = call(
            functools.partial(sum_kernel, chips), [parcel] * chips, [], [mine, other], name="sum"
        )
    returned = [exchange(sums[slab]) for slab in (1, 0)][::-1]
    (scattering,) = call(
        functools.partial(place_kernel, chips),
        [shape(size, size, F32, 2, 2)],
        [],
        returned[0] + returned[1],
        name="scattering",
    )
    return (retarded[None], scattering[None])


def solution(mesh):
    blocks = P("energy", "slab", None, None, None)
    in_specs = (blocks, blocks, P("slab", None, None, None), P("slab", None, None), P(), P(), P())
    body = functools.partial(shards, mesh.shape["energy"], mesh.shape["slab"])
    return jax.shard_map(
        body, mesh=mesh, in_specs=in_specs, out_specs=(blocks, blocks), check_vma=False
    )
```

```python
import functools

import jax
import jax.numpy as jnp
from jax import lax
from jax.experimental import pallas as pl
from jax.experimental.pallas import tpu as pltpu
from jax.sharding import PartitionSpec as P

F32 = jnp.float32
HALF = jnp.bfloat16
HBM = pl.BlockSpec(memory_space=pltpu.HBM)
VMEM = pl.BlockSpec(memory_space=pltpu.VMEM)
SMEM = pl.BlockSpec(memory_space=pltpu.SMEM)
LEADING = 0


def split(value):
    high = value.astype(HALF)
    return high, (value - high.astype(F32)).astype(HALF)


def dot(left, right, transposed):
    dims = (((1,), (1 if transposed else 0,)), ((), ()))
    return lax.dot_general(left, right, dims, preferred_element_type=F32)


def parts_of(block, adjoint=False):
    size = block.shape[1] // 2
    real, imag = block[:, :size], block[:, size:]
    return real, imag, (real - imag if adjoint else real + imag)


def put(matrix, block, adjoint=False):
    for index, part in enumerate(parts_of(block, adjoint)):
        matrix[0, index], matrix[1, index] = split(part)


def times_split(left, matrix, transposed=False):
    products = []
    for index, (high, low) in enumerate(left):
        size = high.shape[0]
        both = dot(jnp.concatenate([high, low], axis=0), matrix[0, index], transposed)
        products.append(both[:size] + both[size:] + dot(high, matrix[1, index], transposed))
    first, second, third = products
    if transposed:
        return jnp.concatenate([first + second, third - first + second], axis=1)
    return jnp.concatenate([first - second, third - first - second], axis=1)


def times(block, matrix, transposed=False):
    return times_split([split(part) for part in parts_of(block)], matrix, transposed)


def row_form(pair):
    return jnp.concatenate([pair[0], pair[1]], axis=1)


def adjoint_row(pair):
    return jnp.concatenate([jnp.transpose(pair[0]), -jnp.transpose(pair[1])], axis=1)


def expand(pattern, size):
    blocks = pattern.shape[0]
    tile = size // blocks
    rows = lax.broadcasted_iota(jnp.int32, (size, blocks), 0)
    first = lax.broadcasted_iota(jnp.int32, (size, blocks), 1) * tile
    member = jnp.where((rows >= first) & (rows < first + tile), 1.0, 0.0).astype(HALF)
    tall = dot(member, pattern.astype(F32).astype(HALF), False)
    return dot(tall.astype(HALF), member, True)


def couple(coupling, pattern):
    mask = expand(pattern[...], coupling.shape[-1])
    return jnp.concatenate([coupling[0] * mask, coupling[1] * mask], axis=1)


def trailing():
    return lax.rem(lax.axis_index("energy") + LEADING, 2)


def shape(rows, columns, dtype=F32, *lead):
    return jax.ShapeDtypeStruct(lead + (rows, columns), dtype)


def matrices(number, size):
    return [pltpu.VMEM((2, 3, size, size), HALF)] * number


def call(kernel, outs, scratch, args, specs=None, out_specs=None, flops=0, name=None, limit=40):
    made = pl.pallas_call(
        kernel,
        out_shape=outs,
        in_specs=specs or [VMEM] * len(args),
        out_specs=out_specs or [VMEM] * len(outs),
        scratch_shapes=scratch,
        compiler_params=pltpu.CompilerParams(vmem_limit_bytes=limit * 2**20),
        cost_estimate=pl.CostEstimate(flops=flops, bytes_accessed=2**20, transcendentals=0),
        name=name,
    )(*args)
    return list(made)


class Loads:
    def __init__(self, args, targets, sems):
        order = [(0, 0), (1, 0), (3, 1), (2, 1), (1, 1), (0, 1), (3, 0), (2, 0)]
        self.copies = {}
        for index, (which, slab) in enumerate(order):
            if which == 3:
                pieces = [(args[which].at[slab], targets[which].at[slab])]
            else:
                pieces = [
                    (args[which].at[slab, part], targets[which].at[slab, part]) for part in range(2)
                ]
            self.copies[which, slab] = [
                pltpu.make_async_copy(*piece, sems.at[2 * index + part])
                for part, piece in enumerate(pieces)
            ]
        self.targets = targets
        for copies in self.copies.values():
            for copy in copies:
                copy.start()

    def get(self, which, slab):
        for copy in self.copies[which, slab]:
            copy.wait()
        return self.targets[which].at[slab]

    def green(self, slab):
        return row_form(self.get(0, slab))

    def sigma(self, slab):
        return row_form(self.get(1, slab))

    def coupler(self, slab):
        tiles = self.get(3, slab)
        return couple(self.get(2, slab), tiles)


def load_scratch(size, blocks):
    return [
        pltpu.VMEM((2, 2, size, size), F32),
        pltpu.VMEM((2, 2, size, size), F32),
        pltpu.VMEM((2, 2, size, size), F32),
        pltpu.VMEM((2, blocks, blocks), jnp.int32),
        pltpu.SemaphoreType.DMA((16,)),
    ]


def left_sources(loads, source, coupler_out, m_a, m_b, m_c):
    first = loads.green(0)
    put(m_b, first)
    put(m_a, loads.sigma(0))
    made = first + times(times(first, m_a), m_b)
    if source is not None:
        source[...] = made
    put(m_a, made)
    coupler = loads.coupler(1)
    if coupler_out is not None:
        coupler_out[...] = coupler
    put(m_c, coupler, True)
    inner = loads.sigma(1) + times(times(coupler, m_a), m_c, True)
    put(m_a, inner)
    second = loads.green(1)
    put(m_b, second)
    return first, second, times(second, m_a)


def source_kernel(green, sigma, coupling, pattern, whole, *scratch):
    *scratch, out_v, out_sems = scratch

    @pl.when((lax.axis_index("slab") == 0) & (trailing() == 0))
    def _():
        loads = Loads((green, sigma, coupling, pattern), scratch[:4], scratch[4])
        _, second, through = left_sources(loads, None, None, *scratch[5:])
        rows = second.shape[0] // 2
        copies = []
        for index in range(2):
            where = slice(index * rows, (index + 1) * rows)
            out_v[where] = second[where] + times(through[where], scratch[6])
            copies.append(
                pltpu.make_async_copy(out_v.at[where], whole.at[where], out_sems.at[index])
            )
            copies[-1].start()
        for which in (2, 3):
            loads.get(which, 0)
        for copy in copies:
            copy.wait()


def map_kernel(
    green, sigma, coupling, pattern,
    whole, source, coupler, opening, lead, tail, forward, backward, *scratch,
):
    m_a, m_b, m_c = scratch[5:]
    loads = Loads((green, sigma, coupling, pattern), scratch[:4], scratch[4])
    first, second, through = left_sources(loads, source, coupler, m_a, m_b, m_c)
    whole[...] = second + times(through, m_b)
    before = loads.coupler(0)

    @pl.when(lax.axis_index("slab") > 0)
    def _():
        opening[...] = before
        put(m_a, first)
        size = before.shape[0]
        behind = times(adjoint_row((before[:, :size], before[:, size:])), m_a)
        backward[...] = behind
        put(tail, times(times(behind, m_c, True), m_b))
        put(m_a, before)
        ahead = times(first, m_a)
        forward[...] = ahead
        put(m_a, ahead)
        put(m_c, coupler[...])
        put(lead, times(times(second, m_c), m_a))


def prepare_kernel(count, *refs):
    arrived = refs[: count - 1]
    source, forward, backward, coupler, opening = refs[count - 1 : count + 4]
    lead, tail, constant, first_lead, first_tail, first_constant = refs[count + 4 : count + 10]
    x_v, m_a, m_b, m_c, m_d = refs[count + 10 :]
    place = lax.axis_index("slab")
    inner = (place > 0) & (place < count - 1)

    for turn in range(count - 1):
        @pl.when(inner & (place == turn + 1 - trailing()))
        def _(turn=turn):
            x_v[...] = arrived[turn][...]

    @pl.when(place == 0)
    def _():
        first_constant[...] = source[...]

    @pl.when(inner)
    def _():
        put(m_a, x_v[...])
        put(m_b, backward[...])
        first_constant[...] = source[...] + times(times(forward[...], m_a), m_b)

    @pl.when(place < count - 1)
    def _():
        first = first_constant[...]
        put(m_c, coupler[...], True)
        put(first_lead, times(first, m_c, True))
        put(m_d, first)
        put(first_tail, times(coupler[...], m_d))

    @pl.when(inner)
    def _():
        x, before = x_v[...], opening[...]
        put(m_b, before, True)
        through = times(times(x, m_b, True), m_d)
        put(lead, times(through, m_c, True))
        put(m_b, times(before, m_a))
        constant[...] = x + times(through, m_b)
        behind = times(first_constant[...], m_b)
        put(m_b, behind)
        put(tail, times(coupler[...], m_b))


def apply_map(mapping, m_x):
    lead, tail, constant = mapping
    ahead = [(lead[0, index], lead[1, index]) for index in range(3)]
    return constant[...] + times(times_split(ahead, m_x), tail)


def relay_kernel(step, count, lefts, rights, *refs):
    refs = list(refs)
    place = lax.axis_index("slab")
    turn = step - trailing()
    is_left = (turn >= 0) & (turn <= count - 2) & (place == turn + 1)
    is_right = (turn >= count - 1) & (place == 2 * count - 3 - turn)
    closing = lefts and step >= count - 2
    arrived = refs.pop(0)
    left_map = [refs.pop(0) for _ in range(3)] if lefts else None
    right_map = [refs.pop(0) for _ in range(3)] if rights else None
    if closing:
        forward, backward, source, coupler, opening = [refs.pop(0) for _ in range(5)]
    if step == 0:
        refs.pop(0)
    out = refs.pop(0)
    if closing:
        first_end, last_end, m_x, m_a, m_b = refs
    else:
        (m_x,) = refs

    if step == 0:
        @pl.when(place == 0)
        def _():
            out[...] = left_map[2][...]

    if lefts:
        @pl.when(is_left)
        def _():
            put(m_x, arrived[...])
            out[...] = apply_map(left_map, m_x)

    if closing:
        @pl.when(is_left & (place == count - 1))
        def _():
            last = out[...]
            last_end[...] = last
            put(m_a, backward[...])
            first = source[...] + times(times(forward[...], m_x), m_a)
            put(m_a, coupler[...], True)
            put(m_b, last)
            through = times(times(first, m_a, True), m_b)
            put(m_a, first)
            put(m_b, times(coupler[...], m_a))
            first = first + times(through, m_b)
            first_end[...] = first
            x, before = arrived[...], opening[...]
            put(m_a, before, True)
            put(m_b, first)
            through = times(times(x, m_a, True), m_b)
            put(m_a, times(before, m_x))
            out[...] = x + times(through, m_a)

    if rights:
        @pl.when(is_right & (place > 0))
        def _():
            put(m_x, arrived[...])
            out[...] = apply_map(right_map, m_x)


def pack_kernel(count, chips, *refs):
    outs, ends = refs[:count], refs[count : count + 2]
    parcels, last_parcels = refs[count + 2 : count + 2 + chips], refs[count + 2 + chips :]
    place, core = lax.axis_index("slab"), trailing()
    at = jnp.where(place == count - 1, count - 2 + core, 2 * count - 3 - place + core)

    for index in range(count):
        @pl.when((place > 0) & (at == count - 2 + index))
        def _(index=index):
            pack(outs[index], parcels)

    for index in range(2):
        @pl.when((place == count - 1) & (core == index))
        def _(index=index):
            pack(ends[index], last_parcels)


def first_kernel(count, *refs):
    arrived, ends = refs[:count], refs[count : count + 2]
    mapping = refs[count + 2 : count + 5]
    block, *parcels, m_x = refs[count + 5 :]
    place, core = lax.axis_index("slab"), trailing()

    for index in range(count):
        @pl.when((place < count - 1) & (count - 2 - place + core == index))
        def _(index=index):
            put(m_x, arrived[index][...])

    @pl.when(place < count - 1)
    def _():
        block[...] = apply_map(mapping, m_x)

    for index in range(2):
        @pl.when((place == count - 1) & (core == index))
        def _(index=index):
            block[...] = ends[index][...]

    pack(block, parcels)


def pack(block, parcels):
    for mask, parcel in enumerate(parcels):
        parcel[...] = block[share(mask, parcel.shape[0]), :]


def retarded_kernel(count, *refs):
    block, arrived, ends, out = refs[0], refs[1 : count + 1], refs[count + 1 : count + 3], refs[-1]
    place, core = lax.axis_index("slab"), trailing()
    size = out.shape[-1]

    def write(slab, block):
        for part in range(2):
            out[slab, part] = block[:, part * size : (part + 1) * size]

    write(0, block)
    for index in range(count):
        @pl.when((place < count - 1) & (count - 2 - place + core == index))
        def _(index=index):
            write(1, arrived[index])

    for index in range(2):
        @pl.when((place == count - 1) & (core == index))
        def _(index=index):
            write(1, ends[index])


def share(mask, rows):
    chip = lax.shift_right_logical(lax.axis_index("energy"), 1)
    return pl.ds(pl.multiple_of(lax.bitwise_xor(chip, mask) * rows, rows), rows)


def mix_kernel(chips, lowest, weights, *refs):
    parcels, (mine, other) = refs[:chips], refs[chips : chips + 2]
    energy = lax.axis_index("energy")
    core = lax.rem(energy, 2)

    @pl.when(lax.axis_index("slab") >= lowest)
    def _():
        sources = [lax.bitwise_xor(energy, 2 * mask) for mask in range(chips)]
        for mask in range(chips):
            for target, out in ((sources[mask], mine), (sources[mask] + 1 - 2 * core, other)):
                total = weights[target, sources[0]] * parcels[0][...]
                for index in range(1, chips):
                    total += weights[target, sources[index]] * parcels[index][...]
                out[mask] = total


def sum_kernel(chips, lowest, mine, other, *outs):
    @pl.when(lax.axis_index("slab") >= lowest)
    def _():
        for mask in range(chips):
            outs[mask][...] = mine[mask] + other[mask]


def place_kernel(count, chips, *refs):
    rounds = [refs[index * chips : (index + 1) * chips] for index in range(3)]
    scattering, sems = refs[3 * chips :]
    size = scattering.shape[-1]
    place = lax.axis_index("slab")

    def copies(slab, parcels):
        for mask, parcel in enumerate(parcels):
            for part in range(2):
                yield pltpu.make_async_copy(
                    parcel.at[:, pl.ds(part * size, size)],
                    scattering.at[slab, part, share(mask, parcel.shape[0]), :],
                    sems.at[slab, mask, part],
                )

    def start(slab, parcels):
        for copy in copies(slab, parcels):
            copy.start()

    before, first, last = rounds
    pl.when(place < count - 1)(lambda: start(1, before))
    pl.when(place == count - 1)(lambda: start(1, last))
    start(0, first)
    for slab, parcels in ((1, before), (0, first)):
        for copy in copies(slab, parcels):
            copy.wait()


def mode_weights(targets, sources, offsets, emission, absorption):
    spacing = sources[None, :, None] - targets[:, None, None]
    emitted = jnp.where(
        spacing == -offsets[None, None, :],
        emission[None, None, :],
        jnp.zeros_like(emission)[None, None, :],
    )
    absorbed = jnp.where(
        spacing == offsets[None, None, :],
        absorption[None, None, :],
        jnp.zeros_like(absorption)[None, None, :],
    )
    return jnp.sum(emitted + absorbed, axis=-1)


def relay_pairs(step, energies, count):
    pairs = []
    for energy in range(energies):
        turn = step - (energy + LEADING) % 2
        if 0 <= turn <= count - 2:
            ends = (turn, turn + 1)
        elif count - 1 <= turn <= 2 * count - 3:
            ends = (2 * count - 2 - turn, 2 * count - 3 - turn)
        else:
            continue
        pairs.append(tuple(energy * count + end for end in ends))
    return pairs


def shards(energies, count, free_green, self_energy, coupling, pattern, offsets, emission, absorption):
    size, blocks = free_green.shape[-1], pattern.shape[-1]
    args = (free_green[0], self_energy[0], coupling, pattern)
    row = shape(size, 2 * size)
    factor = shape(size, size, HALF, 2, 3)
    row_v = pltpu.VMEM(row.shape, F32)
    product = 24 * size**3
    loading = load_scratch(size, blocks) + matrices(3, size)

    def relay(step, value):
        return lax.ppermute(value, ("energy", "slab"), relay_pairs(step, energies, count))

    (begun,) = call(
        source_kernel,
        [row],
        loading + [row_v, pltpu.SemaphoreType.DMA((2,))],
        args,
        [HBM] * 4,
        [HBM],
        flops=6 * product,
        name="source",
        limit=61,
    )
    arrived, outs, firsts, lasts = [relay(0, begun)], [], [], []
    whole, source, coupler, opening, left_lead, left_tail, forward, backward = call(
        map_kernel,
        [row] * 4 + [factor, factor, row, row],
        loading,
        args,
        [HBM] * 4,
        flops=12 * product,
        name="left_maps",
        limit=49,
    )
    left_map = [left_lead, left_tail, whole]
    begun, _ = lax.optimization_barrier((arrived[0], whole))
    token = lax.ppermute(
        begun[:8, :128],
        ("energy", "slab"),
        [
            (energy * count, (energy ^ 1) * count)
            for energy in range(energies)
            if (energy + LEADING) % 2 == 0
        ],
    )
    right_map = None
    for step in range(2 * count - 2):
        lefts, rights = step <= count - 1, step >= count - 1
        closing = lefts and step >= count - 2
        args = [arrived[step]]
        if lefts:
            args += left_map
        if rights:
            args += right_map[:3]
        if closing:
            args += [forward, backward, source, coupler, opening]
        if step == 0:
            args.append(token)
        made = call(
            functools.partial(relay_kernel, step, count, lefts, rights),
            [row] * (3 if closing else 1),
            matrices(3 if closing else 1, size),
            args,
            flops=2 * product,
            name="relay",
        )
        outs.append(made[0])
        firsts += made[1:2]
        lasts += made[2:]
        arrived.append(relay(step + 1, made[0]))
        if step == count - 2:
            right_map = call(
                functools.partial(prepare_kernel, count),
                [factor, factor, row, factor, factor, row],
                [row_v] + matrices(4, size),
                arrived[: count - 1] + [source, forward, backward, coupler, opening],
                flops=11 * product,
                name="right_maps",
            )

    chips = energies // 2
    parcel = shape(size // chips, 2 * size)
    partial = shape(size // chips, 2 * size, F32, chips)
    everyone = jnp.arange(energies, dtype=jnp.int32)
    weights = mode_weights(everyone, everyone, offsets, emission, absorption)

    def send(value, flip, places, down=0):
        pairs = [
            (energy * count + i, (energy ^ flip) * count + i - down)
            for energy in range(energies)
            for i in places
        ]
        return lax.ppermute(value, ("energy", "slab"), pairs)

    def exchange(parcels, places):
        return parcels[:1] + [
            send(value, 2 * mask, places) for mask, value in enumerate(parcels) if mask
        ]

    def mix(parcels, places):
        mine, other = call(
            functools.partial(mix_kernel, chips, places[0]),
            [partial] * 2,
            [],
            [weights] + parcels,
            [SMEM] + [VMEM] * chips,
            flops=product // 8,
            name="mix",
        )
        return mine, send(other, 1, places)

    def add(places, mine, other):
        return call(
            functools.partial(sum_kernel, chips, places[0]),
            [parcel] * chips,
            [],
            [mine, other],
            name="sum",
        )

    below, every, end = list(range(1, count)), list(range(count)), [count - 1]
    packed = call(
        functools.partial(pack_kernel, count, chips),
        [parcel] * (2 * chips),
        [],
        outs[count - 2 :] + lasts,
        name="pack",
    )
    halves = mix(exchange(packed[:chips], below), below)
    last_halves = mix(exchange(packed[chips:], end), end)
    final, *_ = lax.optimization_barrier((arrived[-1], halves[0], last_halves[0]))
    arrived = arrived[count - 1 : -1] + [final]
    block, *parcels = call(
        functools.partial(first_kernel, count),
        [row] + [parcel] * chips,
        matrices(1, size),
        arrived + firsts + right_map[3:],
        flops=2 * product,
        name="first_slab",
    )
    received = exchange(parcels, every)
    sums = add(below, *halves)
    returned = [send(value, 2 * mask, below, 1) for mask, value in enumerate(sums)]
    last_returned = exchange(add(end, *last_halves), end)
    *received, _ = lax.optimization_barrier((*received, returned[0]))
    first_returned = exchange(add(every, *mix(received, every)), every)
    (retarded,) = call(
        functools.partial(retarded_kernel, count),
        [shape(size, size, F32, 2, 2)],
        [],
        [block] + arrived + lasts,
        name="retarded",
    )
    (scattering,) = call(
        functools.partial(place_kernel, count, chips),
        [shape(size, size, F32, 2, 2)],
        [pltpu.SemaphoreType.DMA((2, chips, 2))],
        returned + first_returned + last_returned,
        None,
        [HBM],
        name="scattering",
    )
    return (retarded[None], scattering[None])


def solution(mesh):
    blocks = P("energy", "slab", None, None, None)
    in_specs = (blocks, blocks, P("slab", None, None, None), P("slab", None, None), P(), P(), P())
    body = functools.partial(shards, mesh.shape["energy"], mesh.shape["slab"])
    return jax.shard_map(
        body, mesh=mesh, in_specs=in_specs, out_specs=(blocks, blocks), check_vma=False
    )
```

```python
import functools

import jax
import jax.numpy as jnp
from jax import lax
from jax.experimental import pallas as pl
from jax.experimental.pallas import tpu as pltpu
from jax.sharding import PartitionSpec as P

F32 = jnp.float32
HALF = jnp.bfloat16
HBM = pl.BlockSpec(memory_space=pltpu.HBM)
VMEM = pl.BlockSpec(memory_space=pltpu.VMEM)
SMEM = pl.BlockSpec(memory_space=pltpu.SMEM)
LEADING = 0


def split(value):
    high = value.astype(HALF)
    return high, (value - high.astype(F32)).astype(HALF)


def dot(left, right, transposed):
    dims = (((1,), (1 if transposed else 0,)), ((), ()))
    return lax.dot_general(left, right, dims, preferred_element_type=F32)


def parts_of(block, adjoint=False):
    size = block.shape[0]
    real, imag = block[:, :size], block[:, size:]
    return real, imag, (real - imag if adjoint else real + imag)


def put(matrix, block, adjoint=False):
    for index, part in enumerate(parts_of(block, adjoint)):
        matrix[0, index], matrix[1, index] = split(part)


def times_split(left, matrix, transposed=False):
    products = []
    for index, (high, low) in enumerate(left):
        size = high.shape[0]
        both = dot(jnp.concatenate([high, low], axis=0), matrix[0, index], transposed)
        products.append(both[:size] + both[size:] + dot(high, matrix[1, index], transposed))
    first, second, third = products
    if transposed:
        return jnp.concatenate([first + second, third - first + second], axis=1)
    return jnp.concatenate([first - second, third - first - second], axis=1)


def times(block, matrix, transposed=False):
    return times_split([split(part) for part in parts_of(block)], matrix, transposed)


def row_form(pair):
    return jnp.concatenate([pair[0], pair[1]], axis=1)


def adjoint_row(pair):
    return jnp.concatenate([jnp.transpose(pair[0]), -jnp.transpose(pair[1])], axis=1)


def expand(pattern, size):
    blocks = pattern.shape[0]
    tile = size // blocks
    rows = lax.broadcasted_iota(jnp.int32, (size, blocks), 0)
    first = lax.broadcasted_iota(jnp.int32, (size, blocks), 1) * tile
    member = jnp.where((rows >= first) & (rows < first + tile), 1.0, 0.0).astype(HALF)
    tall = dot(member, pattern.astype(F32).astype(HALF), False)
    return dot(tall.astype(HALF), member, True)


def couple(coupling, pattern):
    mask = expand(pattern[...], coupling.shape[-1])
    return jnp.concatenate([coupling[0] * mask, coupling[1] * mask], axis=1)


def trailing():
    return lax.rem(lax.axis_index("energy") + LEADING, 2)


def shape(rows, columns, dtype=F32, *lead):
    return jax.ShapeDtypeStruct(lead + (rows, columns), dtype)


def matrices(number, size):
    return [pltpu.VMEM((2, 3, size, size), HALF)] * number


def call(kernel, outs, scratch, args, specs=None, flops=0, name=None, limit=40):
    made = pl.pallas_call(
        kernel,
        out_shape=outs,
        in_specs=specs or [VMEM] * len(args),
        out_specs=[VMEM] * len(outs),
        scratch_shapes=scratch,
        compiler_params=pltpu.CompilerParams(vmem_limit_bytes=limit * 2**20),
        cost_estimate=pl.CostEstimate(flops=flops, bytes_accessed=2**20, transcendentals=0),
        name=name,
    )(*args)
    return list(made)


class Loads:
    def __init__(self, args, targets, sems, couplers=(0, 1), blocks=True):
        order = [(0, 0), (1, 0), (3, 1), (2, 1), (1, 1), (0, 1), (3, 0), (2, 0)]
        self.copies = {
            (which, slab): pltpu.make_async_copy(
                args[which].at[slab], targets[which].at[slab], sems.at[index]
            )
            for index, (which, slab) in enumerate(order)
            if (blocks if which < 2 else slab in couplers)
        }
        self.targets = targets
        for copy in self.copies.values():
            copy.start()

    def get(self, which, slab):
        self.copies[which, slab].wait()
        return self.targets[which].at[slab]

    def green(self, slab):
        return row_form(self.get(0, slab))

    def sigma(self, slab):
        return row_form(self.get(1, slab))

    def coupler(self, slab):
        tiles = self.get(3, slab)
        return couple(self.get(2, slab), tiles)


def load_scratch(size, blocks):
    return [
        pltpu.VMEM((2, 2, size, size), F32),
        pltpu.VMEM((2, 2, size, size), F32),
        pltpu.VMEM((2, 2, size, size), F32),
        pltpu.VMEM((2, blocks, blocks), jnp.int32),
        pltpu.SemaphoreType.DMA((8,)),
    ]


def left_sources(loads, whole, source, coupler_out, m_a, m_b, m_c):
    first = loads.green(0)
    put(m_b, first)
    put(m_a, loads.sigma(0))
    made = first + times(times(first, m_a), m_b)
    if source is not None:
        source[...] = made
    put(m_a, made)
    coupler = loads.coupler(1)
    if coupler_out is not None:
        coupler_out[...] = coupler
    put(m_c, coupler, True)
    inner = loads.sigma(1) + times(times(coupler, m_a), m_c, True)
    put(m_a, inner)
    second = loads.green(1)
    put(m_b, second)
    whole[...] = second + times(times(second, m_a), m_b)
    return first, second


def source_kernel(green, sigma, coupling, pattern, whole, gate, *scratch):
    @pl.when(lax.axis_index("slab") == 0)
    def _():
        loads = Loads((green, sigma, coupling, pattern), scratch[:4], scratch[4], (1,))
        left_sources(loads, whole, None, None, *scratch[5:])

    @pl.when((lax.axis_index("slab") > 0) & (trailing() == 1))
    def _():
        loads = Loads((green, sigma, coupling, pattern), scratch[:4], scratch[4], (0,), False)
        gate[...] = loads.coupler(0)[: gate.shape[0]]


def map_kernel(
    green, sigma, coupling, pattern,
    whole, source, coupler, upper, lower, lead, tail, forward, backward, *scratch,
):
    m_a, m_b, m_c = scratch[5:]
    loads = Loads((green, sigma, coupling, pattern), scratch[:4], scratch[4])
    first, second = left_sources(loads, whole, source, coupler, m_a, m_b, m_c)
    before = loads.coupler(0)

    @pl.when(lax.axis_index("slab") > 0)
    def _():
        upper[...] = before[: upper.shape[0]]
        lower[...] = before[upper.shape[0] :]
        put(m_a, first)
        size = before.shape[0]
        behind = times(adjoint_row((before[:, :size], before[:, size:])), m_a)
        backward[...] = behind
        put(tail, times(times(behind, m_c, True), m_b))
        put(m_a, before)
        ahead = times(first, m_a)
        forward[...] = ahead
        put(m_a, ahead)
        put(m_c, coupler[...])
        put(lead, times(times(second, m_c), m_a))


def right_terms(first, last, coupler, m_coupler, m_first, m_last, m_upper):
    put(m_coupler, coupler, True)
    put(m_last, last)
    through = times(times(first, m_coupler, True), m_last)
    put(m_first, first)
    put(m_upper, times(coupler, m_first))
    return through, first + times(through, m_upper)


def prepare_kernel(count, *refs):
    arrived, wholes = refs[: count - 1], refs[count - 1 : 2 * count - 2]
    refs = refs[2 * count - 2 :]
    start_whole, source, forward, backward, coupler = refs[:5]
    gate, upper, lower = refs[5:8]
    lead, tail, constant, last_lead, last_tail = refs[8:13]
    first_v, last_v, m_a, m_b, m_c, m_d = refs[13:]
    place = lax.axis_index("slab")

    @pl.when(place == 0)
    def _():
        first_v[...] = source[...]
        last_v[...] = start_whole[...]

    for turn in range(count - 1):
        @pl.when((place > 0) & (place == turn + 1 - trailing()))
        def _(turn=turn):
            last_v[...] = wholes[turn][...]
            put(m_a, arrived[turn][...])

    @pl.when((place > 0) & (place < count - 1))
    def _():
        put(m_b, backward[...])
        first_v[...] = source[...] + times(times(forward[...], m_a), m_b)

    @pl.when(place < count - 1)
    def _():
        first, last = first_v[...], last_v[...]
        through, joined = right_terms(first, last, coupler[...], m_a, m_b, m_c, m_d)
        constant[...] = joined
        above = jnp.where(trailing() == 0, upper[...], gate[...])
        next_coupler = jnp.concatenate([above, lower[...]], axis=0)
        put(m_a, next_coupler, True)
        put(lead, times(through, m_a, True))
        put(last_lead, times(last, m_a, True))
        behind = times(next_coupler, m_c)
        put(last_tail, behind)
        put(tail, times(behind, m_d))


def apply_map(mapping, m_x):
    lead, tail, constant = mapping
    ahead = [(lead[0, index], lead[1, index]) for index in range(3)]
    return constant[...] + times(times_split(ahead, m_x), tail)


def relay_kernel(step, count, lefts, rights, *refs):
    refs = list(refs)
    place = lax.axis_index("slab")
    turn = step - trailing()
    is_left = (turn >= 0) & (turn <= count - 2) & (place == turn + 1)
    is_right = (turn >= count - 1) & (place == 2 * count - 3 - turn)
    closing = lefts and step >= count - 2
    arrived = refs.pop(0)
    left_map = [refs.pop(0) for _ in range(3)] if lefts else None
    right_map = [refs.pop(0) for _ in range(3)] if rights else None
    if closing:
        forward, backward, source, coupler = [refs.pop(0) for _ in range(4)]
    if step == 0:
        refs.pop(0)
    out = refs.pop(0)
    if closing:
        end, m_x, m_a, m_b, m_c = refs
    else:
        (m_x,) = refs

    if step == 0:
        @pl.when(place == 0)
        def _():
            out[...] = left_map[2][...]

    if lefts:
        @pl.when(is_left)
        def _():
            put(m_x, arrived[...])
            out[...] = apply_map(left_map, m_x)

    if closing:
        @pl.when(is_left & (place == count - 1))
        def _():
            last = out[...]
            end[...] = last
            put(m_a, backward[...])
            first = source[...] + times(times(forward[...], m_x), m_a)
            _, joined = right_terms(first, last, coupler[...], m_a, m_b, m_c, m_x)
            out[...] = joined

    if rights:
        @pl.when(is_right & (place > 0))
        def _():
            put(m_x, arrived[...])
            out[...] = apply_map(right_map, m_x)


def last_kernel(count, *refs):
    refs = list(refs)
    arrived = [refs.pop(0) for _ in range(count)]
    ends = [refs.pop(0) for _ in range(2)]
    last_lead, last_tail, whole_start = [refs.pop(0) for _ in range(3)]
    wholes = [refs.pop(0) for _ in range(count - 1)]
    block, *parcels, m_x = refs
    place = lax.axis_index("slab")
    core = trailing()
    is_last = place == count - 1

    for index in range(count):
        @pl.when(jnp.logical_not(is_last) & (2 * count - 3 - place + core == count - 1 + index))
        def _(index=index):
            put(m_x, arrived[index][...])

    for index in range(2):
        @pl.when(is_last & (core == index))
        def _(index=index):
            block[...] = ends[index][...]

    @pl.when(place == 0)
    def _():
        block[...] = apply_map((last_lead, last_tail, whole_start), m_x)

    for index in range(count - 1):
        @pl.when((place > 0) & jnp.logical_not(is_last) & (place - 1 + core == index))
        def _(index=index):
            block[...] = apply_map((last_lead, last_tail, wholes[index]), m_x)

    pack(block, parcels)


def first_kernel(count, *refs):
    arrived, outs = refs[:2], refs[2 : count + 2]
    right_map = refs[count + 2 : count + 5]
    block, *parcels, m_x = refs[count + 6 :]
    place, core = lax.axis_index("slab"), trailing()
    at = jnp.where(place == count - 1, count - 2 + core, 2 * count - 3 - place + core)

    for index in range(count):
        @pl.when((place > 0) & (at == count - 2 + index))
        def _(index=index):
            block[...] = outs[index][...]

    for index in range(2):
        @pl.when((place == 0) & (core == index))
        def _(index=index):
            put(m_x, arrived[index][...])

    @pl.when(place == 0)
    def _():
        block[...] = apply_map(right_map, m_x)

    pack(block, parcels)


def pack(block, parcels):
    for mask, parcel in enumerate(parcels):
        parcel[...] = block[share(mask, parcel.shape[0]), :]


def unpack_kernel(*refs):
    blocks, out = refs[:2], refs[2]
    size = out.shape[-1]
    for slab, block in enumerate(blocks):
        for part in range(2):
            out[slab, part] = block[:, part * size : (part + 1) * size]


def share(mask, rows):
    chip = lax.shift_right_logical(lax.axis_index("energy"), 1)
    return pl.ds(pl.multiple_of(lax.bitwise_xor(chip, mask) * rows, rows), rows)


def mix_kernel(chips, weights, *refs):
    parcels, (mine, other) = refs[:chips], refs[chips:]
    energy = lax.axis_index("energy")
    core = lax.rem(energy, 2)
    sources = [lax.bitwise_xor(energy, 2 * mask) for mask in range(chips)]
    rows = parcels[0].shape[0]
    for row in range(0, rows, 8):
        where = slice(row, row + 8)
        values = [parcel[where] for parcel in parcels]
        for mask in range(chips):
            for target, out in ((sources[mask], mine), (sources[mask] + 1 - 2 * core, other)):
                total = weights[target, sources[0]] * values[0]
                for index in range(1, chips):
                    total += weights[target, sources[index]] * values[index]
                out[mask, where] = total


def sum_kernel(chips, mine, other, *outs):
    for mask in range(chips):
        outs[mask][...] = mine[mask] + other[mask]


def place_kernel(chips, *refs):
    scattering = refs[2 * chips]
    size = scattering.shape[-1]
    for slab in range(2):
        for mask, parcel in enumerate(refs[slab * chips : (slab + 1) * chips]):
            where = share(mask, parcel.shape[0])
            for part in range(2):
                scattering[slab, part, where, :] = parcel[:, part * size : (part + 1) * size]


def mode_weights(targets, sources, offsets, emission, absorption):
    spacing = sources[None, :, None] - targets[:, None, None]
    emitted = jnp.where(
        spacing == -offsets[None, None, :],
        emission[None, None, :],
        jnp.zeros_like(emission)[None, None, :],
    )
    absorbed = jnp.where(
        spacing == offsets[None, None, :],
        absorption[None, None, :],
        jnp.zeros_like(absorption)[None, None, :],
    )
    return jnp.sum(emitted + absorbed, axis=-1)


def relay_pairs(step, energies, count):
    pairs = []
    for energy in range(energies):
        turn = step - (energy + LEADING) % 2
        if 0 <= turn <= count - 2:
            ends = (turn, turn + 1)
        elif count - 1 <= turn <= 2 * count - 3:
            ends = (2 * count - 2 - turn, 2 * count - 3 - turn)
        else:
            continue
        pairs.append(tuple(energy * count + end for end in ends))
    return pairs


def shards(energies, count, free_green, self_energy, coupling, pattern, offsets, emission, absorption):
    size, blocks = free_green.shape[-1], pattern.shape[-1]
    args = (free_green[0], self_energy[0], coupling, pattern)
    row = shape(size, 2 * size)
    half = shape(size // 2, 2 * size)
    factor = shape(size, size, HALF, 2, 3)
    row_v = pltpu.VMEM(row.shape, F32)
    product = 24 * size**3
    loading = load_scratch(size, blocks) + matrices(3, size)

    def relay(step, value):
        return lax.ppermute(value, ("energy", "slab"), relay_pairs(step, energies, count))

    def lower_place(value, cores):
        pairs = [
            (energy * count + i, energy * count + i - 1)
            for energy in range(energies)
            for i in range(1, count)
            if (energy + LEADING) % 2 in cores
        ]
        return lax.ppermute(value, ("energy", "slab"), pairs)

    begun = call(
        source_kernel,
        [row, half],
        loading,
        args,
        [HBM] * 4,
        flops=6 * product,
        name="source",
        limit=61,
    )
    arrived, outs, ends = [relay(0, begun[0])], [], []
    gate = lower_place(begun[1], [1])
    whole, source, coupler, upper, lower, left_lead, left_tail, forward, backward = call(
        map_kernel,
        [row] * 3 + [half] * 2 + [factor, factor, row, row],
        loading,
        args,
        [HBM] * 4,
        flops=12 * product,
        name="left_maps",
        limit=49,
    )
    left_map = [left_lead, left_tail, whole]
    right_map = None
    for step in range(2 * count - 2):
        lefts, rights = step <= count - 1, step >= count - 1
        closing = lefts and step >= count - 2
        args = [arrived[step]]
        if lefts:
            args += left_map
        if rights:
            args += right_map[:3]
        if closing:
            args += [forward, backward, source, coupler]
        if step == 0:
            args.append(gate)
        made = call(
            functools.partial(relay_kernel, step, count, lefts, rights),
            [row] * (2 if closing else 1),
            matrices(4 if closing else 1, size),
            args,
            flops=2 * product,
            name="relay",
        )
        outs.append(made[0])
        ends += made[1:]
        arrived.append(relay(step + 1, made[0]))
        if step == 0:
            lower = lower_place(lower, [0, 1])
            upper = lower_place(upper, [0])
        if step == count - 2:
            args = arrived[: count - 1] + outs[: count - 1]
            args += [whole, source, forward, backward, coupler, gate, upper, lower]
            right_map = call(
                functools.partial(prepare_kernel, count),
                [factor, factor, row, factor, factor],
                [row_v] * 2 + matrices(4, size),
                args,
                flops=10 * product,
                name="right_maps",
            )
    chips = energies // 2
    parcel = shape(size // chips, 2 * size)
    blocks, parcels = [None, None], [None, None]
    args = arrived[count - 1 :] + ends + right_map[3:] + [whole] + outs[: count - 1]
    blocks[1], *parcels[1] = call(
        functools.partial(last_kernel, count),
        [row] + [parcel] * chips,
        matrices(1, size),
        args,
        flops=2 * product,
        name="second_slab",
    )
    args = arrived[-2:] + outs[count - 2 :] + right_map[:3] + blocks[1:]
    blocks[0], *parcels[0] = call(
        functools.partial(first_kernel, count),
        [row] + [parcel] * chips,
        matrices(1, size),
        args,
        flops=2 * product,
        name="first_slab",
    )
    (retarded,) = call(
        unpack_kernel, [shape(size, size, F32, 2, 2)], [], blocks, name="retarded"
    )

    def exchange(values):
        return values[:1] + [
            lax.ppermute(value, "energy", [(i, i ^ (2 * mask)) for i in range(energies)])
            for mask, value in enumerate(values)
            if mask
        ]

    everyone = jnp.arange(energies, dtype=jnp.int32)
    weights = mode_weights(everyone, everyone, offsets, emission, absorption)
    partial = shape(size // chips, 2 * size, F32, chips)
    sums = [None, None]
    for slab in (1, 0):
        mine, other = call(
            functools.partial(mix_kernel, chips),
            [partial] * 2,
            [],
            [weights] + exchange(parcels[slab]),
            [SMEM] + [VMEM] * chips,
            flops=product // 8,
            name="mix",
        )
        other = lax.ppermute(other, "energy", [(i, i ^ 1) for i in range(energies)])
        sums[slab] = call(
            functools.partial(sum_kernel, chips), [parcel] * chips, [], [mine, other], name="sum"
        )
    returned = [exchange(sums[slab]) for slab in (1, 0)][::-1]
    (scattering,) = call(
        functools.partial(place_kernel, chips),
        [shape(size, size, F32, 2, 2)],
        [],
        returned[0] + returned[1],
        name="scattering",
    )
    return (retarded[None], scattering[None])


def solution(mesh):
    blocks = P("energy", "slab", None, None, None)
    in_specs = (blocks, blocks, P("slab", None, None, None), P("slab", None, None), P(), P(), P())
    body = functools.partial(shards, mesh.shape["energy"], mesh.shape["slab"])
    return jax.shard_map(
        body, mesh=mesh, in_specs=in_specs, out_specs=(blocks, blocks), check_vma=False
    )
```

```python
import functools

import jax
import jax.numpy as jnp
from jax import lax
from jax.experimental import pallas as pl
from jax.experimental.pallas import tpu as pltpu
from jax.sharding import PartitionSpec as P

F32 = jnp.float32
HALF = jnp.bfloat16
HBM = pl.BlockSpec(memory_space=pltpu.HBM)
VMEM = pl.BlockSpec(memory_space=pltpu.VMEM)
SMEM = pl.BlockSpec(memory_space=pltpu.SMEM)
LEADING = 0


def split(value):
    high = value.astype(HALF)
    return high, (value - high.astype(F32)).astype(HALF)


def dot(left, right, transposed):
    dims = (((1,), (1 if transposed else 0,)), ((), ()))
    return lax.dot_general(left, right, dims, preferred_element_type=F32)


def parts_of(block, adjoint=False):
    size = block.shape[0]
    real, imag = block[:, :size], block[:, size:]
    return real, imag, (real - imag if adjoint else real + imag)


def put(matrix, block, adjoint=False):
    for index, part in enumerate(parts_of(block, adjoint)):
        matrix[0, index], matrix[1, index] = split(part)


def times_split(left, matrix, transposed=False):
    products = []
    for index, (high, low) in enumerate(left):
        size = high.shape[0]
        both = dot(jnp.concatenate([high, low], axis=0), matrix[0, index], transposed)
        products.append(both[:size] + both[size:] + dot(high, matrix[1, index], transposed))
    first, second, third = products
    if transposed:
        return jnp.concatenate([first + second, third - first + second], axis=1)
    return jnp.concatenate([first - second, third - first - second], axis=1)


def times(block, matrix, transposed=False):
    return times_split([split(part) for part in parts_of(block)], matrix, transposed)


def row_form(pair):
    return jnp.concatenate([pair[0], pair[1]], axis=1)


def adjoint_row(pair):
    return jnp.concatenate([jnp.transpose(pair[0]), -jnp.transpose(pair[1])], axis=1)


def expand(pattern, size):
    blocks = pattern.shape[0]
    tile = size // blocks
    rows = lax.broadcasted_iota(jnp.int32, (size, blocks), 0)
    first = lax.broadcasted_iota(jnp.int32, (size, blocks), 1) * tile
    member = jnp.where((rows >= first) & (rows < first + tile), 1.0, 0.0).astype(HALF)
    tall = dot(member, pattern.astype(F32).astype(HALF), False)
    return dot(tall.astype(HALF), member, True)


def couple(coupling, pattern):
    mask = expand(pattern[...], coupling.shape[-1])
    return jnp.concatenate([coupling[0] * mask, coupling[1] * mask], axis=1)


def trailing():
    return lax.rem(lax.axis_index("energy") + LEADING, 2)


def shape(rows, columns, dtype=F32, *lead):
    return jax.ShapeDtypeStruct(lead + (rows, columns), dtype)


def matrices(number, size):
    return [pltpu.VMEM((2, 3, size, size), HALF)] * number


def call(kernel, outs, scratch, args, specs=None, flops=0, name=None, limit=40):
    made = pl.pallas_call(
        kernel,
        out_shape=outs,
        in_specs=specs or [VMEM] * len(args),
        out_specs=[VMEM] * len(outs),
        scratch_shapes=scratch,
        compiler_params=pltpu.CompilerParams(vmem_limit_bytes=int(limit * 2**20)),
        cost_estimate=pl.CostEstimate(flops=flops, bytes_accessed=2**20, transcendentals=0),
        name=name,
    )(*args)
    return list(made)


class Loads:
    def __init__(self, args, targets, sems, couplers=(0, 1), blocks=True):
        order = [(0, 0), (1, 0), (3, 1), (2, 1), (1, 1), (0, 1), (3, 0), (2, 0)]
        self.copies = {
            (which, slab): pltpu.make_async_copy(
                args[which].at[slab], targets[which].at[slab], sems.at[index]
            )
            for index, (which, slab) in enumerate(order)
            if (blocks if which < 2 else slab in couplers)
        }
        self.targets = targets
        for copy in self.copies.values():
            copy.start()

    def get(self, which, slab):
        self.copies[which, slab].wait()
        return self.targets[which].at[slab]

    def green(self, slab):
        return row_form(self.get(0, slab))

    def sigma(self, slab):
        return row_form(self.get(1, slab))

    def coupler(self, slab):
        tiles = self.get(3, slab)
        return couple(self.get(2, slab), tiles)


def load_scratch(size, blocks):
    return [
        pltpu.VMEM((2, 2, size, size), F32),
        pltpu.VMEM((2, 2, size, size), F32),
        pltpu.VMEM((2, 2, size, size), F32),
        pltpu.VMEM((2, blocks, blocks), jnp.int32),
        pltpu.SemaphoreType.DMA((8,)),
    ]


def left_sources(loads, whole, source, coupler_out, m_a, m_b, m_c):
    first = loads.green(0)
    put(m_b, first)
    put(m_a, loads.sigma(0))
    made = first + times(times(first, m_a), m_b)
    if source is not None:
        source[...] = made
    put(m_a, made)
    coupler = loads.coupler(1)
    if coupler_out is not None:
        coupler_out[...] = coupler
    put(m_c, coupler, True)
    inner = loads.sigma(1) + times(times(coupler, m_a), m_c, True)
    put(m_a, inner)
    second = loads.green(1)
    put(m_b, second)
    whole[...] = second + times(times(second, m_a), m_b)
    return first, second


def source_kernel(green, sigma, coupling, pattern, whole, gate, *scratch):
    @pl.when(lax.axis_index("slab") == 0)
    def _():
        loads = Loads((green, sigma, coupling, pattern), scratch[:4], scratch[4], (1,))
        left_sources(loads, whole, None, None, *scratch[5:])

    @pl.when((lax.axis_index("slab") > 0) & (trailing() == 1))
    def _():
        loads = Loads((green, sigma, coupling, pattern), scratch[:4], scratch[4], (0,), False)
        gate[...] = loads.coupler(0)[: gate.shape[0]]


def map_kernel(
    green, sigma, coupling, pattern,
    whole, source, coupler, upper, lower, lead, tail, forward, backward, *scratch,
):
    m_a, m_b, m_c = scratch[5:]
    loads = Loads((green, sigma, coupling, pattern), scratch[:4], scratch[4])
    first, second = left_sources(loads, whole, source, coupler, m_a, m_b, m_c)
    before = loads.coupler(0)

    @pl.when(lax.axis_index("slab") > 0)
    def _():
        upper[...] = before[: upper.shape[0]]
        lower[...] = before[upper.shape[0] :]
        put(m_a, first)
        size = before.shape[0]
        behind = times(adjoint_row((before[:, :size], before[:, size:])), m_a)
        backward[...] = behind
        put(tail, times(times(behind, m_c, True), m_b))
        put(m_a, before)
        ahead = times(first, m_a)
        forward[...] = ahead
        put(m_a, ahead)
        put(m_c, coupler[...])
        put(lead, times(times(second, m_c), m_a))


def right_terms(first, last, coupler, m_coupler, m_first, m_last, m_upper):
    put(m_coupler, coupler, True)
    put(m_last, last)
    through = times(times(first, m_coupler, True), m_last)
    put(m_first, first)
    put(m_upper, times(coupler, m_first))
    return through, first + times(through, m_upper)


def prepare_kernel(count, *refs):
    arrived, wholes = refs[: count - 1], refs[count - 1 : 2 * count - 2]
    refs = refs[2 * count - 2 :]
    start_whole, source, forward, backward, coupler = refs[:5]
    gate, upper, lower = refs[5:8]
    lead, tail, constant, last_lead, last_tail = refs[8:13]
    first_v, last_v, m_a, m_b, m_c, m_d = refs[13:]
    place = lax.axis_index("slab")

    @pl.when(place == 0)
    def _():
        first_v[...] = source[...]
        last_v[...] = start_whole[...]

    for turn in range(count - 1):
        @pl.when((place > 0) & (place == turn + 1 - trailing()))
        def _(turn=turn):
            last_v[...] = wholes[turn][...]
            put(m_a, arrived[turn][...])

    @pl.when((place > 0) & (place < count - 1))
    def _():
        put(m_b, backward[...])
        first_v[...] = source[...] + times(times(forward[...], m_a), m_b)

    @pl.when(place < count - 1)
    def _():
        first, last = first_v[...], last_v[...]
        through, joined = right_terms(first, last, coupler[...], m_a, m_b, m_c, m_d)
        constant[...] = joined
        above = jnp.where(trailing() == 0, upper[...], gate[...])
        next_coupler = jnp.concatenate([above, lower[...]], axis=0)
        put(m_a, next_coupler, True)
        put(lead, times(through, m_a, True))
        put(last_lead, times(last, m_a, True))
        behind = times(next_coupler, m_c)
        put(last_tail, behind)
        put(tail, times(behind, m_d))


def apply_map(mapping, m_x):
    lead, tail, constant = mapping
    ahead = [(lead[0, index], lead[1, index]) for index in range(3)]
    return constant[...] + times(times_split(ahead, m_x), tail)


def relay_kernel(step, count, lefts, rights, *refs):
    refs = list(refs)
    place = lax.axis_index("slab")
    turn = step - trailing()
    is_left = (turn >= 0) & (turn <= count - 2) & (place == turn + 1)
    is_right = (turn >= count - 1) & (place == 2 * count - 3 - turn)
    closing = lefts and step >= count - 2
    arrived = refs.pop(0)
    left_map = [refs.pop(0) for _ in range(3)] if lefts else None
    right_map = [refs.pop(0) for _ in range(3)] if rights else None
    if closing:
        forward, backward, source, coupler = [refs.pop(0) for _ in range(4)]
    if step == 0:
        refs.pop(0)
    out = refs.pop(0)
    if closing:
        end, m_x, m_a, m_b, m_c = refs
    else:
        (m_x,) = refs

    if step == 0:
        @pl.when(place == 0)
        def _():
            out[...] = left_map[2][...]

    if lefts:
        @pl.when(is_left)
        def _():
            put(m_x, arrived[...])
            out[...] = apply_map(left_map, m_x)

    if closing:
        @pl.when(is_left & (place == count - 1))
        def _():
            last = out[...]
            end[...] = last
            put(m_a, backward[...])
            first = source[...] + times(times(forward[...], m_x), m_a)
            _, joined = right_terms(first, last, coupler[...], m_a, m_b, m_c, m_x)
            out[...] = joined

    if rights:
        @pl.when(is_right & (place > 0))
        def _():
            put(m_x, arrived[...])
            out[...] = apply_map(right_map, m_x)


def last_kernel(count, *refs):
    refs = list(refs)
    arrived = [refs.pop(0) for _ in range(count)]
    ends = [refs.pop(0) for _ in range(2)]
    last_lead, last_tail, whole_start = [refs.pop(0) for _ in range(3)]
    wholes = [refs.pop(0) for _ in range(count - 1)]
    refs.pop(0)
    block, *parcels, m_x = refs
    place = lax.axis_index("slab")
    core = trailing()
    is_last = place == count - 1

    for index in range(count):
        @pl.when(jnp.logical_not(is_last) & (2 * count - 3 - place + core == count - 1 + index))
        def _(index=index):
            put(m_x, arrived[index][...])

    for index in range(2):
        @pl.when(is_last & (core == index))
        def _(index=index):
            block[...] = ends[index][...]

    @pl.when(place == 0)
    def _():
        block[...] = apply_map((last_lead, last_tail, whole_start), m_x)

    for index in range(count - 1):
        @pl.when((place > 0) & jnp.logical_not(is_last) & (place - 1 + core == index))
        def _(index=index):
            block[...] = apply_map((last_lead, last_tail, wholes[index]), m_x)

    pack(block, parcels)


def first_kernel(count, *refs):
    arrived, outs = refs[:2], refs[2 : count + 2]
    right_map = refs[count + 2 : count + 5]
    block, *parcels, m_x = refs[count + 6 :]
    place, core = lax.axis_index("slab"), trailing()
    at = jnp.where(place == count - 1, count - 2 + core, 2 * count - 3 - place + core)

    for index in range(count):
        @pl.when((place > 0) & (at == count - 2 + index))
        def _(index=index):
            block[...] = outs[index][...]

    for index in range(2):
        @pl.when((place == 0) & (core == index))
        def _(index=index):
            put(m_x, arrived[index][...])

    @pl.when(place == 0)
    def _():
        block[...] = apply_map(right_map, m_x)

    pack(block, parcels)


def pack(block, parcels):
    for mask, parcel in enumerate(parcels):
        parcel[...] = block[share(mask, parcel.shape[0]), :]


def unpack_kernel(*refs):
    blocks, out = refs[:2], refs[2]
    size = out.shape[-1]
    for slab, block in enumerate(blocks):
        for part in range(2):
            out[slab, part] = block[:, part * size : (part + 1) * size]


def share(mask, rows):
    chip = lax.shift_right_logical(lax.axis_index("energy"), 1)
    return pl.ds(pl.multiple_of(lax.bitwise_xor(chip, mask) * rows, rows), rows)


def weight_kernel(chips, weights, tiles):
    energy = lax.axis_index("energy")
    core = lax.rem(energy, 2)
    sources = [lax.bitwise_xor(energy, 2 * mask) for mask in range(chips)]
    for mask in range(chips):
        for side, target in enumerate((sources[mask], sources[mask] + 1 - 2 * core)):
            for index in range(chips):
                weight = weights[target, sources[index]]
                tiles[side, mask, index] = jnp.full(tiles.shape[3:], weight, F32)


def mix_kernel(chips, tiles, *refs):
    parcels, outs = refs[:chips], refs[chips:]
    rows, columns = parcels[0].shape
    step, width = tiles.shape[3:]
    for row in range(0, rows, step):
        where = slice(row, row + step)
        values = [parcel[where] for parcel in parcels]
        for side, out in enumerate(outs):
            for mask in range(chips):
                total = None
                for index in range(chips):
                    weight = jnp.concatenate([tiles[side, mask, index]] * (columns // width), axis=1)
                    term = weight * values[index]
                    total = term if total is None else total + term
                out[mask, where] = total


def sum_kernel(chips, mine, other, *outs):
    for mask in range(chips):
        outs[mask][...] = mine[mask] + other[mask]


def place_kernel(chips, *refs):
    scattering = refs[2 * chips]
    size = scattering.shape[-1]
    for slab in range(2):
        for mask, parcel in enumerate(refs[slab * chips : (slab + 1) * chips]):
            where = share(mask, parcel.shape[0])
            for part in range(2):
                scattering[slab, part, where, :] = parcel[:, part * size : (part + 1) * size]


def mode_weights(targets, sources, offsets, emission, absorption):
    spacing = sources[None, :, None] - targets[:, None, None]
    emitted = jnp.where(
        spacing == -offsets[None, None, :],
        emission[None, None, :],
        jnp.zeros_like(emission)[None, None, :],
    )
    absorbed = jnp.where(
        spacing == offsets[None, None, :],
        absorption[None, None, :],
        jnp.zeros_like(absorption)[None, None, :],
    )
    return jnp.sum(emitted + absorbed, axis=-1)


def relay_pairs(step, energies, count):
    pairs = []
    for energy in range(energies):
        turn = step - (energy + LEADING) % 2
        if 0 <= turn <= count - 2:
            ends = (turn, turn + 1)
        elif count - 1 <= turn <= 2 * count - 3:
            ends = (2 * count - 2 - turn, 2 * count - 3 - turn)
        else:
            continue
        pairs.append(tuple(energy * count + end for end in ends))
    return pairs


def shards(energies, count, free_green, self_energy, coupling, pattern, offsets, emission, absorption):
    size, blocks = free_green.shape[-1], pattern.shape[-1]
    args = (free_green[0], self_energy[0], coupling, pattern)
    row = shape(size, 2 * size)
    half = shape(size // 2, 2 * size)
    factor = shape(size, size, HALF, 2, 3)
    row_v = pltpu.VMEM(row.shape, F32)
    product = 24 * size**3
    loading = load_scratch(size, blocks) + matrices(3, size)

    def relay(step, value):
        return lax.ppermute(value, ("energy", "slab"), relay_pairs(step, energies, count))

    def lower_place(value, cores):
        pairs = [
            (energy * count + i, energy * count + i - 1)
            for energy in range(energies)
            for i in range(1, count)
            if (energy + LEADING) % 2 in cores
        ]
        return lax.ppermute(value, ("energy", "slab"), pairs)

    begun = call(
        source_kernel,
        [row, half],
        loading,
        args,
        [HBM] * 4,
        flops=6 * product,
        name="source",
        limit=53,
    )
    arrived, outs, ends = [relay(0, begun[0])], [], []
    gate = lower_place(begun[1], [1])
    whole, source, coupler, upper, lower, left_lead, left_tail, forward, backward = call(
        map_kernel,
        [row] * 3 + [half] * 2 + [factor, factor, row, row],
        loading,
        args,
        [HBM] * 4,
        flops=12 * product,
        name="left_maps",
        limit=48.6,
    )
    left_map = [left_lead, left_tail, whole]
    right_map = None
    for step in range(2 * count - 2):
        lefts, rights = step <= count - 1, step >= count - 1
        closing = lefts and step >= count - 2
        args = [arrived[step]]
        if lefts:
            args += left_map
        if rights:
            args += right_map[:3]
        if closing:
            args += [forward, backward, source, coupler]
        if step == 0:
            args.append(gate)
        made = call(
            functools.partial(relay_kernel, step, count, lefts, rights),
            [row] * (2 if closing else 1),
            matrices(4 if closing else 1, size),
            args,
            flops=2 * product,
            name="relay",
        )
        outs.append(made[0])
        ends += made[1:]
        arrived.append(relay(step + 1, made[0]))
        if step == 0:
            lower = lower_place(lower, [0, 1])
            upper = lower_place(upper, [0])
        if step == count - 2:
            args = arrived[: count - 1] + outs[: count - 1]
            args += [whole, source, forward, backward, coupler, gate, upper, lower]
            right_map = call(
                functools.partial(prepare_kernel, count),
                [factor, factor, row, factor, factor],
                [row_v] * 2 + matrices(4, size),
                args,
                flops=10 * product,
                name="right_maps",
            )
    chips = energies // 2
    parcel = shape(size // chips, 2 * size)
    blocks, parcels = [None, None], [None, None]
    everyone = jnp.arange(energies, dtype=jnp.int32)
    weights = mode_weights(everyone, everyone, offsets, emission, absorption)
    (tiles,) = call(
        functools.partial(weight_kernel, chips),
        [shape(8, 128, F32, 2, chips, chips)],
        [],
        [weights],
        [SMEM],
        name="weights",
    )
    args = arrived[count - 1 :] + ends + right_map[3:] + [whole] + outs[: count - 1] + [tiles]
    blocks[1], *parcels[1] = call(
        functools.partial(last_kernel, count),
        [row] + [parcel] * chips,
        matrices(1, size),
        args,
        flops=2 * product,
        name="second_slab",
    )
    args = arrived[-2:] + outs[count - 2 :] + right_map[:3] + blocks[1:]
    blocks[0], *parcels[0] = call(
        functools.partial(first_kernel, count),
        [row] + [parcel] * chips,
        matrices(1, size),
        args,
        flops=2 * product,
        name="first_slab",
    )
    (retarded,) = call(
        unpack_kernel, [shape(size, size, F32, 2, 2)], [], blocks, name="retarded"
    )

    def exchange(values):
        return values[:1] + [
            lax.ppermute(value, "energy", [(i, i ^ (2 * mask)) for i in range(energies)])
            for mask, value in enumerate(values)
            if mask
        ]

    partial = shape(size // chips, 2 * size, F32, chips)
    sums = [None, None]
    for slab in (1, 0):
        mine, other = call(
            functools.partial(mix_kernel, chips),
            [partial] * 2,
            [],
            [tiles] + exchange(parcels[slab]),
            flops=product // 8,
            name="mix",
        )
        other = lax.ppermute(other, "energy", [(i, i ^ 1) for i in range(energies)])
        sums[slab] = call(
            functools.partial(sum_kernel, chips), [parcel] * chips, [], [mine, other], name="sum"
        )
    returned = [exchange(sums[slab]) for slab in (1, 0)][::-1]
    (scattering,) = call(
        functools.partial(place_kernel, chips),
        [shape(size, size, F32, 2, 2)],
        [],
        returned[0] + returned[1],
        name="scattering",
    )
    return (retarded[None], scattering[None])


def solution(mesh):
    blocks = P("energy", "slab", None, None, None)
    in_specs = (blocks, blocks, P("slab", None, None, None), P("slab", None, None), P(), P(), P())
    body = functools.partial(shards, mesh.shape["energy"], mesh.shape["slab"])
    return jax.shard_map(
        body, mesh=mesh, in_specs=in_specs, out_specs=(blocks, blocks), check_vma=False
    )
```

```python
import functools

import jax
import jax.numpy as jnp
from jax import lax
from jax.experimental import pallas as pl
from jax.experimental.pallas import tpu as pltpu
from jax.sharding import PartitionSpec as P

F32 = jnp.float32
HALF = jnp.bfloat16
HBM = pl.BlockSpec(memory_space=pltpu.HBM)
VMEM = pl.BlockSpec(memory_space=pltpu.VMEM)
SMEM = pl.BlockSpec(memory_space=pltpu.SMEM)
LEADING = 0


def split(value):
    high = value.astype(HALF)
    return high, (value - high.astype(F32)).astype(HALF)


def dot(left, right, transposed):
    dims = (((1,), (1 if transposed else 0,)), ((), ()))
    return lax.dot_general(left, right, dims, preferred_element_type=F32)


def parts_of(block, adjoint=False):
    size = block.shape[0]
    real, imag = block[:, :size], block[:, size:]
    return real, imag, (real - imag if adjoint else real + imag)


def put(matrix, block, adjoint=False):
    for index, part in enumerate(parts_of(block, adjoint)):
        matrix[0, index], matrix[1, index] = split(part)


def times_split(left, matrix, transposed=False):
    products = []
    for index, (high, low) in enumerate(left):
        size = high.shape[0]
        both = dot(jnp.concatenate([high, low], axis=0), matrix[0, index], transposed)
        products.append(both[:size] + both[size:] + dot(high, matrix[1, index], transposed))
    first, second, third = products
    if transposed:
        return jnp.concatenate([first + second, third - first + second], axis=1)
    return jnp.concatenate([first - second, third - first - second], axis=1)


def times(block, matrix, transposed=False):
    return times_split([split(part) for part in parts_of(block)], matrix, transposed)


def row_form(pair):
    return jnp.concatenate([pair[0], pair[1]], axis=1)


def adjoint_row(pair):
    return jnp.concatenate([jnp.transpose(pair[0]), -jnp.transpose(pair[1])], axis=1)


def expand(pattern, size):
    blocks = pattern.shape[0]
    tile = size // blocks
    rows = lax.broadcasted_iota(jnp.int32, (size, blocks), 0)
    first = lax.broadcasted_iota(jnp.int32, (size, blocks), 1) * tile
    member = jnp.where((rows >= first) & (rows < first + tile), 1.0, 0.0).astype(HALF)
    tall = dot(member, pattern.astype(F32).astype(HALF), False)
    return dot(tall.astype(HALF), member, True)


def couple(coupling, pattern):
    mask = expand(pattern[...], coupling.shape[-1])
    return jnp.concatenate([coupling[0] * mask, coupling[1] * mask], axis=1)


def trailing():
    return lax.rem(lax.axis_index("energy") + LEADING, 2)


def shape(rows, columns, dtype=F32, *lead):
    return jax.ShapeDtypeStruct(lead + (rows, columns), dtype)


def matrices(number, size):
    return [pltpu.VMEM((2, 3, size, size), HALF)] * number


def call(kernel, outs, scratch, args, specs=None, flops=0, name=None, limit=40):
    made = pl.pallas_call(
        kernel,
        out_shape=outs,
        in_specs=specs or [VMEM] * len(args),
        out_specs=[VMEM] * len(outs),
        scratch_shapes=scratch,
        compiler_params=pltpu.CompilerParams(vmem_limit_bytes=int(limit * 2**20)),
        cost_estimate=pl.CostEstimate(flops=flops, bytes_accessed=2**20, transcendentals=0),
        name=name,
    )(*args)
    return list(made)


class Loads:
    def __init__(self, args, targets, sems, couplers=(0, 1), blocks=True):
        order = [(0, 0), (1, 0), (3, 1), (2, 1), (1, 1), (0, 1), (3, 0), (2, 0)]
        self.copies = {
            (which, slab): pltpu.make_async_copy(
                args[which].at[slab], targets[which].at[slab], sems.at[index]
            )
            for index, (which, slab) in enumerate(order)
            if (blocks if which < 2 else slab in couplers)
        }
        self.targets = targets
        for copy in self.copies.values():
            copy.start()

    def get(self, which, slab):
        self.copies[which, slab].wait()
        return self.targets[which].at[slab]

    def green(self, slab):
        return row_form(self.get(0, slab))

    def sigma(self, slab):
        return row_form(self.get(1, slab))

    def coupler(self, slab):
        tiles = self.get(3, slab)
        return couple(self.get(2, slab), tiles)


def load_scratch(size, blocks):
    return [
        pltpu.VMEM((2, 2, size, size), F32),
        pltpu.VMEM((2, 2, size, size), F32),
        pltpu.VMEM((2, 2, size, size), F32),
        pltpu.VMEM((2, blocks, blocks), jnp.int32),
        pltpu.SemaphoreType.DMA((8,)),
    ]


def left_sources(loads, whole, source, coupler_out, m_a, m_b, m_c):
    first = loads.green(0)
    put(m_b, first)
    put(m_a, loads.sigma(0))
    made = first + times(times(first, m_a), m_b)
    if source is not None:
        source[...] = made
    put(m_a, made)
    coupler = loads.coupler(1)
    if coupler_out is not None:
        coupler_out[...] = coupler
    put(m_c, coupler, True)
    inner = loads.sigma(1) + times(times(coupler, m_a), m_c, True)
    put(m_a, inner)
    second = loads.green(1)
    put(m_b, second)
    whole[...] = second + times(times(second, m_a), m_b)
    return first, second


def source_kernel(green, sigma, coupling, pattern, whole, gate, *scratch):
    @pl.when(lax.axis_index("slab") == 0)
    def _():
        loads = Loads((green, sigma, coupling, pattern), scratch[:4], scratch[4], (1,))
        left_sources(loads, whole, None, None, *scratch[5:])

    @pl.when((lax.axis_index("slab") > 0) & (trailing() == 1))
    def _():
        loads = Loads((green, sigma, coupling, pattern), scratch[:4], scratch[4], (0,), False)
        gate[...] = loads.coupler(0)[: gate.shape[0]]


def map_kernel(
    green, sigma, coupling, pattern,
    whole, source, coupler, upper, lower, lead, tail, forward, backward, *scratch,
):
    m_a, m_b, m_c = scratch[5:]
    loads = Loads((green, sigma, coupling, pattern), scratch[:4], scratch[4])
    first, second = left_sources(loads, whole, source, coupler, m_a, m_b, m_c)
    before = loads.coupler(0)

    @pl.when(lax.axis_index("slab") > 0)
    def _():
        upper[...] = before[: upper.shape[0]]
        lower[...] = before[upper.shape[0] :]
        put(m_a, first)
        size = before.shape[0]
        behind = times(adjoint_row((before[:, :size], before[:, size:])), m_a)
        backward[...] = behind
        put(tail, times(times(behind, m_c, True), m_b))
        put(m_a, before)
        ahead = times(first, m_a)
        forward[...] = ahead
        put(m_a, ahead)
        put(m_c, coupler[...])
        put(lead, times(times(second, m_c), m_a))


def right_terms(first, last, coupler, m_coupler, m_first, m_last, m_upper):
    put(m_coupler, coupler, True)
    put(m_last, last)
    through = times(times(first, m_coupler, True), m_last)
    put(m_first, first)
    put(m_upper, times(coupler, m_first))
    return through, first + times(through, m_upper)


def prepare_kernel(count, *refs):
    arrived, wholes = refs[: count - 1], refs[count - 1 : 2 * count - 2]
    refs = refs[2 * count - 2 :]
    start_whole, source, forward, backward, coupler = refs[:5]
    gate, upper, lower = refs[5:8]
    lead, tail, constant, last_lead, last_tail = refs[9:14]
    first_v, last_v, m_a, m_b, m_c, m_d = refs[14:]
    place = lax.axis_index("slab")

    @pl.when(place == 0)
    def _():
        first_v[...] = source[...]
        last_v[...] = start_whole[...]

    for turn in range(count - 1):
        @pl.when((place > 0) & (place == turn + 1 - trailing()))
        def _(turn=turn):
            last_v[...] = wholes[turn][...]
            put(m_a, arrived[turn][...])

    @pl.when((place > 0) & (place < count - 1))
    def _():
        put(m_b, backward[...])
        first_v[...] = source[...] + times(times(forward[...], m_a), m_b)

    @pl.when(place < count - 1)
    def _():
        first, last = first_v[...], last_v[...]
        through, joined = right_terms(first, last, coupler[...], m_a, m_b, m_c, m_d)
        constant[...] = joined
        above = jnp.where(trailing() == 0, upper[...], gate[...])
        next_coupler = jnp.concatenate([above, lower[...]], axis=0)
        put(m_a, next_coupler, True)
        put(lead, times(through, m_a, True))
        put(last_lead, times(last, m_a, True))
        behind = times(next_coupler, m_c)
        put(last_tail, behind)
        put(tail, times(behind, m_d))


def apply_map(mapping, m_x):
    lead, tail, constant = mapping
    ahead = [(lead[0, index], lead[1, index]) for index in range(3)]
    return constant[...] + times(times_split(ahead, m_x), tail)


def relay_kernel(step, count, lefts, rights, *refs):
    refs = list(refs)
    place = lax.axis_index("slab")
    turn = step - trailing()
    is_left = (turn >= 0) & (turn <= count - 2) & (place == turn + 1)
    is_right = (turn >= count - 1) & (place == 2 * count - 3 - turn)
    closing = lefts and step >= count - 2
    arrived = refs.pop(0)
    left_map = [refs.pop(0) for _ in range(3)] if lefts else None
    right_map = [refs.pop(0) for _ in range(3)] if rights else None
    if closing:
        forward, backward, source, coupler = [refs.pop(0) for _ in range(4)]
    if step == 0:
        refs.pop(0)
    out = refs.pop(0)
    if closing:
        end, m_x, m_a, m_b, m_c = refs
    else:
        (m_x,) = refs

    if step == 0:
        @pl.when(place == 0)
        def _():
            out[...] = left_map[2][...]

    if lefts:
        @pl.when(is_left)
        def _():
            put(m_x, arrived[...])
            out[...] = apply_map(left_map, m_x)

    if closing:
        @pl.when(is_left & (place == count - 1))
        def _():
            last = out[...]
            end[...] = last
            put(m_a, backward[...])
            first = source[...] + times(times(forward[...], m_x), m_a)
            _, joined = right_terms(first, last, coupler[...], m_a, m_b, m_c, m_x)
            out[...] = joined

    if rights:
        @pl.when(is_right & (place > 0))
        def _():
            put(m_x, arrived[...])
            out[...] = apply_map(right_map, m_x)


def last_kernel(count, *refs):
    refs = list(refs)
    arrived = [refs.pop(0) for _ in range(count)]
    ends = [refs.pop(0) for _ in range(2)]
    last_lead, last_tail, whole_start = [refs.pop(0) for _ in range(3)]
    wholes = [refs.pop(0) for _ in range(count - 1)]
    block, *parcels, m_x = refs
    place = lax.axis_index("slab")
    core = trailing()
    is_last = place == count - 1

    for index in range(count):
        @pl.when(jnp.logical_not(is_last) & (2 * count - 3 - place + core == count - 1 + index))
        def _(index=index):
            put(m_x, arrived[index][...])

    for index in range(2):
        @pl.when(is_last & (core == index))
        def _(index=index):
            block[...] = ends[index][...]

    @pl.when(place == 0)
    def _():
        block[...] = apply_map((last_lead, last_tail, whole_start), m_x)

    for index in range(count - 1):
        @pl.when((place > 0) & jnp.logical_not(is_last) & (place - 1 + core == index))
        def _(index=index):
            block[...] = apply_map((last_lead, last_tail, wholes[index]), m_x)

    pack(block, parcels)


def first_kernel(count, *refs):
    arrived, outs = refs[:2], refs[2 : count + 2]
    right_map = refs[count + 2 : count + 5]
    block, *parcels, m_x = refs[count + 6 :]
    place, core = lax.axis_index("slab"), trailing()
    at = jnp.where(place == count - 1, count - 2 + core, 2 * count - 3 - place + core)

    for index in range(count):
        @pl.when((place > 0) & (at == count - 2 + index))
        def _(index=index):
            block[...] = outs[index][...]

    for index in range(2):
        @pl.when((place == 0) & (core == index))
        def _(index=index):
            put(m_x, arrived[index][...])

    @pl.when(place == 0)
    def _():
        block[...] = apply_map(right_map, m_x)

    pack(block, parcels)


def pack(block, parcels):
    for mask, parcel in enumerate(parcels):
        parcel[...] = block[share(mask, parcel.shape[0]), :]


def unpack_kernel(*refs):
    blocks, out = refs[:2], refs[2]
    size = out.shape[-1]
    for slab, block in enumerate(blocks):
        for part in range(2):
            out[slab, part] = block[:, part * size : (part + 1) * size]


def share(mask, rows):
    chip = lax.shift_right_logical(lax.axis_index("energy"), 1)
    return pl.ds(pl.multiple_of(lax.bitwise_xor(chip, mask) * rows, rows), rows)


def far_first(chips):
    return sorted(range(chips), key=lambda mask: -bin(mask).count("1"))


def weight_kernel(chips, weights, tiles):
    energy = lax.axis_index("energy")
    core = lax.rem(energy, 2)
    sources = [lax.bitwise_xor(energy, 2 * mask) for mask in range(chips)]
    for mask in range(chips):
        for side, target in enumerate((sources[mask], sources[mask] + 1 - 2 * core)):
            for index in range(chips):
                weight = weights[target, sources[index]]
                tiles[side, mask, index] = jnp.full(tiles.shape[3:], weight, F32)


def mix_kernel(chips, tiles, *refs):
    parcels, outs = dict(zip(far_first(chips), refs[:chips])), refs[chips:]
    rows, columns = parcels[0].shape
    step, width = tiles.shape[3:]
    for row in range(0, rows, step):
        where = slice(row, row + step)
        values = [parcels[mask][where] for mask in range(chips)]
        for side, out in enumerate(outs):
            for mask in range(chips):
                total = None
                for index in range(chips):
                    weight = jnp.concatenate([tiles[side, mask, index]] * (columns // width), axis=1)
                    term = weight * values[index]
                    total = term if total is None else total + term
                out[mask, where] = total


def sum_kernel(chips, mine, other, *outs):
    for mask in range(chips):
        outs[mask][...] = mine[mask] + other[mask]


def place_kernel(chips, *refs):
    scattering = refs[2 * chips]
    size = scattering.shape[-1]
    for slab in range(2):
        parcels = refs[slab * chips : (slab + 1) * chips]
        for mask, parcel in zip(far_first(chips), parcels):
            where = share(mask, parcel.shape[0])
            for part in range(2):
                scattering[slab, part, where, :] = parcel[:, part * size : (part + 1) * size]


def mode_weights(targets, sources, offsets, emission, absorption):
    spacing = sources[None, :, None] - targets[:, None, None]
    emitted = jnp.where(
        spacing == -offsets[None, None, :],
        emission[None, None, :],
        jnp.zeros_like(emission)[None, None, :],
    )
    absorbed = jnp.where(
        spacing == offsets[None, None, :],
        absorption[None, None, :],
        jnp.zeros_like(absorption)[None, None, :],
    )
    return jnp.sum(emitted + absorbed, axis=-1)


def relay_pairs(step, energies, count):
    pairs = []
    for energy in range(energies):
        turn = step - (energy + LEADING) % 2
        if 0 <= turn <= count - 2:
            ends = (turn, turn + 1)
        elif count - 1 <= turn <= 2 * count - 3:
            ends = (2 * count - 2 - turn, 2 * count - 3 - turn)
        else:
            continue
        pairs.append(tuple(energy * count + end for end in ends))
    return pairs


def shards(energies, count, free_green, self_energy, coupling, pattern, offsets, emission, absorption):
    size, blocks = free_green.shape[-1], pattern.shape[-1]
    args = (free_green[0], self_energy[0], coupling, pattern)
    row = shape(size, 2 * size)
    half = shape(size // 2, 2 * size)
    factor = shape(size, size, HALF, 2, 3)
    row_v = pltpu.VMEM(row.shape, F32)
    product = 24 * size**3
    loading = load_scratch(size, blocks) + matrices(3, size)

    def relay(step, value):
        return lax.ppermute(value, ("energy", "slab"), relay_pairs(step, energies, count))

    def lower_place(value, cores):
        pairs = [
            (energy * count + i, energy * count + i - 1)
            for energy in range(energies)
            for i in range(1, count)
            if (energy + LEADING) % 2 in cores
        ]
        return lax.ppermute(value, ("energy", "slab"), pairs)

    begun = call(
        source_kernel,
        [row, half],
        loading,
        args,
        [HBM] * 4,
        flops=6 * product,
        name="source",
        limit=53,
    )
    arrived, outs, ends = [relay(0, begun[0])], [], []
    gate = lower_place(begun[1], [1])
    whole, source, coupler, upper, lower, left_lead, left_tail, forward, backward = call(
        map_kernel,
        [row] * 3 + [half] * 2 + [factor, factor, row, row],
        loading,
        args,
        [HBM] * 4,
        flops=12 * product,
        name="left_maps",
        limit=48.6,
    )
    left_map = [left_lead, left_tail, whole]
    chips = energies // 2
    everyone = jnp.arange(energies, dtype=jnp.int32)
    weights = mode_weights(everyone, everyone, offsets, emission, absorption)
    (tiles,) = call(
        functools.partial(weight_kernel, chips),
        [shape(8, 128, F32, 2, chips, chips)],
        [],
        [weights],
        [SMEM],
        name="weights",
    )
    right_map = None
    for step in range(2 * count - 2):
        lefts, rights = step <= count - 1, step >= count - 1
        closing = lefts and step >= count - 2
        args = [arrived[step]]
        if lefts:
            args += left_map
        if rights:
            args += right_map[:3]
        if closing:
            args += [forward, backward, source, coupler]
        if step == 0:
            args.append(gate)
        made = call(
            functools.partial(relay_kernel, step, count, lefts, rights),
            [row] * (2 if closing else 1),
            matrices(4 if closing else 1, size),
            args,
            flops=2 * product,
            name="relay",
        )
        outs.append(made[0])
        ends += made[1:]
        arrived.append(relay(step + 1, made[0]))
        if step == 0:
            lower = lower_place(lower, [0, 1])
            upper = lower_place(upper, [0])
        if step == count - 2:
            args = arrived[: count - 1] + outs[: count - 1]
            args += [whole, source, forward, backward, coupler, gate, upper, lower, tiles]
            right_map = call(
                functools.partial(prepare_kernel, count),
                [factor, factor, row, factor, factor],
                [row_v] * 2 + matrices(4, size),
                args,
                flops=10 * product,
                name="right_maps",
            )
    parcel = shape(size // chips, 2 * size)
    blocks, parcels = [None, None], [None, None]
    args = arrived[count - 1 :] + ends + right_map[3:] + [whole] + outs[: count - 1]
    blocks[1], *parcels[1] = call(
        functools.partial(last_kernel, count),
        [row] + [parcel] * chips,
        matrices(1, size),
        args,
        flops=2 * product,
        name="second_slab",
    )
    args = arrived[-2:] + outs[count - 2 :] + right_map[:3] + blocks[1:]
    blocks[0], *parcels[0] = call(
        functools.partial(first_kernel, count),
        [row] + [parcel] * chips,
        matrices(1, size),
        args,
        flops=2 * product,
        name="first_slab",
    )
    (retarded,) = call(
        unpack_kernel, [shape(size, size, F32, 2, 2)], [], blocks, name="retarded"
    )

    masks = far_first(chips)

    def exchange(values):
        sent = list(values)
        for mask in masks[:-1]:
            pairs = [(i, i ^ (2 * mask)) for i in range(energies)]
            sent[mask] = lax.ppermute(values[mask], "energy", pairs)
        return [sent[mask] for mask in masks]

    partial = shape(size // chips, 2 * size, F32, chips)
    sums = [None, None]
    for slab in (1, 0):
        mine, other = call(
            functools.partial(mix_kernel, chips),
            [partial] * 2,
            [],
            [tiles] + exchange(parcels[slab]),
            flops=product // 8,
            name="mix",
        )
        other = lax.ppermute(other, "energy", [(i, i ^ 1) for i in range(energies)])
        sums[slab] = call(
            functools.partial(sum_kernel, chips), [parcel] * chips, [], [mine, other], name="sum"
        )
    returned = [exchange(sums[slab]) for slab in (1, 0)][::-1]
    (scattering,) = call(
        functools.partial(place_kernel, chips),
        [shape(size, size, F32, 2, 2)],
        [],
        returned[0] + returned[1],
        name="scattering",
    )
    return (retarded[None], scattering[None])


def solution(mesh):
    blocks = P("energy", "slab", None, None, None)
    in_specs = (blocks, blocks, P("slab", None, None, None), P("slab", None, None), P(), P(), P())
    body = functools.partial(shards, mesh.shape["energy"], mesh.shape["slab"])
    return jax.shard_map(
        body, mesh=mesh, in_specs=in_specs, out_specs=(blocks, blocks), check_vma=False
    )
```

```python
import functools

import jax
import jax.numpy as jnp
from jax import lax
from jax.experimental import pallas as pl
from jax.experimental.pallas import tpu as pltpu
from jax.sharding import PartitionSpec as P

F32 = jnp.float32
HALF = jnp.bfloat16
HBM = pl.BlockSpec(memory_space=pltpu.HBM)
VMEM = pl.BlockSpec(memory_space=pltpu.VMEM)
SMEM = pl.BlockSpec(memory_space=pltpu.SMEM)
LEADING = 0


def split(value):
    high = value.astype(HALF)
    return high, (value - high.astype(F32)).astype(HALF)


def dot(left, right, transposed):
    dims = (((1,), (1 if transposed else 0,)), ((), ()))
    return lax.dot_general(left, right, dims, preferred_element_type=F32)


def parts_of(block, adjoint=False):
    size = block.shape[0]
    real, imag = block[:, :size], block[:, size:]
    return real, imag, (real - imag if adjoint else real + imag)


def put(matrix, block, adjoint=False):
    for index, part in enumerate(parts_of(block, adjoint)):
        matrix[0, index], matrix[1, index] = split(part)


def put_left(matrix, block):
    size = block.shape[0]
    for index, part in enumerate(parts_of(block)):
        matrix[index, :size], matrix[index, size:] = split(part)


def times_split(left, matrix, transposed=False):
    products = []
    for index, stacked in enumerate(left):
        size = stacked.shape[0] // 2
        both = dot(stacked, matrix[0, index], transposed)
        high = stacked[:size]
        products.append(both[:size] + both[size:] + dot(high, matrix[1, index], transposed))
    first, second, third = products
    if transposed:
        return jnp.concatenate([first + second, third - first + second], axis=1)
    return jnp.concatenate([first - second, third - first - second], axis=1)


def times(block, matrix, transposed=False):
    left = [jnp.concatenate(split(part), axis=0) for part in parts_of(block)]
    return times_split(left, matrix, transposed)


def row_form(pair):
    return jnp.concatenate([pair[0], pair[1]], axis=1)


def adjoint_row(pair):
    return jnp.concatenate([jnp.transpose(pair[0]), -jnp.transpose(pair[1])], axis=1)


def expand(pattern, size):
    blocks = pattern.shape[0]
    tile = size // blocks
    rows = lax.broadcasted_iota(jnp.int32, (size, blocks), 0)
    first = lax.broadcasted_iota(jnp.int32, (size, blocks), 1) * tile
    member = jnp.where((rows >= first) & (rows < first + tile), 1.0, 0.0).astype(HALF)
    tall = dot(member, pattern.astype(F32).astype(HALF), False)
    return dot(tall.astype(HALF), member, True)


def couple(coupling, pattern):
    mask = expand(pattern[...], coupling.shape[-1])
    return jnp.concatenate([coupling[0] * mask, coupling[1] * mask], axis=1)


def trailing():
    return lax.rem(lax.axis_index("energy") + LEADING, 2)


def shape(rows, columns, dtype=F32, *lead):
    return jax.ShapeDtypeStruct(lead + (rows, columns), dtype)


def matrices(number, size):
    return [pltpu.VMEM((2, 3, size, size), HALF)] * number


def call(kernel, outs, scratch, args, specs=None, flops=0, name=None, limit=40):
    made = pl.pallas_call(
        kernel,
        out_shape=outs,
        in_specs=specs or [VMEM] * len(args),
        out_specs=[VMEM] * len(outs),
        scratch_shapes=scratch,
        compiler_params=pltpu.CompilerParams(vmem_limit_bytes=int(limit * 2**20)),
        cost_estimate=pl.CostEstimate(flops=flops, bytes_accessed=2**20, transcendentals=0),
        name=name,
    )(*args)
    return list(made)


class Loads:
    def __init__(self, args, targets, sems, couplers=(0, 1), blocks=True):
        order = [(0, 0), (1, 0), (3, 1), (2, 1), (1, 1), (0, 1), (3, 0), (2, 0)]
        self.copies = {
            (which, slab): pltpu.make_async_copy(
                args[which].at[slab], targets[which].at[slab], sems.at[index]
            )
            for index, (which, slab) in enumerate(order)
            if (blocks if which < 2 else slab in couplers)
        }
        self.targets = targets
        for copy in self.copies.values():
            copy.start()

    def get(self, which, slab):
        self.copies[which, slab].wait()
        return self.targets[which].at[slab]

    def green(self, slab):
        return row_form(self.get(0, slab))

    def sigma(self, slab):
        return row_form(self.get(1, slab))

    def coupler(self, slab):
        tiles = self.get(3, slab)
        return couple(self.get(2, slab), tiles)


def load_scratch(size, blocks):
    return [
        pltpu.VMEM((2, 2, size, size), F32),
        pltpu.VMEM((2, 2, size, size), F32),
        pltpu.VMEM((2, 2, size, size), F32),
        pltpu.VMEM((2, blocks, blocks), jnp.int32),
        pltpu.SemaphoreType.DMA((8,)),
    ]


def left_sources(loads, whole, source, coupler_out, m_a, m_b, m_c):
    first = loads.green(0)
    put(m_b, first)
    put(m_a, loads.sigma(0))
    made = first + times(times(first, m_a), m_b)
    if source is not None:
        source[...] = made
    put(m_a, made)
    coupler = loads.coupler(1)
    if coupler_out is not None:
        coupler_out[...] = coupler
    put(m_c, coupler, True)
    inner = loads.sigma(1) + times(times(coupler, m_a), m_c, True)
    put(m_a, inner)
    second = loads.green(1)
    put(m_b, second)
    whole[...] = second + times(times(second, m_a), m_b)
    return first, second


def source_kernel(green, sigma, coupling, pattern, whole, *scratch):
    @pl.when(lax.axis_index("slab") == 0)
    def _():
        loads = Loads((green, sigma, coupling, pattern), scratch[:4], scratch[4], (1,))
        left_sources(loads, whole, None, None, *scratch[5:])

    @pl.when((lax.axis_index("slab") > 0) & (trailing() == 1))
    def _():
        loads = Loads((green, sigma, coupling, pattern), scratch[:4], scratch[4], (0,), False)
        whole[...] = loads.coupler(0)


def map_kernel(
    green, sigma, coupling, pattern,
    whole, source, coupler, opening, lead, tail, forward, backward, *scratch,
):
    m_a, m_b, m_c = scratch[5:]
    loads = Loads((green, sigma, coupling, pattern), scratch[:4], scratch[4])
    first, second = left_sources(loads, whole, source, coupler, m_a, m_b, m_c)
    before = loads.coupler(0)

    @pl.when(lax.axis_index("slab") > 0)
    def _():
        opening[...] = before
        put(m_a, first)
        size = before.shape[0]
        behind = times(adjoint_row((before[:, :size], before[:, size:])), m_a)
        backward[...] = behind
        put(tail, times(times(behind, m_c, True), m_b))
        put(m_a, before)
        ahead = times(first, m_a)
        forward[...] = ahead
        put(m_a, ahead)
        put(m_c, coupler[...])
        put_left(lead, times(times(second, m_c), m_a))


def right_terms(first, last, coupler, m_coupler, m_first, m_last, m_upper):
    put(m_coupler, coupler, True)
    put(m_last, last)
    through = times(times(first, m_coupler, True), m_last)
    put(m_first, first)
    put(m_upper, times(coupler, m_first))
    return through, first + times(through, m_upper)


def prepare_kernel(count, *refs):
    arrived, wholes = refs[: count - 1], refs[count - 1 : 2 * count - 2]
    refs = refs[2 * count - 2 :]
    start_whole, source, forward, backward, coupler = refs[:5]
    followings = refs[5:7]
    lead, tail, constant, last_lead, last_tail = refs[8:13]
    first_v, last_v, m_a, m_b, m_c, m_d = refs[13:]
    place = lax.axis_index("slab")

    @pl.when(place == 0)
    def _():
        first_v[...] = source[...]
        last_v[...] = start_whole[...]

    for turn in range(count - 1):
        @pl.when((place > 0) & (place == turn + 1 - trailing()))
        def _(turn=turn):
            last_v[...] = wholes[turn][...]
            put(m_a, arrived[turn][...])

    @pl.when((place > 0) & (place < count - 1))
    def _():
        put(m_b, backward[...])
        first_v[...] = source[...] + times(times(forward[...], m_a), m_b)

    @pl.when(place < count - 1)
    def _():
        first, last = first_v[...], last_v[...]
        through, joined = right_terms(first, last, coupler[...], m_a, m_b, m_c, m_d)
        constant[...] = joined
        next_coupler = jnp.where(trailing() == 0, followings[0][...], followings[1][...])
        put(m_a, next_coupler, True)
        put_left(lead, times(through, m_a, True))
        put_left(last_lead, times(last, m_a, True))
        behind = times(next_coupler, m_c)
        put(last_tail, behind)
        put(tail, times(behind, m_d))


def apply_map(mapping, m_x):
    lead, tail, constant = mapping
    ahead = [lead[index] for index in range(3)]
    return constant[...] + times(times_split(ahead, m_x), tail)


def relay_kernel(step, count, lefts, rights, *refs):
    refs = list(refs)
    place = lax.axis_index("slab")
    turn = step - trailing()
    is_left = (turn >= 0) & (turn <= count - 2) & (place == turn + 1)
    is_right = (turn >= count - 1) & (place == 2 * count - 3 - turn)
    closing = lefts and step >= count - 2
    arrived = refs.pop(0)
    left_map = [refs.pop(0) for _ in range(3)] if lefts else None
    right_map = [refs.pop(0) for _ in range(3)] if rights else None
    if closing:
        forward, backward, source, coupler = [refs.pop(0) for _ in range(4)]
    out = refs.pop(0)
    if closing:
        end, m_x, m_a, m_b, m_c = refs
    else:
        (m_x,) = refs

    if step == 0:
        @pl.when(place == 0)
        def _():
            out[...] = left_map[2][...]

    if lefts:
        @pl.when(is_left)
        def _():
            put(m_x, arrived[...])
            out[...] = apply_map(left_map, m_x)

    if closing:
        @pl.when(is_left & (place == count - 1))
        def _():
            last = out[...]
            end[...] = last
            put(m_a, backward[...])
            first = source[...] + times(times(forward[...], m_x), m_a)
            _, joined = right_terms(first, last, coupler[...], m_a, m_b, m_c, m_x)
            out[...] = joined

    if rights:
        @pl.when(is_right & (place > 0))
        def _():
            put(m_x, arrived[...])
            out[...] = apply_map(right_map, m_x)


def last_kernel(count, *refs):
    refs = list(refs)
    arrived = [refs.pop(0) for _ in range(count)]
    ends = [refs.pop(0) for _ in range(2)]
    last_lead, last_tail, whole_start = [refs.pop(0) for _ in range(3)]
    wholes = [refs.pop(0) for _ in range(count - 1)]
    block, *parcels, m_x = refs
    place = lax.axis_index("slab")
    core = trailing()
    is_last = place == count - 1

    for index in range(count):
        @pl.when(jnp.logical_not(is_last) & (2 * count - 3 - place + core == count - 1 + index))
        def _(index=index):
            put(m_x, arrived[index][...])

    for index in range(2):
        @pl.when(is_last & (core == index))
        def _(index=index):
            block[...] = ends[index][...]

    @pl.when(place == 0)
    def _():
        block[...] = apply_map((last_lead, last_tail, whole_start), m_x)

    for index in range(count - 1):
        @pl.when((place > 0) & jnp.logical_not(is_last) & (place - 1 + core == index))
        def _(index=index):
            block[...] = apply_map((last_lead, last_tail, wholes[index]), m_x)

    pack(block, parcels)


def first_kernel(count, *refs):
    arrived, outs = refs[:2], refs[2 : count + 2]
    right_map = refs[count + 2 : count + 5]
    block, *parcels, m_x = refs[count + 6 :]
    place, core = lax.axis_index("slab"), trailing()
    at = jnp.where(place == count - 1, count - 2 + core, 2 * count - 3 - place + core)

    for index in range(count):
        @pl.when((place > 0) & (at == count - 2 + index))
        def _(index=index):
            block[...] = outs[index][...]

    for index in range(2):
        @pl.when((place == 0) & (core == index))
        def _(index=index):
            put(m_x, arrived[index][...])

    @pl.when(place == 0)
    def _():
        block[...] = apply_map(right_map, m_x)

    pack(block, parcels)


def pack(block, parcels):
    for mask, parcel in enumerate(parcels):
        parcel[...] = block[share(mask, parcel.shape[0]), :]


def unpack_kernel(*refs):
    blocks, out = refs[:2], refs[2]
    size = out.shape[-1]
    for slab, block in enumerate(blocks):
        for part in range(2):
            out[slab, part] = block[:, part * size : (part + 1) * size]


def share(mask, rows):
    chip = lax.shift_right_logical(lax.axis_index("energy"), 1)
    return pl.ds(pl.multiple_of(lax.bitwise_xor(chip, mask) * rows, rows), rows)


def far_first(chips):
    return sorted(range(chips), key=lambda mask: -bin(mask).count("1"))


def weight_kernel(chips, weights, tiles):
    energy = lax.axis_index("energy")
    core = lax.rem(energy, 2)
    sources = [lax.bitwise_xor(energy, 2 * mask) for mask in range(chips)]
    for mask in range(chips):
        for side, target in enumerate((sources[mask], sources[mask] + 1 - 2 * core)):
            for index in range(chips):
                weight = weights[target, sources[index]]
                tiles[side, mask, index] = jnp.full(tiles.shape[3:], weight, F32)


def mix_kernel(chips, tiles, *refs):
    parcels, outs = dict(zip(far_first(chips), refs[:chips])), refs[chips:]
    rows, columns = parcels[0].shape
    step, width = tiles.shape[3:]
    for row in range(0, rows, step):
        where = slice(row, row + step)
        values = [parcels[mask][where] for mask in range(chips)]
        for side, out in enumerate(outs):
            for mask in range(chips):
                total = None
                for index in range(chips):
                    weight = jnp.concatenate([tiles[side, mask, index]] * (columns // width), axis=1)
                    term = weight * values[index]
                    total = term if total is None else total + term
                out[mask, where] = total


def sum_kernel(chips, mine, other, *outs):
    for mask in range(chips):
        outs[mask][...] = mine[mask] + other[mask]


def place_kernel(chips, *refs):
    scattering = refs[2 * chips]
    size = scattering.shape[-1]
    for slab in range(2):
        parcels = refs[slab * chips : (slab + 1) * chips]
        for mask, parcel in zip(far_first(chips), parcels):
            where = share(mask, parcel.shape[0])
            for part in range(2):
                scattering[slab, part, where, :] = parcel[:, part * size : (part + 1) * size]


def mode_weights(targets, sources, offsets, emission, absorption):
    spacing = sources[None, :, None] - targets[:, None, None]
    emitted = jnp.where(
        spacing == -offsets[None, None, :],
        emission[None, None, :],
        jnp.zeros_like(emission)[None, None, :],
    )
    absorbed = jnp.where(
        spacing == offsets[None, None, :],
        absorption[None, None, :],
        jnp.zeros_like(absorption)[None, None, :],
    )
    return jnp.sum(emitted + absorbed, axis=-1)


def relay_pairs(step, energies, count):
    pairs = []
    for energy in range(energies):
        turn = step - (energy + LEADING) % 2
        if turn < 0:
            pairs += [(energy * count + i, energy * count + i - 1) for i in range(1, count)]
        if 0 <= turn <= count - 2:
            ends = (turn, turn + 1)
        elif count - 1 <= turn <= 2 * count - 3:
            ends = (2 * count - 2 - turn, 2 * count - 3 - turn)
        else:
            continue
        pairs.append(tuple(energy * count + end for end in ends))
    return pairs


def shards(energies, count, free_green, self_energy, coupling, pattern, offsets, emission, absorption):
    size, blocks = free_green.shape[-1], pattern.shape[-1]
    args = (free_green[0], self_energy[0], coupling, pattern)
    row = shape(size, 2 * size)
    left_factor = shape(2 * size, size, HALF, 3)
    factor = shape(size, size, HALF, 2, 3)
    row_v = pltpu.VMEM(row.shape, F32)
    product = 24 * size**3
    loading = load_scratch(size, blocks) + matrices(3, size)

    def relay(step, value):
        return lax.ppermute(value, ("energy", "slab"), relay_pairs(step, energies, count))

    begun = call(
        source_kernel,
        [row],
        loading,
        args,
        [HBM] * 4,
        flops=6 * product,
        name="source",
        limit=53,
    )
    arrived, outs, ends = [relay(0, begun[0])], [], []
    whole, source, coupler, opening, left_lead, left_tail, forward, backward = call(
        map_kernel,
        [row] * 4 + [left_factor, factor, row, row],
        loading,
        args,
        [HBM] * 4,
        flops=12 * product,
        name="left_maps",
        limit=48.6,
    )
    left_map = [left_lead, left_tail, whole]
    chips = energies // 2
    everyone = jnp.arange(energies, dtype=jnp.int32)
    weights = mode_weights(everyone, everyone, offsets, emission, absorption)
    (tiles,) = call(
        functools.partial(weight_kernel, chips),
        [shape(8, 128, F32, 2, chips, chips)],
        [],
        [weights],
        [SMEM],
        name="weights",
    )
    right_map = None
    for step in range(2 * count - 2):
        lefts, rights = step <= count - 1, step >= count - 1
        closing = lefts and step >= count - 2
        args = [arrived[step]]
        if lefts:
            args += left_map
        if rights:
            args += right_map[:3]
        if closing:
            args += [forward, backward, source, coupler]
        made = call(
            functools.partial(relay_kernel, step, count, lefts, rights),
            [row] * (2 if closing else 1),
            matrices(4 if closing else 1, size),
            args,
            flops=2 * product,
            name="relay",
        )
        outs.append(made[0])
        ends += made[1:]
        arrived.append(relay(step + 1, made[0]))
        if step == 0:
            down = [
                (energy * count + i, energy * count + i - 1)
                for energy in range(energies)
                for i in range(1, count)
                if (energy + LEADING) % 2 == 0
            ]
            following = lax.ppermute(opening, ("energy", "slab"), down)
        if step == count - 2:
            args = arrived[: count - 1] + outs[: count - 1]
            args += [whole, source, forward, backward, coupler, following, arrived[0], tiles]
            right_map = call(
                functools.partial(prepare_kernel, count),
                [left_factor, factor, row, left_factor, factor],
                [row_v] * 2 + matrices(4, size),
                args,
                flops=10 * product,
                name="right_maps",
            )
    parcel = shape(size // chips, 2 * size)
    blocks, parcels = [None, None], [None, None]
    args = arrived[count - 1 :] + ends + right_map[3:] + [whole] + outs[: count - 1]
    blocks[1], *parcels[1] = call(
        functools.partial(last_kernel, count),
        [row] + [parcel] * chips,
        matrices(1, size),
        args,
        flops=2 * product,
        name="second_slab",
    )
    args = arrived[-2:] + outs[count - 2 :] + right_map[:3] + blocks[1:]
    blocks[0], *parcels[0] = call(
        functools.partial(first_kernel, count),
        [row] + [parcel] * chips,
        matrices(1, size),
        args,
        flops=2 * product,
        name="first_slab",
    )
    (retarded,) = call(
        unpack_kernel, [shape(size, size, F32, 2, 2)], [], blocks, name="retarded"
    )

    masks = far_first(chips)

    def exchange(values):
        sent = list(values)
        for mask in masks[:-1]:
            pairs = [(i, i ^ (2 * mask)) for i in range(energies)]
            sent[mask] = lax.ppermute(values[mask], "energy", pairs)
        return [sent[mask] for mask in masks]

    partial = shape(size // chips, 2 * size, F32, chips)
    sums = [None, None]
    for slab in (1, 0):
        mine, other = call(
            functools.partial(mix_kernel, chips),
            [partial] * 2,
            [],
            [tiles] + exchange(parcels[slab]),
            flops=product // 8,
            name="mix",
        )
        other = lax.ppermute(other, "energy", [(i, i ^ 1) for i in range(energies)])
        sums[slab] = call(
            functools.partial(sum_kernel, chips), [parcel] * chips, [], [mine, other], name="sum"
        )
    returned = [exchange(sums[slab]) for slab in (1, 0)][::-1]
    (scattering,) = call(
        functools.partial(place_kernel, chips),
        [shape(size, size, F32, 2, 2)],
        [],
        returned[0] + returned[1],
        name="scattering",
    )
    return (retarded[None], scattering[None])


def solution(mesh):
    blocks = P("energy", "slab", None, None, None)
    in_specs = (blocks, blocks, P("slab", None, None, None), P("slab", None, None), P(), P(), P())
    body = functools.partial(shards, mesh.shape["energy"], mesh.shape["slab"])
    return jax.shard_map(
        body, mesh=mesh, in_specs=in_specs, out_specs=(blocks, blocks), check_vma=False
    )
```

```python
import functools

import jax
import jax.numpy as jnp
from jax import lax
from jax.experimental import pallas as pl
from jax.experimental.pallas import tpu as pltpu
from jax.sharding import PartitionSpec as P

F32 = jnp.float32
HALF = jnp.bfloat16
HBM = pl.BlockSpec(memory_space=pltpu.HBM)
VMEM = pl.BlockSpec(memory_space=pltpu.VMEM)
SMEM = pl.BlockSpec(memory_space=pltpu.SMEM)
LEADING = 0


def split(value):
    high = value.astype(HALF)
    return high, (value - high.astype(F32)).astype(HALF)


def dot(left, right, transposed):
    dims = (((1,), (1 if transposed else 0,)), ((), ()))
    return lax.dot_general(left, right, dims, preferred_element_type=F32)


def parts_of(block, adjoint=False):
    size = block.shape[0]
    real, imag = block[:, :size], block[:, size:]
    return real, imag, (real - imag if adjoint else real + imag)


def put(matrix, block, adjoint=False):
    size = block.shape[0]
    for index, part in enumerate(parts_of(block, adjoint)):
        matrix[index, :size], matrix[index, size:] = split(part)


def times_split(left, matrix, transposed=False):
    products = []
    for index, stacked in enumerate(left):
        rows, size = stacked.shape[0] // 2, matrix.shape[1] // 2
        high, low = stacked[:rows], stacked[rows:]
        if transposed:
            both = dot(stacked, matrix[index, :size], True)
            both = both[:rows] + both[rows:] + dot(high, matrix[index, size:], True)
        else:
            both = dot(jnp.concatenate([high, high], axis=1), matrix[index], False)
            both += dot(low, matrix[index, :size], False)
        products.append(both)
    first, second, third = products
    if transposed:
        return jnp.concatenate([first + second, third - first + second], axis=1)
    return jnp.concatenate([first - second, third - first - second], axis=1)


def times(block, matrix, transposed=False):
    left = [jnp.concatenate(split(part), axis=0) for part in parts_of(block)]
    return times_split(left, matrix, transposed)


def row_form(pair):
    return jnp.concatenate([pair[0], pair[1]], axis=1)


def adjoint_row(pair):
    return jnp.concatenate([jnp.transpose(pair[0]), -jnp.transpose(pair[1])], axis=1)


def expand(pattern, size):
    blocks = pattern.shape[0]
    tile = size // blocks
    rows = lax.broadcasted_iota(jnp.int32, (size, blocks), 0)
    first = lax.broadcasted_iota(jnp.int32, (size, blocks), 1) * tile
    member = jnp.where((rows >= first) & (rows < first + tile), 1.0, 0.0).astype(HALF)
    tall = dot(member, pattern.astype(F32).astype(HALF), False)
    return dot(tall.astype(HALF), member, True)


def couple(coupling, pattern):
    mask = expand(pattern[...], coupling.shape[-1])
    return jnp.concatenate([coupling[0] * mask, coupling[1] * mask], axis=1)


def trailing():
    return lax.rem(lax.axis_index("energy") + LEADING, 2)


def shape(rows, columns, dtype=F32, *lead):
    return jax.ShapeDtypeStruct(lead + (rows, columns), dtype)


def matrices(number, size):
    return [pltpu.VMEM((3, 2 * size, size), HALF)] * number


def call(kernel, outs, scratch, args, specs=None, flops=0, name=None, limit=40):
    made = pl.pallas_call(
        kernel,
        out_shape=outs,
        in_specs=specs or [VMEM] * len(args),
        out_specs=[VMEM] * len(outs),
        scratch_shapes=scratch,
        compiler_params=pltpu.CompilerParams(vmem_limit_bytes=int(limit * 2**20)),
        cost_estimate=pl.CostEstimate(flops=flops, bytes_accessed=2**20, transcendentals=0),
        name=name,
    )(*args)
    return list(made)


class Loads:
    def __init__(self, args, targets, sems, couplers=(0, 1), blocks=True):
        order = [(0, 0), (1, 0), (3, 1), (2, 1), (1, 1), (0, 1), (3, 0), (2, 0)]
        self.copies = {
            (which, slab): pltpu.make_async_copy(
                args[which].at[slab], targets[which].at[slab], sems.at[index]
            )
            for index, (which, slab) in enumerate(order)
            if (blocks if which < 2 else slab in couplers)
        }
        self.targets = targets
        for copy in self.copies.values():
            copy.start()

    def get(self, which, slab):
        self.copies[which, slab].wait()
        return self.targets[which].at[slab]

    def green(self, slab):
        return row_form(self.get(0, slab))

    def sigma(self, slab):
        return row_form(self.get(1, slab))

    def coupler(self, slab):
        tiles = self.get(3, slab)
        return couple(self.get(2, slab), tiles)


def load_scratch(size, blocks):
    return [
        pltpu.VMEM((2, 2, size, size), F32),
        pltpu.VMEM((2, 2, size, size), F32),
        pltpu.VMEM((2, 2, size, size), F32),
        pltpu.VMEM((2, blocks, blocks), jnp.int32),
        pltpu.SemaphoreType.DMA((8,)),
    ]


def left_sources(loads, whole, source, coupler_out, m_a, m_b, m_c):
    first = loads.green(0)
    put(m_b, first)
    put(m_a, loads.sigma(0))
    made = first + times(times(first, m_a), m_b)
    if source is not None:
        source[...] = made
    put(m_a, made)
    coupler = loads.coupler(1)
    if coupler_out is not None:
        coupler_out[...] = coupler
    put(m_c, coupler, True)
    inner = loads.sigma(1) + times(times(coupler, m_a), m_c, True)
    put(m_a, inner)
    second = loads.green(1)
    put(m_b, second)
    whole[...] = second + times(times(second, m_a), m_b)
    return first, second


def source_kernel(green, sigma, coupling, pattern, whole, *scratch):
    @pl.when(lax.axis_index("slab") == 0)
    def _():
        loads = Loads((green, sigma, coupling, pattern), scratch[:4], scratch[4], (1,))
        left_sources(loads, whole, None, None, *scratch[5:])

    @pl.when((lax.axis_index("slab") > 0) & (trailing() == 1))
    def _():
        loads = Loads((green, sigma, coupling, pattern), scratch[:4], scratch[4], (0,), False)
        whole[...] = loads.coupler(0)


def map_kernel(
    green, sigma, coupling, pattern,
    whole, source, coupler, opening, lead, tail, forward, backward, *scratch,
):
    m_a, m_b, m_c = scratch[5:]
    loads = Loads((green, sigma, coupling, pattern), scratch[:4], scratch[4])
    first, second = left_sources(loads, whole, source, coupler, m_a, m_b, m_c)
    before = loads.coupler(0)

    @pl.when(lax.axis_index("slab") > 0)
    def _():
        opening[...] = before
        put(m_a, first)
        size = before.shape[0]
        behind = times(adjoint_row((before[:, :size], before[:, size:])), m_a)
        backward[...] = behind
        put(tail, times(times(behind, m_c, True), m_b))
        put(m_a, before)
        ahead = times(first, m_a)
        forward[...] = ahead
        put(m_a, ahead)
        put(m_c, coupler[...])
        put(lead, times(times(second, m_c), m_a))


def right_terms(first, last, coupler, m_coupler, m_first, m_last, m_upper):
    put(m_coupler, coupler, True)
    put(m_last, last)
    through = times(times(first, m_coupler, True), m_last)
    put(m_first, first)
    put(m_upper, times(coupler, m_first))
    return through, first + times(through, m_upper)


def prepare_kernel(count, *refs):
    arrived, wholes = refs[: count - 1], refs[count - 1 : 2 * count - 2]
    refs = refs[2 * count - 2 :]
    start_whole, source, forward, backward, coupler = refs[:5]
    followings = refs[5:7]
    lead, tail, constant, last_lead, last_tail = refs[8:13]
    first_v, last_v, m_a, m_b, m_c, m_d = refs[13:]
    place = lax.axis_index("slab")

    @pl.when(place == 0)
    def _():
        first_v[...] = source[...]
        last_v[...] = start_whole[...]

    for turn in range(count - 1):
        @pl.when((place > 0) & (place == turn + 1 - trailing()))
        def _(turn=turn):
            last_v[...] = wholes[turn][...]
            put(m_a, arrived[turn][...])

    @pl.when((place > 0) & (place < count - 1))
    def _():
        put(m_b, backward[...])
        first_v[...] = source[...] + times(times(forward[...], m_a), m_b)

    @pl.when(place < count - 1)
    def _():
        first, last = first_v[...], last_v[...]
        through, joined = right_terms(first, last, coupler[...], m_a, m_b, m_c, m_d)
        constant[...] = joined
        next_coupler = jnp.where(trailing() == 0, followings[0][...], followings[1][...])
        put(m_a, next_coupler, True)
        put(lead, times(through, m_a, True))
        put(last_lead, times(last, m_a, True))
        behind = times(next_coupler, m_c)
        put(last_tail, behind)
        put(tail, times(behind, m_d))


def apply_map(mapping, m_x):
    lead, tail, constant = mapping
    ahead = [lead[index] for index in range(3)]
    return constant[...] + times(times_split(ahead, m_x), tail)


def relay_kernel(step, count, lefts, rights, *refs):
    refs = list(refs)
    place = lax.axis_index("slab")
    turn = step - trailing()
    is_left = (turn >= 0) & (turn <= count - 2) & (place == turn + 1)
    is_right = (turn >= count - 1) & (place == 2 * count - 3 - turn)
    closing = lefts and step >= count - 2
    arrived = refs.pop(0)
    left_map = [refs.pop(0) for _ in range(3)] if lefts else None
    right_map = [refs.pop(0) for _ in range(3)] if rights else None
    if closing:
        forward, backward, source, coupler = [refs.pop(0) for _ in range(4)]
    out = refs.pop(0)
    if closing:
        end, m_x, m_a, m_b, m_c = refs
    else:
        (m_x,) = refs

    if step == 0:
        @pl.when(place == 0)
        def _():
            out[...] = left_map[2][...]

    if lefts:
        @pl.when(is_left & (place < count - 1) if closing else is_left)
        def _():
            put(m_x, arrived[...])
            out[...] = apply_map(left_map, m_x)

    if closing:
        @pl.when(is_left & (place == count - 1))
        def _():
            put(m_x, arrived[...])
            last = apply_map(left_map, m_x)
            end[...] = last
            put(m_a, backward[...])
            first = source[...] + times(times(forward[...], m_x), m_a)
            _, joined = right_terms(first, last, coupler[...], m_a, m_b, m_c, m_x)
            out[...] = joined

    if rights:
        @pl.when(is_right & (place > 0))
        def _():
            put(m_x, arrived[...])
            out[...] = apply_map(right_map, m_x)


def last_kernel(count, *refs):
    refs = list(refs)
    arrived = [refs.pop(0) for _ in range(count)]
    ends = [refs.pop(0) for _ in range(2)]
    last_lead, last_tail, whole_start = [refs.pop(0) for _ in range(3)]
    wholes = [refs.pop(0) for _ in range(count - 1)]
    block, *parcels, m_x = refs
    place = lax.axis_index("slab")
    core = trailing()
    is_last = place == count - 1

    for index in range(count):
        @pl.when(jnp.logical_not(is_last) & (2 * count - 3 - place + core == count - 1 + index))
        def _(index=index):
            put(m_x, arrived[index][...])

    for index in range(2):
        @pl.when(is_last & (core == index))
        def _(index=index):
            block[...] = ends[index][...]

    @pl.when(place == 0)
    def _():
        block[...] = apply_map((last_lead, last_tail, whole_start), m_x)

    for index in range(count - 1):
        @pl.when((place > 0) & jnp.logical_not(is_last) & (place - 1 + core == index))
        def _(index=index):
            block[...] = apply_map((last_lead, last_tail, wholes[index]), m_x)

    pack(block, parcels)


def first_kernel(count, *refs):
    arrived, outs = refs[:2], refs[2 : count + 2]
    right_map = refs[count + 2 : count + 5]
    block, *parcels, m_x = refs[count + 6 :]
    place, core = lax.axis_index("slab"), trailing()
    at = jnp.where(place == count - 1, count - 2 + core, 2 * count - 3 - place + core)

    for index in range(count):
        @pl.when((place > 0) & (at == count - 2 + index))
        def _(index=index):
            block[...] = outs[index][...]

    for index in range(2):
        @pl.when((place == 0) & (core == index))
        def _(index=index):
            put(m_x, arrived[index][...])

    @pl.when(place == 0)
    def _():
        block[...] = apply_map(right_map, m_x)

    pack(block, parcels)


def pack(block, parcels):
    for mask, parcel in enumerate(parcels):
        parcel[...] = block[share(mask, parcel.shape[0]), :]


def unpack_kernel(*refs):
    blocks, out = refs[:2], refs[2]
    size = out.shape[-1]
    for slab, block in enumerate(blocks):
        for part in range(2):
            out[slab, part] = block[:, part * size : (part + 1) * size]


def share(mask, rows):
    chip = lax.shift_right_logical(lax.axis_index("energy"), 1)
    return pl.ds(pl.multiple_of(lax.bitwise_xor(chip, mask) * rows, rows), rows)


def far_first(chips):
    return sorted(range(chips), key=lambda mask: -bin(mask).count("1"))


def weight_kernel(chips, weights, tiles):
    energy = lax.axis_index("energy")
    core = lax.rem(energy, 2)
    sources = [lax.bitwise_xor(energy, 2 * mask) for mask in range(chips)]
    for mask in range(chips):
        for side, target in enumerate((sources[mask], sources[mask] + 1 - 2 * core)):
            for index in range(chips):
                weight = weights[target, sources[index]]
                tiles[side, mask, index] = jnp.full(tiles.shape[3:], weight, F32)


def mix_kernel(chips, tiles, *refs):
    parcels, outs = dict(zip(far_first(chips), refs[:chips])), refs[chips:]
    rows, columns = parcels[0].shape
    step, width = tiles.shape[3:]
    for row in range(0, rows, step):
        where = slice(row, row + step)
        values = [parcels[mask][where] for mask in range(chips)]
        for side, out in enumerate(outs):
            for mask in range(chips):
                total = None
                for index in range(chips):
                    weight = jnp.concatenate([tiles[side, mask, index]] * (columns // width), axis=1)
                    term = weight * values[index]
                    total = term if total is None else total + term
                out[mask, where] = total


def sum_kernel(chips, mine, other, *outs):
    for mask in range(chips):
        outs[mask][...] = mine[mask] + other[mask]


def place_kernel(chips, *refs):
    scattering = refs[2 * chips]
    size = scattering.shape[-1]
    for slab in range(2):
        parcels = refs[slab * chips : (slab + 1) * chips]
        for mask, parcel in zip(far_first(chips), parcels):
            where = share(mask, parcel.shape[0])
            for part in range(2):
                scattering[slab, part, where, :] = parcel[:, part * size : (part + 1) * size]


def mode_weights(targets, sources, offsets, emission, absorption):
    spacing = sources[None, :, None] - targets[:, None, None]
    emitted = jnp.where(
        spacing == -offsets[None, None, :],
        emission[None, None, :],
        jnp.zeros_like(emission)[None, None, :],
    )
    absorbed = jnp.where(
        spacing == offsets[None, None, :],
        absorption[None, None, :],
        jnp.zeros_like(absorption)[None, None, :],
    )
    return jnp.sum(emitted + absorbed, axis=-1)


def relay_pairs(step, energies, count):
    pairs = []
    for energy in range(energies):
        turn = step - (energy + LEADING) % 2
        if turn < 0:
            pairs += [(energy * count + i, energy * count + i - 1) for i in range(1, count)]
        if 0 <= turn <= count - 2:
            ends = (turn, turn + 1)
        elif count - 1 <= turn <= 2 * count - 3:
            ends = (2 * count - 2 - turn, 2 * count - 3 - turn)
        else:
            continue
        pairs.append(tuple(energy * count + end for end in ends))
    return pairs


def shards(energies, count, free_green, self_energy, coupling, pattern, offsets, emission, absorption):
    size, blocks = free_green.shape[-1], pattern.shape[-1]
    args = (free_green[0], self_energy[0], coupling, pattern)
    row = shape(size, 2 * size)
    factor = shape(2 * size, size, HALF, 3)
    row_v = pltpu.VMEM(row.shape, F32)
    product = 24 * size**3
    loading = load_scratch(size, blocks) + matrices(3, size)

    def relay(step, value):
        return lax.ppermute(value, ("energy", "slab"), relay_pairs(step, energies, count))

    begun = call(
        source_kernel,
        [row],
        loading,
        args,
        [HBM] * 4,
        flops=6 * product,
        name="source",
        limit=53,
    )
    arrived, outs, ends = [relay(0, begun[0])], [], []
    whole, source, coupler, opening, left_lead, left_tail, forward, backward = call(
        map_kernel,
        [row] * 4 + [factor, factor, row, row],
        loading,
        args,
        [HBM] * 4,
        flops=12 * product,
        name="left_maps",
        limit=48.6,
    )
    left_map = [left_lead, left_tail, whole]
    chips = energies // 2
    everyone = jnp.arange(energies, dtype=jnp.int32)
    weights = mode_weights(everyone, everyone, offsets, emission, absorption)
    (tiles,) = call(
        functools.partial(weight_kernel, chips),
        [shape(8, 128, F32, 2, chips, chips)],
        [],
        [weights],
        [SMEM],
        name="weights",
    )
    right_map = None
    for step in range(2 * count - 2):
        lefts, rights = step <= count - 1, step >= count - 1
        closing = lefts and step >= count - 2
        args = [arrived[step]]
        if lefts:
            args += left_map
        if rights:
            args += right_map[:3]
        if closing:
            args += [forward, backward, source, coupler]
        made = call(
            functools.partial(relay_kernel, step, count, lefts, rights),
            [row] * (2 if closing else 1),
            matrices(4 if closing else 1, size),
            args,
            flops=2 * product,
            name="relay",
        )
        outs.append(made[0])
        ends += made[1:]
        arrived.append(relay(step + 1, made[0]))
        if step == 0:
            down = [
                (energy * count + i, energy * count + i - 1)
                for energy in range(energies)
                for i in range(1, count)
                if (energy + LEADING) % 2 == 0
            ]
            following = lax.ppermute(opening, ("energy", "slab"), down)
        if step == count - 2:
            args = arrived[: count - 1] + outs[: count - 1]
            args += [whole, source, forward, backward, coupler, following, arrived[0], tiles]
            right_map = call(
                functools.partial(prepare_kernel, count),
                [factor, factor, row, factor, factor],
                [row_v] * 2 + matrices(4, size),
                args,
                flops=10 * product,
                name="right_maps",
            )
    parcel = shape(size // chips, 2 * size)
    blocks, parcels = [None, None], [None, None]
    args = arrived[count - 1 :] + ends + right_map[3:] + [whole] + outs[: count - 1]
    blocks[1], *parcels[1] = call(
        functools.partial(last_kernel, count),
        [row] + [parcel] * chips,
        matrices(1, size),
        args,
        flops=2 * product,
        name="second_slab",
    )
    args = arrived[-2:] + outs[count - 2 :] + right_map[:3] + blocks[1:]
    blocks[0], *parcels[0] = call(
        functools.partial(first_kernel, count),
        [row] + [parcel] * chips,
        matrices(1, size),
        args,
        flops=2 * product,
        name="first_slab",
    )
    (retarded,) = call(
        unpack_kernel, [shape(size, size, F32, 2, 2)], [], blocks, name="retarded"
    )

    masks = far_first(chips)

    def exchange(values):
        sent = list(values)
        for mask in masks[:-1]:
            pairs = [(i, i ^ (2 * mask)) for i in range(energies)]
            sent[mask] = lax.ppermute(values[mask], "energy", pairs)
        return [sent[mask] for mask in masks]

    partial = shape(size // chips, 2 * size, F32, chips)
    sums = [None, None]
    for slab in (1, 0):
        mine, other = call(
            functools.partial(mix_kernel, chips),
            [partial] * 2,
            [],
            [tiles] + exchange(parcels[slab]),
            flops=product // 8,
            name="mix",
        )
        other = lax.ppermute(other, "energy", [(i, i ^ 1) for i in range(energies)])
        sums[slab] = call(
            functools.partial(sum_kernel, chips), [parcel] * chips, [], [mine, other], name="sum"
        )
    returned = [exchange(sums[slab]) for slab in (1, 0)][::-1]
    (scattering,) = call(
        functools.partial(place_kernel, chips),
        [shape(size, size, F32, 2, 2)],
        [],
        returned[0] + returned[1],
        name="scattering",
    )
    return (retarded[None], scattering[None])


def solution(mesh):
    blocks = P("energy", "slab", None, None, None)
    in_specs = (blocks, blocks, P("slab", None, None, None), P("slab", None, None), P(), P(), P())
    body = functools.partial(shards, mesh.shape["energy"], mesh.shape["slab"])
    return jax.shard_map(
        body, mesh=mesh, in_specs=in_specs, out_specs=(blocks, blocks), check_vma=False
    )
```

```python
import functools

import jax
import jax.numpy as jnp
from jax import lax
from jax.experimental import pallas as pl
from jax.experimental.pallas import tpu as pltpu
from jax.sharding import PartitionSpec as P

F32 = jnp.float32
HALF = jnp.bfloat16
HBM = pl.BlockSpec(memory_space=pltpu.HBM)
VMEM = pl.BlockSpec(memory_space=pltpu.VMEM)
SMEM = pl.BlockSpec(memory_space=pltpu.SMEM)
LEADING = 0


def split(value):
    high = value.astype(HALF)
    return high, (value - high.astype(F32)).astype(HALF)


def dot(left, right, transposed):
    dims = (((1,), (1 if transposed else 0,)), ((), ()))
    return lax.dot_general(left, right, dims, preferred_element_type=F32)


def parts_of(block, adjoint=False):
    size = block.shape[0]
    real, imag = block[:, :size], block[:, size:]
    return real, imag, (real - imag if adjoint else real + imag)


def put(matrix, block, adjoint=False):
    size = block.shape[0]
    for index, part in enumerate(parts_of(block, adjoint)):
        matrix[index, :size], matrix[index, size:] = split(part)


def times_split(left, matrix, transposed=False):
    products = []
    for index, stacked in enumerate(left):
        rows, size = stacked.shape[0] // 2, matrix.shape[1] // 2
        high, low = stacked[:rows], stacked[rows:]
        if transposed:
            both = dot(stacked, matrix[index, :size], True)
            both = both[:rows] + both[rows:] + dot(high, matrix[index, size:], True)
        else:
            both = dot(jnp.concatenate([high, high], axis=1), matrix[index], False)
            both += dot(low, matrix[index, :size], False)
        products.append(both)
    first, second, third = products
    if transposed:
        return jnp.concatenate([first + second, third - first + second], axis=1)
    return jnp.concatenate([first - second, third - first - second], axis=1)


def times(block, matrix, transposed=False):
    left = [jnp.concatenate(split(part), axis=0) for part in parts_of(block)]
    return times_split(left, matrix, transposed)


def row_form(pair):
    return jnp.concatenate([pair[0], pair[1]], axis=1)


def adjoint_row(pair):
    return jnp.concatenate([jnp.transpose(pair[0]), -jnp.transpose(pair[1])], axis=1)


def expand(pattern, size):
    blocks = pattern.shape[0]
    tile = size // blocks
    rows = lax.broadcasted_iota(jnp.int32, (size, blocks), 0)
    first = lax.broadcasted_iota(jnp.int32, (size, blocks), 1) * tile
    member = jnp.where((rows >= first) & (rows < first + tile), 1.0, 0.0).astype(HALF)
    tall = dot(member, pattern.astype(F32).astype(HALF), False)
    return dot(tall.astype(HALF), member, True)


def couple(coupling, pattern):
    mask = expand(pattern[...], coupling.shape[-1])
    return jnp.concatenate([coupling[0] * mask, coupling[1] * mask], axis=1)


def trailing():
    return lax.rem(lax.axis_index("energy") + LEADING, 2)


def shape(rows, columns, dtype=F32, *lead):
    return jax.ShapeDtypeStruct(lead + (rows, columns), dtype)


def matrices(number, size):
    return [pltpu.VMEM((3, 2 * size, size), HALF)] * number


def call(
    kernel, outs, scratch, args, specs=None, out_specs=None, aliases=None, flops=0, name=None, limit=40
):
    made = pl.pallas_call(
        kernel,
        out_shape=outs,
        in_specs=specs or [VMEM] * len(args),
        out_specs=out_specs or [VMEM] * len(outs),
        input_output_aliases=aliases or {},
        scratch_shapes=scratch,
        compiler_params=pltpu.CompilerParams(vmem_limit_bytes=int(limit * 2**20)),
        cost_estimate=pl.CostEstimate(flops=flops, bytes_accessed=2**20, transcendentals=0),
        name=name,
    )(*args)
    return list(made)


class Loads:
    def __init__(self, args, targets, sems, couplers=(0, 1), blocks=True):
        order = [(0, 0), (1, 0), (3, 1), (2, 1), (1, 1), (0, 1), (3, 0), (2, 0)]
        self.copies = {
            (which, slab): pltpu.make_async_copy(
                args[which].at[slab], targets[which].at[slab], sems.at[index]
            )
            for index, (which, slab) in enumerate(order)
            if (blocks if which < 2 else slab in couplers)
        }
        self.targets = targets
        for copy in self.copies.values():
            copy.start()

    def get(self, which, slab):
        self.copies[which, slab].wait()
        return self.targets[which].at[slab]

    def green(self, slab):
        return row_form(self.get(0, slab))

    def sigma(self, slab):
        return row_form(self.get(1, slab))

    def coupler(self, slab):
        tiles = self.get(3, slab)
        return couple(self.get(2, slab), tiles)


def load_scratch(size, blocks):
    return [
        pltpu.VMEM((2, 2, size, size), F32),
        pltpu.VMEM((2, 2, size, size), F32),
        pltpu.VMEM((2, 2, size, size), F32),
        pltpu.VMEM((2, blocks, blocks), jnp.int32),
        pltpu.SemaphoreType.DMA((8,)),
    ]


def left_sources(loads, whole, source, coupler_out, m_a, m_b, m_c):
    first = loads.green(0)
    put(m_b, first)
    put(m_a, loads.sigma(0))
    made = first + times(times(first, m_a), m_b)
    if source is not None:
        source[...] = made
    put(m_a, made)
    coupler = loads.coupler(1)
    if coupler_out is not None:
        coupler_out[...] = coupler
    put(m_c, coupler, True)
    inner = loads.sigma(1) + times(times(coupler, m_a), m_c, True)
    put(m_a, inner)
    second = loads.green(1)
    put(m_b, second)
    whole[...] = second + times(times(second, m_a), m_b)
    return first, second


def source_kernel(green, sigma, coupling, pattern, whole, *scratch):
    @pl.when(lax.axis_index("slab") == 0)
    def _():
        loads = Loads((green, sigma, coupling, pattern), scratch[:4], scratch[4], (1,))
        left_sources(loads, whole, None, None, *scratch[5:])

    @pl.when((lax.axis_index("slab") > 0) & (trailing() == 1))
    def _():
        loads = Loads((green, sigma, coupling, pattern), scratch[:4], scratch[4], (0,), False)
        whole[...] = loads.coupler(0)


def map_kernel(
    green, sigma, coupling, pattern,
    whole, source, coupler, opening, lead, tail, forward, backward, *scratch,
):
    m_a, m_b, m_c = scratch[5:]
    loads = Loads((green, sigma, coupling, pattern), scratch[:4], scratch[4])
    first, second = left_sources(loads, whole, source, coupler, m_a, m_b, m_c)
    before = loads.coupler(0)

    @pl.when(lax.axis_index("slab") > 0)
    def _():
        opening[...] = before
        put(m_a, first)
        size = before.shape[0]
        behind = times(adjoint_row((before[:, :size], before[:, size:])), m_a)
        backward[...] = behind
        put(tail, times(times(behind, m_c, True), m_b))
        put(m_a, before)
        ahead = times(first, m_a)
        forward[...] = ahead
        put(m_a, ahead)
        put(m_c, coupler[...])
        put(lead, times(times(second, m_c), m_a))


def right_terms(first, last, coupler, m_coupler, m_first, m_last, m_upper):
    put(m_coupler, coupler, True)
    put(m_last, last)
    through = times(times(first, m_coupler, True), m_last)
    put(m_first, first)
    put(m_upper, times(coupler, m_first))
    return through, first + times(through, m_upper)


def prepare_kernel(count, *refs):
    arrived, wholes = refs[: count - 1], refs[count - 1 : 2 * count - 2]
    refs = refs[2 * count - 2 :]
    start_whole, source, forward, backward, coupler = refs[:5]
    followings = refs[5:7]
    lead, tail, constant, last_lead, last_tail = refs[8:13]
    first_v, last_v, m_a, m_b, m_c, m_d = refs[13:]
    place = lax.axis_index("slab")

    @pl.when(place == 0)
    def _():
        first_v[...] = source[...]
        last_v[...] = start_whole[...]

    for turn in range(count - 1):
        @pl.when((place > 0) & (place == turn + 1 - trailing()))
        def _(turn=turn):
            last_v[...] = wholes[turn][...]
            put(m_a, arrived[turn][...])

    @pl.when((place > 0) & (place < count - 1))
    def _():
        put(m_b, backward[...])
        first_v[...] = source[...] + times(times(forward[...], m_a), m_b)

    @pl.when(place < count - 1)
    def _():
        first, last = first_v[...], last_v[...]
        through, joined = right_terms(first, last, coupler[...], m_a, m_b, m_c, m_d)
        constant[...] = joined
        next_coupler = jnp.where(trailing() == 0, followings[0][...], followings[1][...])
        put(m_a, next_coupler, True)
        put(lead, times(through, m_a, True))
        put(last_lead, times(last, m_a, True))
        behind = times(next_coupler, m_c)
        put(last_tail, behind)
        put(tail, times(behind, m_d))


def apply_map(mapping, m_x):
    lead, tail, constant = mapping
    ahead = [lead[index] for index in range(3)]
    return constant[...] + times(times_split(ahead, m_x), tail)


def relay_kernel(step, count, lefts, rights, *refs):
    refs = list(refs)
    place = lax.axis_index("slab")
    turn = step - trailing()
    is_left = (turn >= 0) & (turn <= count - 2) & (place == turn + 1)
    is_right = (turn >= count - 1) & (place == 2 * count - 3 - turn)
    closing = lefts and step >= count - 2
    arrived = refs.pop(0)
    left_map = [refs.pop(0) for _ in range(3)] if lefts else None
    right_map = [refs.pop(0) for _ in range(3)] if rights else None
    if closing:
        forward, backward, source, coupler = [refs.pop(0) for _ in range(4)]
    out = refs.pop(0)
    if closing:
        end, m_x, m_a, m_b, m_c = refs
    else:
        (m_x,) = refs

    if step == 0:
        @pl.when(place == 0)
        def _():
            out[...] = left_map[2][...]

    if lefts:
        @pl.when(is_left & (place < count - 1) if closing else is_left)
        def _():
            put(m_x, arrived[...])
            out[...] = apply_map(left_map, m_x)

    if closing:
        @pl.when(is_left & (place == count - 1))
        def _():
            put(m_x, arrived[...])
            last = apply_map(left_map, m_x)
            end[...] = last
            put(m_a, backward[...])
            first = source[...] + times(times(forward[...], m_x), m_a)
            _, joined = right_terms(first, last, coupler[...], m_a, m_b, m_c, m_x)
            out[...] = joined

    if rights:
        @pl.when(is_right & (place > 0))
        def _():
            put(m_x, arrived[...])
            out[...] = apply_map(right_map, m_x)


def last_kernel(count, *refs):
    refs = list(refs)
    arrived = [refs.pop(0) for _ in range(count)]
    ends = [refs.pop(0) for _ in range(2)]
    last_lead, last_tail, whole_start = [refs.pop(0) for _ in range(3)]
    wholes = [refs.pop(0) for _ in range(count - 1)]
    block, *parcels, m_x = refs
    place = lax.axis_index("slab")
    core = trailing()
    is_last = place == count - 1

    for index in range(count):
        @pl.when(jnp.logical_not(is_last) & (2 * count - 3 - place + core == count - 1 + index))
        def _(index=index):
            put(m_x, arrived[index][...])

    for index in range(2):
        @pl.when(is_last & (core == index))
        def _(index=index):
            block[...] = ends[index][...]

    @pl.when(place == 0)
    def _():
        block[...] = apply_map((last_lead, last_tail, whole_start), m_x)

    for index in range(count - 1):
        @pl.when((place > 0) & jnp.logical_not(is_last) & (place - 1 + core == index))
        def _(index=index):
            block[...] = apply_map((last_lead, last_tail, wholes[index]), m_x)

    pack(block, parcels)


def first_kernel(count, *refs):
    arrived, outs = refs[:2], refs[2 : count + 2]
    right_map = refs[count + 2 : count + 5]
    block, *parcels, m_x = refs[count + 6 :]
    place, core = lax.axis_index("slab"), trailing()
    at = jnp.where(place == count - 1, count - 2 + core, 2 * count - 3 - place + core)

    for index in range(count):
        @pl.when((place > 0) & (at == count - 2 + index))
        def _(index=index):
            block[...] = outs[index][...]

    for index in range(2):
        @pl.when((place == 0) & (core == index))
        def _(index=index):
            put(m_x, arrived[index][...])

    @pl.when(place == 0)
    def _():
        block[...] = apply_map(right_map, m_x)

    pack(block, parcels)


def pack(block, parcels):
    for mask, parcel in enumerate(parcels):
        parcel[...] = block[share(mask, parcel.shape[0]), :]


def unpack_kernel(*refs):
    blocks, out = refs[:2], refs[2]
    size = out.shape[-1]
    for slab, block in enumerate(blocks):
        for part in range(2):
            out[slab, part] = block[:, part * size : (part + 1) * size]


def share(mask, rows):
    chip = lax.shift_right_logical(lax.axis_index("energy"), 1)
    return pl.ds(pl.multiple_of(lax.bitwise_xor(chip, mask) * rows, rows), rows)


def far_first(chips):
    return sorted(range(chips), key=lambda mask: -bin(mask).count("1"))


def weight_kernel(chips, weights, tiles):
    energy = lax.axis_index("energy")
    core = lax.rem(energy, 2)
    sources = [lax.bitwise_xor(energy, 2 * mask) for mask in range(chips)]
    for mask in range(chips):
        for side, target in enumerate((sources[mask], sources[mask] + 1 - 2 * core)):
            for index in range(chips):
                weight = weights[target, sources[index]]
                tiles[side, mask, index] = jnp.full(tiles.shape[3:], weight, F32)


def mix_kernel(chips, tiles, *refs):
    parcels, outs = dict(zip(far_first(chips), refs[:chips])), refs[chips:]
    rows, columns = parcels[0].shape
    step, width = tiles.shape[3:]
    for row in range(0, rows, step):
        where = slice(row, row + step)
        values = [parcels[mask][where] for mask in range(chips)]
        for side, out in enumerate(outs):
            for mask in range(chips):
                total = None
                for index in range(chips):
                    weight = jnp.concatenate([tiles[side, mask, index]] * (columns // width), axis=1)
                    term = weight * values[index]
                    total = term if total is None else total + term
                out[mask, where] = total


def sum_kernel(chips, mine, other, *outs):
    for mask in range(chips):
        outs[mask][...] = mine[mask] + other[mask]


def place_kernel(chips, slab, *refs):
    parcels, scattering, sems = refs[:chips], refs[-2], refs[-1]
    size = scattering.shape[-1]
    copies = []
    for index, (mask, parcel) in enumerate(zip(far_first(chips), parcels)):
        for part in range(2):
            copies.append(
                pltpu.make_async_copy(
                    parcel.at[:, pl.ds(part * size, size)],
                    scattering.at[slab, part, share(mask, parcel.shape[0]), :],
                    sems.at[index, part],
                )
            )
            copies[-1].start()
    for copy in copies:
        copy.wait()


def mode_weights(targets, sources, offsets, emission, absorption):
    spacing = sources[None, :, None] - targets[:, None, None]
    emitted = jnp.where(
        spacing == -offsets[None, None, :],
        emission[None, None, :],
        jnp.zeros_like(emission)[None, None, :],
    )
    absorbed = jnp.where(
        spacing == offsets[None, None, :],
        absorption[None, None, :],
        jnp.zeros_like(absorption)[None, None, :],
    )
    return jnp.sum(emitted + absorbed, axis=-1)


def relay_pairs(step, energies, count):
    pairs = []
    for energy in range(energies):
        turn = step - (energy + LEADING) % 2
        if turn < 0:
            pairs += [(energy * count + i, energy * count + i - 1) for i in range(1, count)]
        if 0 <= turn <= count - 2:
            ends = (turn, turn + 1)
        elif count - 1 <= turn <= 2 * count - 3:
            ends = (2 * count - 2 - turn, 2 * count - 3 - turn)
        else:
            continue
        pairs.append(tuple(energy * count + end for end in ends))
    return pairs


def shards(energies, count, free_green, self_energy, coupling, pattern, offsets, emission, absorption):
    size, blocks = free_green.shape[-1], pattern.shape[-1]
    args = (free_green[0], self_energy[0], coupling, pattern)
    row = shape(size, 2 * size)
    factor = shape(2 * size, size, HALF, 3)
    row_v = pltpu.VMEM(row.shape, F32)
    product = 24 * size**3
    loading = load_scratch(size, blocks) + matrices(3, size)

    def relay(step, value):
        return lax.ppermute(value, ("energy", "slab"), relay_pairs(step, energies, count))

    begun = call(
        source_kernel,
        [row],
        loading,
        args,
        [HBM] * 4,
        flops=6 * product,
        name="source",
        limit=53,
    )
    arrived, outs, ends = [relay(0, begun[0])], [], []
    whole, source, coupler, opening, left_lead, left_tail, forward, backward = call(
        map_kernel,
        [row] * 4 + [factor, factor, row, row],
        loading,
        args,
        [HBM] * 4,
        flops=12 * product,
        name="left_maps",
        limit=48.6,
    )
    left_map = [left_lead, left_tail, whole]
    chips = energies // 2
    everyone = jnp.arange(energies, dtype=jnp.int32)
    weights = mode_weights(everyone, everyone, offsets, emission, absorption)
    (tiles,) = call(
        functools.partial(weight_kernel, chips),
        [shape(8, 128, F32, 2, chips, chips)],
        [],
        [weights],
        [SMEM],
        name="weights",
    )
    right_map = None
    for step in range(2 * count - 2):
        lefts, rights = step <= count - 1, step >= count - 1
        closing = lefts and step >= count - 2
        args = [arrived[step]]
        if lefts:
            args += left_map
        if rights:
            args += right_map[:3]
        if closing:
            args += [forward, backward, source, coupler]
        made = call(
            functools.partial(relay_kernel, step, count, lefts, rights),
            [row] * (2 if closing else 1),
            matrices(4 if closing else 1, size),
            args,
            flops=2 * product,
            name="relay",
        )
        outs.append(made[0])
        ends += made[1:]
        arrived.append(relay(step + 1, made[0]))
        if step == 0:
            down = [
                (energy * count + i, energy * count + i - 1)
                for energy in range(energies)
                for i in range(1, count)
                if (energy + LEADING) % 2 == 0
            ]
            following = lax.ppermute(opening, ("energy", "slab"), down)
        if step == count - 2:
            args = arrived[: count - 1] + outs[: count - 1]
            args += [whole, source, forward, backward, coupler, following, arrived[0], tiles]
            right_map = call(
                functools.partial(prepare_kernel, count),
                [factor, factor, row, factor, factor],
                [row_v] * 2 + matrices(4, size),
                args,
                flops=10 * product,
                name="right_maps",
            )
    parcel = shape(size // chips, 2 * size)
    blocks, parcels = [None, None], [None, None]
    args = arrived[count - 1 :] + ends + right_map[3:] + [whole] + outs[: count - 1]
    blocks[1], *parcels[1] = call(
        functools.partial(last_kernel, count),
        [row] + [parcel] * chips,
        matrices(1, size),
        args,
        flops=2 * product,
        name="second_slab",
    )
    args = arrived[-2:] + outs[count - 2 :] + right_map[:3] + blocks[1:]
    blocks[0], *parcels[0] = call(
        functools.partial(first_kernel, count),
        [row] + [parcel] * chips,
        matrices(1, size),
        args,
        flops=2 * product,
        name="first_slab",
    )
    (retarded,) = call(
        unpack_kernel, [shape(size, size, F32, 2, 2)], [], blocks, name="retarded"
    )

    masks = far_first(chips)

    def exchange(values):
        sent = list(values)
        for mask in masks[:-1]:
            pairs = [(i, i ^ (2 * mask)) for i in range(energies)]
            sent[mask] = lax.ppermute(values[mask], "energy", pairs)
        return [sent[mask] for mask in masks]

    partial = shape(size // chips, 2 * size, F32, chips)
    sums = [None, None]
    received = exchange(parcels[1])
    for slab in (1, 0):
        if slab == 0 and chips > 1:
            last = masks[-2]
            parcels[0][last], _ = lax.optimization_barrier((parcels[0][last], received[0]))
            received = exchange(parcels[0])
        mine, other = call(
            functools.partial(mix_kernel, chips),
            [partial] * 2,
            [],
            [tiles] + received,
            flops=product // 8,
            name="mix",
        )
        other = lax.ppermute(other, "energy", [(i, i ^ 1) for i in range(energies)])
        sums[slab] = call(
            functools.partial(sum_kernel, chips), [parcel] * chips, [], [mine, other], name="sum"
        )
    returned = [exchange(sums[slab]) for slab in (1, 0)][::-1]
    scattering = []
    for slab in (1, 0):
        scattering = call(
            functools.partial(place_kernel, chips, slab),
            [shape(size, size, F32, 2, 2)],
            [pltpu.SemaphoreType.DMA((chips, 2))],
            returned[slab] + scattering,
            [VMEM] * chips + [HBM] * len(scattering),
            [HBM],
            aliases={chips: 0} if scattering else {},
            name="scattering",
        )
    (scattering,) = scattering
    return (retarded[None], scattering[None])


def solution(mesh):
    blocks = P("energy", "slab", None, None, None)
    in_specs = (blocks, blocks, P("slab", None, None, None), P("slab", None, None), P(), P(), P())
    body = functools.partial(shards, mesh.shape["energy"], mesh.shape["slab"])
    return jax.shard_map(
        body, mesh=mesh, in_specs=in_specs, out_specs=(blocks, blocks), check_vma=False
    )
```

```python
import functools

import jax
import jax.numpy as jnp
from jax import lax
from jax.experimental import pallas as pl
from jax.experimental.pallas import tpu as pltpu
from jax.sharding import PartitionSpec as P

F32 = jnp.float32
HALF = jnp.bfloat16
HBM = pl.BlockSpec(memory_space=pltpu.HBM)
VMEM = pl.BlockSpec(memory_space=pltpu.VMEM)
SMEM = pl.BlockSpec(memory_space=pltpu.SMEM)
LEADING = 0


def split(value):
    high = value.astype(HALF)
    return high, (value - high.astype(F32)).astype(HALF)


def dot(left, right, transposed):
    dims = (((1,), (1 if transposed else 0,)), ((), ()))
    return lax.dot_general(left, right, dims, preferred_element_type=F32)


def parts_of(block, adjoint=False):
    size = block.shape[0]
    real, imag = block[:, :size], block[:, size:]
    return real, imag, (real - imag if adjoint else real + imag)


def put(matrix, block, adjoint=False):
    size = block.shape[0]
    for index, part in enumerate(parts_of(block, adjoint)):
        matrix[index, :size], matrix[index, size:] = split(part)


def times_split(left, matrix, transposed=False):
    products = []
    for index, stacked in enumerate(left):
        rows, size = stacked.shape[0] // 2, matrix.shape[1] // 2
        high, low = stacked[:rows], stacked[rows:]
        if transposed:
            both = dot(stacked, matrix[index, :size], True)
            both = both[:rows] + both[rows:] + dot(high, matrix[index, size:], True)
        else:
            both = dot(jnp.concatenate([high, high], axis=1), matrix[index], False)
            both += dot(low, matrix[index, :size], False)
        products.append(both)
    first, second, third = products
    if transposed:
        return jnp.concatenate([first + second, third - first + second], axis=1)
    return jnp.concatenate([first - second, third - first - second], axis=1)


def times(block, matrix, transposed=False):
    left = [jnp.concatenate(split(part), axis=0) for part in parts_of(block)]
    return times_split(left, matrix, transposed)


def row_form(pair):
    return jnp.concatenate([pair[0], pair[1]], axis=1)


def adjoint_row(pair):
    return jnp.concatenate([jnp.transpose(pair[0]), -jnp.transpose(pair[1])], axis=1)


def expand(pattern, size):
    blocks = pattern.shape[0]
    tile = size // blocks
    rows = lax.broadcasted_iota(jnp.int32, (size, blocks), 0)
    first = lax.broadcasted_iota(jnp.int32, (size, blocks), 1) * tile
    member = jnp.where((rows >= first) & (rows < first + tile), 1.0, 0.0).astype(HALF)
    tall = dot(member, pattern.astype(F32).astype(HALF), False)
    return dot(tall.astype(HALF), member, True)


def couple(coupling, pattern):
    mask = expand(pattern[...], coupling.shape[-1])
    return jnp.concatenate([coupling[0] * mask, coupling[1] * mask], axis=1)


def trailing():
    return lax.rem(lax.axis_index("energy") + LEADING, 2)


def shape(rows, columns, dtype=F32, *lead):
    return jax.ShapeDtypeStruct(lead + (rows, columns), dtype)


def matrices(number, size):
    return [pltpu.VMEM((3, 2 * size, size), HALF)] * number


def call(
    kernel, outs, scratch, args, specs=None, out_specs=None, aliases=None, flops=0, name=None, limit=40
):
    made = pl.pallas_call(
        kernel,
        out_shape=outs,
        in_specs=specs or [VMEM] * len(args),
        out_specs=out_specs or [VMEM] * len(outs),
        input_output_aliases=aliases or {},
        scratch_shapes=scratch,
        compiler_params=pltpu.CompilerParams(vmem_limit_bytes=int(limit * 2**20)),
        cost_estimate=pl.CostEstimate(flops=flops, bytes_accessed=2**20, transcendentals=0),
        name=name,
    )(*args)
    return list(made)


class Loads:
    def __init__(self, args, targets, sems, couplers=(0, 1), blocks=True):
        order = [(0, 0), (1, 0), (3, 1), (2, 1), (1, 1), (0, 1), (3, 0), (2, 0)]
        self.copies = {
            (which, slab): pltpu.make_async_copy(
                args[which].at[slab], targets[which].at[slab], sems.at[index]
            )
            for index, (which, slab) in enumerate(order)
            if (blocks if which < 2 else slab in couplers)
        }
        self.targets = targets
        for copy in self.copies.values():
            copy.start()

    def get(self, which, slab):
        self.copies[which, slab].wait()
        return self.targets[which].at[slab]

    def green(self, slab):
        return row_form(self.get(0, slab))

    def sigma(self, slab):
        return row_form(self.get(1, slab))

    def coupler(self, slab):
        tiles = self.get(3, slab)
        return couple(self.get(2, slab), tiles)


def load_scratch(size, blocks):
    return [
        pltpu.VMEM((2, 2, size, size), F32),
        pltpu.VMEM((2, 2, size, size), F32),
        pltpu.VMEM((2, 2, size, size), F32),
        pltpu.VMEM((2, blocks, blocks), jnp.int32),
        pltpu.SemaphoreType.DMA((8,)),
    ]


def left_sources(loads, whole, source, coupler_out, m_a, m_b, m_c):
    first = loads.green(0)
    put(m_b, first)
    put(m_a, loads.sigma(0))
    coupler = loads.coupler(1)
    put(m_c, coupler, True)
    if coupler_out is not None:
        coupler_out[...] = coupler
    made = first + times(times(first, m_a), m_b)
    if source is not None:
        source[...] = made
    sigma, second = loads.sigma(1), loads.green(1)
    put(m_a, made)
    put(m_b, second)
    inner = sigma + times(times(coupler, m_a), m_c, True)
    put(m_a, inner)
    whole[...] = second + times(times(second, m_a), m_b)
    return first, second


def source_kernel(green, sigma, coupling, pattern, whole, *scratch):
    @pl.when(lax.axis_index("slab") == 0)
    def _():
        loads = Loads((green, sigma, coupling, pattern), scratch[:4], scratch[4], (1,))
        left_sources(loads, whole, None, None, *scratch[5:])

    @pl.when((lax.axis_index("slab") > 0) & (trailing() == 1))
    def _():
        loads = Loads((green, sigma, coupling, pattern), scratch[:4], scratch[4], (0,), False)
        whole[...] = loads.coupler(0)


def map_kernel(
    green, sigma, coupling, pattern,
    whole, source, coupler, opening, lead, tail, forward, backward, *scratch,
):
    m_a, m_b, m_c = scratch[5:]
    loads = Loads((green, sigma, coupling, pattern), scratch[:4], scratch[4])
    first, second = left_sources(loads, whole, source, coupler, m_a, m_b, m_c)
    before = loads.coupler(0)

    @pl.when(lax.axis_index("slab") > 0)
    def _():
        opening[...] = before
        put(m_a, first)
        size = before.shape[0]
        behind = times(adjoint_row((before[:, :size], before[:, size:])), m_a)
        backward[...] = behind
        put(tail, times(times(behind, m_c, True), m_b))
        put(m_a, before)
        ahead = times(first, m_a)
        forward[...] = ahead
        put(m_a, ahead)
        put(m_c, coupler[...])
        put(lead, times(times(second, m_c), m_a))


def right_terms(first, last, coupler, m_coupler, m_first, m_last, m_upper):
    put(m_coupler, coupler, True)
    put(m_last, last)
    through = times(times(first, m_coupler, True), m_last)
    put(m_first, first)
    put(m_upper, times(coupler, m_first))
    return through, first + times(through, m_upper)


def prepare_kernel(count, *refs):
    arrived, wholes = refs[: count - 1], refs[count - 1 : 2 * count - 2]
    refs = refs[2 * count - 2 :]
    start_whole, source, forward, backward, coupler = refs[:5]
    followings = refs[5:7]
    lead, tail, constant, last_lead, last_tail = refs[8:13]
    first_v, last_v, m_a, m_b, m_c, m_d = refs[13:]
    place = lax.axis_index("slab")

    @pl.when(place == 0)
    def _():
        first_v[...] = source[...]
        last_v[...] = start_whole[...]

    for turn in range(count - 1):
        @pl.when((place > 0) & (place == turn + 1 - trailing()))
        def _(turn=turn):
            last_v[...] = wholes[turn][...]
            put(m_a, arrived[turn][...])

    @pl.when((place > 0) & (place < count - 1))
    def _():
        put(m_b, backward[...])
        first_v[...] = source[...] + times(times(forward[...], m_a), m_b)

    @pl.when(place < count - 1)
    def _():
        first, last = first_v[...], last_v[...]
        through, joined = right_terms(first, last, coupler[...], m_a, m_b, m_c, m_d)
        constant[...] = joined
        next_coupler = jnp.where(trailing() == 0, followings[0][...], followings[1][...])
        put(m_a, next_coupler, True)
        put(lead, times(through, m_a, True))
        put(last_lead, times(last, m_a, True))
        behind = times(next_coupler, m_c)
        put(last_tail, behind)
        put(tail, times(behind, m_d))


def apply_map(mapping, m_x):
    lead, tail, constant = mapping
    ahead = [lead[index] for index in range(3)]
    return constant[...] + times(times_split(ahead, m_x), tail)


def relay_kernel(step, count, lefts, rights, *refs):
    refs = list(refs)
    place = lax.axis_index("slab")
    turn = step - trailing()
    is_left = (turn >= 0) & (turn <= count - 2) & (place == turn + 1)
    is_right = (turn >= count - 1) & (place == 2 * count - 3 - turn)
    closing = lefts and step >= count - 2
    arrived = refs.pop(0)
    left_map = [refs.pop(0) for _ in range(3)] if lefts else None
    right_map = [refs.pop(0) for _ in range(3)] if rights else None
    if closing:
        forward, backward, source, coupler = [refs.pop(0) for _ in range(4)]
    out = refs.pop(0)
    if closing:
        end, m_x, m_a, m_b, m_c = refs
    else:
        (m_x,) = refs

    if step == 0:
        @pl.when(place == 0)
        def _():
            out[...] = left_map[2][...]

    if lefts:
        @pl.when(is_left & (place < count - 1) if closing else is_left)
        def _():
            put(m_x, arrived[...])
            out[...] = apply_map(left_map, m_x)

    if closing:
        @pl.when(is_left & (place == count - 1))
        def _():
            put(m_x, arrived[...])
            last = apply_map(left_map, m_x)
            end[...] = last
            put(m_a, backward[...])
            first = source[...] + times(times(forward[...], m_x), m_a)
            _, joined = right_terms(first, last, coupler[...], m_a, m_b, m_c, m_x)
            out[...] = joined

    if rights:
        @pl.when(is_right & (place > 0))
        def _():
            put(m_x, arrived[...])
            out[...] = apply_map(right_map, m_x)


def last_kernel(count, *refs):
    refs = list(refs)
    arrived = [refs.pop(0) for _ in range(count)]
    ends = [refs.pop(0) for _ in range(2)]
    last_lead, last_tail, whole_start = [refs.pop(0) for _ in range(3)]
    wholes = [refs.pop(0) for _ in range(count - 1)]
    block, *parcels, m_x = refs
    place = lax.axis_index("slab")
    core = trailing()
    is_last = place == count - 1

    for index in range(count):
        @pl.when(jnp.logical_not(is_last) & (2 * count - 3 - place + core == count - 1 + index))
        def _(index=index):
            put(m_x, arrived[index][...])

    for index in range(2):
        @pl.when(is_last & (core == index))
        def _(index=index):
            block[...] = ends[index][...]

    @pl.when(place == 0)
    def _():
        block[...] = apply_map((last_lead, last_tail, whole_start), m_x)

    for index in range(count - 1):
        @pl.when((place > 0) & jnp.logical_not(is_last) & (place - 1 + core == index))
        def _(index=index):
            block[...] = apply_map((last_lead, last_tail, wholes[index]), m_x)

    pack(block, parcels)


def first_kernel(count, *refs):
    arrived, outs = refs[:2], refs[2 : count + 2]
    right_map = refs[count + 2 : count + 5]
    block, *parcels, m_x = refs[count + 6 :]
    place, core = lax.axis_index("slab"), trailing()
    at = jnp.where(place == count - 1, count - 2 + core, 2 * count - 3 - place + core)

    for index in range(count):
        @pl.when((place > 0) & (at == count - 2 + index))
        def _(index=index):
            block[...] = outs[index][...]

    for index in range(2):
        @pl.when((place == 0) & (core == index))
        def _(index=index):
            put(m_x, arrived[index][...])

    @pl.when(place == 0)
    def _():
        block[...] = apply_map(right_map, m_x)

    pack(block, parcels)


def pack(block, parcels):
    for mask, parcel in enumerate(parcels):
        parcel[...] = block[share(mask, parcel.shape[0]), :]


def unpack_kernel(*refs):
    blocks, out = refs[:2], refs[2]
    size = out.shape[-1]
    for slab, block in enumerate(blocks):
        for part in range(2):
            out[slab, part] = block[:, part * size : (part + 1) * size]


def share(mask, rows):
    chip = lax.shift_right_logical(lax.axis_index("energy"), 1)
    return pl.ds(pl.multiple_of(lax.bitwise_xor(chip, mask) * rows, rows), rows)


def far_first(chips):
    return sorted(range(chips), key=lambda mask: -bin(mask).count("1"))


def weight_kernel(chips, weights, tiles):
    energy = lax.axis_index("energy")
    core = lax.rem(energy, 2)
    sources = [lax.bitwise_xor(energy, 2 * mask) for mask in range(chips)]
    for mask in range(chips):
        for side, target in enumerate((sources[mask], sources[mask] + 1 - 2 * core)):
            for index in range(chips):
                weight = weights[target, sources[index]]
                tiles[side, mask, index] = jnp.full(tiles.shape[3:], weight, F32)


def mix_kernel(chips, tiles, *refs):
    parcels, outs = dict(zip(far_first(chips), refs[:chips])), refs[chips:]
    rows, columns = parcels[0].shape
    step, width = tiles.shape[3:]
    for row in range(0, rows, step):
        where = slice(row, row + step)
        values = [parcels[mask][where] for mask in range(chips)]
        for side, out in enumerate(outs):
            for mask in range(chips):
                total = None
                for index in range(chips):
                    weight = jnp.concatenate([tiles[side, mask, index]] * (columns // width), axis=1)
                    term = weight * values[index]
                    total = term if total is None else total + term
                out[mask, where] = total


def sum_kernel(chips, mine, other, *outs):
    for mask in range(chips):
        outs[mask][...] = mine[mask] + other[mask]


def place_kernel(chips, slab, *refs):
    parcels, scattering, sems = refs[:chips], refs[-2], refs[-1]
    size = scattering.shape[-1]
    copies = []
    for index, (mask, parcel) in enumerate(zip(far_first(chips), parcels)):
        for part in range(2):
            copies.append(
                pltpu.make_async_copy(
                    parcel.at[:, pl.ds(part * size, size)],
                    scattering.at[slab, part, share(mask, parcel.shape[0]), :],
                    sems.at[index, part],
                )
            )
            copies[-1].start()
    for copy in copies:
        copy.wait()


def mode_weights(targets, sources, offsets, emission, absorption):
    spacing = sources[None, :, None] - targets[:, None, None]
    emitted = jnp.where(
        spacing == -offsets[None, None, :],
        emission[None, None, :],
        jnp.zeros_like(emission)[None, None, :],
    )
    absorbed = jnp.where(
        spacing == offsets[None, None, :],
        absorption[None, None, :],
        jnp.zeros_like(absorption)[None, None, :],
    )
    return jnp.sum(emitted + absorbed, axis=-1)


def relay_pairs(step, energies, count):
    pairs = []
    for energy in range(energies):
        turn = step - (energy + LEADING) % 2
        if turn < 0:
            pairs += [(energy * count + i, energy * count + i - 1) for i in range(1, count)]
        if 0 <= turn <= count - 2:
            ends = (turn, turn + 1)
        elif count - 1 <= turn <= 2 * count - 3:
            ends = (2 * count - 2 - turn, 2 * count - 3 - turn)
        else:
            continue
        pairs.append(tuple(energy * count + end for end in ends))
    return pairs


def shards(energies, count, free_green, self_energy, coupling, pattern, offsets, emission, absorption):
    size, blocks = free_green.shape[-1], pattern.shape[-1]
    args = (free_green[0], self_energy[0], coupling, pattern)
    row = shape(size, 2 * size)
    factor = shape(2 * size, size, HALF, 3)
    row_v = pltpu.VMEM(row.shape, F32)
    product = 24 * size**3
    loading = load_scratch(size, blocks) + matrices(3, size)

    def relay(step, value):
        return lax.ppermute(value, ("energy", "slab"), relay_pairs(step, energies, count))

    begun = call(
        source_kernel,
        [row],
        loading,
        args,
        [HBM] * 4,
        flops=6 * product,
        name="source",
        limit=53,
    )
    arrived, outs, ends = [relay(0, begun[0])], [], []
    whole, source, coupler, opening, left_lead, left_tail, forward, backward = call(
        map_kernel,
        [row] * 4 + [factor, factor, row, row],
        loading,
        args,
        [HBM] * 4,
        flops=12 * product,
        name="left_maps",
        limit=48.6,
    )
    left_map = [left_lead, left_tail, whole]
    chips = energies // 2
    everyone = jnp.arange(energies, dtype=jnp.int32)
    weights = mode_weights(everyone, everyone, offsets, emission, absorption)
    (tiles,) = call(
        functools.partial(weight_kernel, chips),
        [shape(8, 128, F32, 2, chips, chips)],
        [],
        [weights],
        [SMEM],
        name="weights",
    )
    right_map = None
    for step in range(2 * count - 2):
        lefts, rights = step <= count - 1, step >= count - 1
        closing = lefts and step >= count - 2
        args = [arrived[step]]
        if lefts:
            args += left_map
        if rights:
            args += right_map[:3]
        if closing:
            args += [forward, backward, source, coupler]
        made = call(
            functools.partial(relay_kernel, step, count, lefts, rights),
            [row] * (2 if closing else 1),
            matrices(4 if closing else 1, size),
            args,
            flops=2 * product,
            name="relay",
        )
        outs.append(made[0])
        ends += made[1:]
        arrived.append(relay(step + 1, made[0]))
        if step == 0:
            down = [
                (energy * count + i, energy * count + i - 1)
                for energy in range(energies)
                for i in range(1, count)
                if (energy + LEADING) % 2 == 0
            ]
            following = lax.ppermute(opening, ("energy", "slab"), down)
        if step == count - 2:
            args = arrived[: count - 1] + outs[: count - 1]
            args += [whole, source, forward, backward, coupler, following, arrived[0], tiles]
            right_map = call(
                functools.partial(prepare_kernel, count),
                [factor, factor, row, factor, factor],
                [row_v] * 2 + matrices(4, size),
                args,
                flops=10 * product,
                name="right_maps",
            )
    parcel = shape(size // chips, 2 * size)
    blocks, parcels = [None, None], [None, None]
    args = arrived[count - 1 :] + ends + right_map[3:] + [whole] + outs[: count - 1]
    blocks[1], *parcels[1] = call(
        functools.partial(last_kernel, count),
        [row] + [parcel] * chips,
        matrices(1, size),
        args,
        flops=2 * product,
        name="second_slab",
    )
    args = arrived[-2:] + outs[count - 2 :] + right_map[:3] + blocks[1:]
    blocks[0], *parcels[0] = call(
        functools.partial(first_kernel, count),
        [row] + [parcel] * chips,
        matrices(1, size),
        args,
        flops=2 * product,
        name="first_slab",
    )
    (retarded,) = call(
        unpack_kernel, [shape(size, size, F32, 2, 2)], [], blocks, name="retarded"
    )

    masks = far_first(chips)

    def exchange(values):
        sent = list(values)
        for mask in masks[:-1]:
            pairs = [(i, i ^ (2 * mask)) for i in range(energies)]
            sent[mask] = lax.ppermute(values[mask], "energy", pairs)
        return [sent[mask] for mask in masks]

    partial = shape(size // chips, 2 * size, F32, chips)
    sums = [None, None]
    received = exchange(parcels[1])
    for slab in (1, 0):
        if slab == 0 and chips > 1:
            last = masks[-2]
            parcels[0][last], _ = lax.optimization_barrier((parcels[0][last], received[0]))
            received = exchange(parcels[0])
        mine, other = call(
            functools.partial(mix_kernel, chips),
            [partial] * 2,
            [],
            [tiles] + received,
            flops=product // 8,
            name="mix",
        )
        other = lax.ppermute(other, "energy", [(i, i ^ 1) for i in range(energies)])
        sums[slab] = call(
            functools.partial(sum_kernel, chips), [parcel] * chips, [], [mine, other], name="sum"
        )
    returned = [exchange(sums[slab]) for slab in (1, 0)][::-1]
    scattering = []
    for slab in (1, 0):
        scattering = call(
            functools.partial(place_kernel, chips, slab),
            [shape(size, size, F32, 2, 2)],
            [pltpu.SemaphoreType.DMA((chips, 2))],
            returned[slab] + scattering,
            [VMEM] * chips + [HBM] * len(scattering),
            [HBM],
            aliases={chips: 0} if scattering else {},
            name="scattering",
        )
    (scattering,) = scattering
    return (retarded[None], scattering[None])


def solution(mesh):
    blocks = P("energy", "slab", None, None, None)
    in_specs = (blocks, blocks, P("slab", None, None, None), P("slab", None, None), P(), P(), P())
    body = functools.partial(shards, mesh.shape["energy"], mesh.shape["slab"])
    return jax.shard_map(
        body, mesh=mesh, in_specs=in_specs, out_specs=(blocks, blocks), check_vma=False
    )
```

```python
import functools

import jax
import jax.numpy as jnp
from jax import lax
from jax.experimental import pallas as pl
from jax.experimental.pallas import tpu as pltpu
from jax.sharding import PartitionSpec as P

F32 = jnp.float32
HALF = jnp.bfloat16
HBM = pl.BlockSpec(memory_space=pltpu.HBM)
VMEM = pl.BlockSpec(memory_space=pltpu.VMEM)
SMEM = pl.BlockSpec(memory_space=pltpu.SMEM)
LEADING = 0


def split(value):
    high = value.astype(HALF)
    return high, (value - high.astype(F32)).astype(HALF)


def dot(left, right, transposed):
    dims = (((1,), (1 if transposed else 0,)), ((), ()))
    return lax.dot_general(left, right, dims, preferred_element_type=F32)


def parts_of(block, adjoint=False):
    size = block.shape[0]
    real, imag = block[:, :size], block[:, size:]
    return real, imag, (real - imag if adjoint else real + imag)


def put(matrix, block, adjoint=False):
    size = block.shape[0]
    for index, part in enumerate(parts_of(block, adjoint)):
        matrix[index, :size], matrix[index, size:] = split(part)


def times_split(left, matrix, transposed=False):
    products = []
    for index, stacked in enumerate(left):
        rows, size = stacked.shape[0] // 2, matrix.shape[1] // 2
        high, low = stacked[:rows], stacked[rows:]
        if transposed:
            both = dot(stacked, matrix[index, :size], True)
            both = both[:rows] + both[rows:] + dot(high, matrix[index, size:], True)
        else:
            both = dot(jnp.concatenate([high, high], axis=1), matrix[index], False)
            both += dot(low, matrix[index, :size], False)
        products.append(both)
    first, second, third = products
    if transposed:
        return jnp.concatenate([first + second, third - first + second], axis=1)
    return jnp.concatenate([first - second, third - first - second], axis=1)


def times(block, matrix, transposed=False):
    left = [jnp.concatenate(split(part), axis=0) for part in parts_of(block)]
    return times_split(left, matrix, transposed)


def row_form(pair):
    return jnp.concatenate([pair[0], pair[1]], axis=1)


def adjoint_row(pair):
    return jnp.concatenate([jnp.transpose(pair[0]), -jnp.transpose(pair[1])], axis=1)


def expand(pattern, size):
    blocks = pattern.shape[0]
    tile = size // blocks
    rows = lax.broadcasted_iota(jnp.int32, (size, blocks), 0)
    first = lax.broadcasted_iota(jnp.int32, (size, blocks), 1) * tile
    member = jnp.where((rows >= first) & (rows < first + tile), 1.0, 0.0).astype(HALF)
    tall = dot(member, pattern.astype(F32).astype(HALF), False)
    return dot(tall.astype(HALF), member, True)


def couple(coupling, pattern):
    mask = expand(pattern[...], coupling.shape[-1])
    return jnp.concatenate([coupling[0] * mask, coupling[1] * mask], axis=1)


def trailing():
    return lax.rem(lax.axis_index("energy") + LEADING, 2)


def shape(rows, columns, dtype=F32, *lead):
    return jax.ShapeDtypeStruct(lead + (rows, columns), dtype)


def matrices(number, size):
    return [pltpu.VMEM((3, 2 * size, size), HALF)] * number


def call(
    kernel, outs, scratch, args, specs=None, out_specs=None, aliases=None, flops=0, name=None, limit=40
):
    made = pl.pallas_call(
        kernel,
        out_shape=outs,
        in_specs=specs or [VMEM] * len(args),
        out_specs=out_specs or [VMEM] * len(outs),
        input_output_aliases=aliases or {},
        scratch_shapes=scratch,
        compiler_params=pltpu.CompilerParams(vmem_limit_bytes=int(limit * 2**20)),
        cost_estimate=pl.CostEstimate(flops=flops, bytes_accessed=2**20, transcendentals=0),
        name=name,
    )(*args)
    return list(made)


class Loads:
    def __init__(self, args, targets, sems, couplers=(0, 1), blocks=True):
        order = [(3, 1), (0, 0), (1, 0), (2, 1), (1, 1), (0, 1), (3, 0), (2, 0)]
        self.copies = {
            (which, slab): pltpu.make_async_copy(
                args[which].at[slab], targets[which].at[slab], sems.at[index]
            )
            for index, (which, slab) in enumerate(order)
            if (blocks if which < 2 else slab in couplers)
        }
        self.targets = targets
        for copy in self.copies.values():
            copy.start()

    def get(self, which, slab):
        self.copies[which, slab].wait()
        return self.targets[which].at[slab]

    def green(self, slab):
        return row_form(self.get(0, slab))

    def sigma(self, slab):
        return row_form(self.get(1, slab))

    def coupler(self, slab):
        tiles = self.get(3, slab)
        return couple(self.get(2, slab), tiles)


def load_scratch(size, blocks):
    return [
        pltpu.VMEM((2, 2, size, size), F32),
        pltpu.VMEM((2, 2, size, size), F32),
        pltpu.VMEM((2, 2, size, size), F32),
        pltpu.VMEM((2, blocks, blocks), jnp.int32),
        pltpu.SemaphoreType.DMA((8,)),
    ]


def left_sources(loads, whole, source, coupler_out, m_a, m_b, m_c):
    first = loads.green(0)
    put(m_b, first)
    put(m_a, loads.sigma(0))
    coupler = loads.coupler(1)
    put(m_c, coupler, True)
    if coupler_out is not None:
        coupler_out[...] = coupler
    made = first + times(times(first, m_a), m_b)
    if source is not None:
        source[...] = made
    sigma, second = loads.sigma(1), loads.green(1)
    put(m_a, made)
    put(m_b, second)
    inner = sigma + times(times(coupler, m_a), m_c, True)
    put(m_a, inner)
    whole[...] = second + times(times(second, m_a), m_b)
    return first, second


def source_kernel(green, sigma, coupling, pattern, whole, *scratch):
    @pl.when(lax.axis_index("slab") == 0)
    def _():
        loads = Loads((green, sigma, coupling, pattern), scratch[:4], scratch[4], (1,))
        left_sources(loads, whole, None, None, *scratch[5:])

    @pl.when((lax.axis_index("slab") > 0) & (trailing() == 1))
    def _():
        loads = Loads((green, sigma, coupling, pattern), scratch[:4], scratch[4], (0,), False)
        whole[...] = loads.coupler(0)


def map_kernel(
    green, sigma, coupling, pattern,
    whole, source, coupler, opening, lead, tail, forward, backward, *scratch,
):
    m_a, m_b, m_c = scratch[5:]
    loads = Loads((green, sigma, coupling, pattern), scratch[:4], scratch[4])
    first, second = left_sources(loads, whole, source, coupler, m_a, m_b, m_c)
    before = loads.coupler(0)

    @pl.when(lax.axis_index("slab") > 0)
    def _():
        opening[...] = before
        put(m_a, first)
        size = before.shape[0]
        behind = times(adjoint_row((before[:, :size], before[:, size:])), m_a)
        backward[...] = behind
        put(tail, times(times(behind, m_c, True), m_b))
        put(m_a, before)
        ahead = times(first, m_a)
        forward[...] = ahead
        put(m_a, ahead)
        put(m_c, coupler[...])
        put(lead, times(times(second, m_c), m_a))


def right_terms(first, last, coupler, m_coupler, m_first, m_last, m_upper):
    put(m_coupler, coupler, True)
    put(m_last, last)
    through = times(times(first, m_coupler, True), m_last)
    put(m_first, first)
    put(m_upper, times(coupler, m_first))
    return through, first + times(through, m_upper)


def prepare_kernel(count, *refs):
    arrived, wholes = refs[: count - 1], refs[count - 1 : 2 * count - 2]
    refs = refs[2 * count - 2 :]
    start_whole, source, forward, backward, coupler = refs[:5]
    followings = refs[5:7]
    lead, tail, constant, last_lead, last_tail = refs[8:13]
    first_v, last_v, m_a, m_b, m_c, m_d = refs[13:]
    place = lax.axis_index("slab")

    @pl.when(place == 0)
    def _():
        first_v[...] = source[...]
        last_v[...] = start_whole[...]

    for turn in range(count - 1):
        @pl.when((place > 0) & (place == turn + 1 - trailing()))
        def _(turn=turn):
            last_v[...] = wholes[turn][...]
            put(m_a, arrived[turn][...])

    @pl.when((place > 0) & (place < count - 1))
    def _():
        put(m_b, backward[...])
        first_v[...] = source[...] + times(times(forward[...], m_a), m_b)

    @pl.when(place < count - 1)
    def _():
        first, last = first_v[...], last_v[...]
        through, joined = right_terms(first, last, coupler[...], m_a, m_b, m_c, m_d)
        constant[...] = joined
        next_coupler = jnp.where(trailing() == 0, followings[0][...], followings[1][...])
        put(m_a, next_coupler, True)
        put(lead, times(through, m_a, True))
        put(last_lead, times(last, m_a, True))
        behind = times(next_coupler, m_c)
        put(last_tail, behind)
        put(tail, times(behind, m_d))


def apply_map(mapping, m_x):
    lead, tail, constant = mapping
    ahead = [lead[index] for index in range(3)]
    return constant[...] + times(times_split(ahead, m_x), tail)


def relay_kernel(step, count, lefts, rights, *refs):
    refs = list(refs)
    place = lax.axis_index("slab")
    turn = step - trailing()
    is_left = (turn >= 0) & (turn <= count - 2) & (place == turn + 1)
    is_right = (turn >= count - 1) & (place == 2 * count - 3 - turn)
    closing = lefts and step >= count - 2
    arrived = refs.pop(0)
    left_map = [refs.pop(0) for _ in range(3)] if lefts else None
    right_map = [refs.pop(0) for _ in range(3)] if rights else None
    if closing:
        forward, backward, source, coupler = [refs.pop(0) for _ in range(4)]
    out = refs.pop(0)
    if closing:
        end, m_x, m_a, m_b, m_c = refs
    else:
        (m_x,) = refs

    if step == 0:
        @pl.when(place == 0)
        def _():
            out[...] = left_map[2][...]

    if lefts:
        @pl.when(is_left & (place < count - 1) if closing else is_left)
        def _():
            put(m_x, arrived[...])
            out[...] = apply_map(left_map, m_x)

    if closing:
        @pl.when(is_left & (place == count - 1))
        def _():
            put(m_x, arrived[...])
            last = apply_map(left_map, m_x)
            end[...] = last
            put(m_a, backward[...])
            first = source[...] + times(times(forward[...], m_x), m_a)
            _, joined = right_terms(first, last, coupler[...], m_a, m_b, m_c, m_x)
            out[...] = joined

    if rights:
        @pl.when(is_right & (place > 0))
        def _():
            put(m_x, arrived[...])
            out[...] = apply_map(right_map, m_x)


def last_kernel(count, *refs):
    refs = list(refs)
    arrived = [refs.pop(0) for _ in range(count)]
    ends = [refs.pop(0) for _ in range(2)]
    last_lead, last_tail, whole_start = [refs.pop(0) for _ in range(3)]
    wholes = [refs.pop(0) for _ in range(count - 1)]
    block, *parcels, m_x = refs
    place = lax.axis_index("slab")
    core = trailing()
    is_last = place == count - 1

    for index in range(count):
        @pl.when(jnp.logical_not(is_last) & (2 * count - 3 - place + core == count - 1 + index))
        def _(index=index):
            put(m_x, arrived[index][...])

    for index in range(2):
        @pl.when(is_last & (core == index))
        def _(index=index):
            block[...] = ends[index][...]

    @pl.when(place == 0)
    def _():
        block[...] = apply_map((last_lead, last_tail, whole_start), m_x)

    for index in range(count - 1):
        @pl.when((place > 0) & jnp.logical_not(is_last) & (place - 1 + core == index))
        def _(index=index):
            block[...] = apply_map((last_lead, last_tail, wholes[index]), m_x)

    pack(block, parcels)


def first_kernel(count, *refs):
    arrived, outs = refs[:2], refs[2 : count + 2]
    right_map = refs[count + 2 : count + 5]
    block, *parcels, m_x = refs[count + 6 :]
    place, core = lax.axis_index("slab"), trailing()
    at = jnp.where(place == count - 1, count - 2 + core, 2 * count - 3 - place + core)

    for index in range(count):
        @pl.when((place > 0) & (at == count - 2 + index))
        def _(index=index):
            block[...] = outs[index][...]

    for index in range(2):
        @pl.when((place == 0) & (core == index))
        def _(index=index):
            put(m_x, arrived[index][...])

    @pl.when(place == 0)
    def _():
        block[...] = apply_map(right_map, m_x)

    pack(block, parcels)


def pack(block, parcels):
    for mask, parcel in enumerate(parcels):
        parcel[...] = block[share(mask, parcel.shape[0]), :]


def unpack_kernel(*refs):
    blocks, out = refs[:2], refs[2]
    size = out.shape[-1]
    for slab, block in enumerate(blocks):
        for part in range(2):
            out[slab, part] = block[:, part * size : (part + 1) * size]


def share(mask, rows):
    chip = lax.shift_right_logical(lax.axis_index("energy"), 1)
    return pl.ds(pl.multiple_of(lax.bitwise_xor(chip, mask) * rows, rows), rows)


def far_first(chips):
    return sorted(range(chips), key=lambda mask: -bin(mask).count("1"))


def weight_kernel(chips, weights, tiles):
    energy = lax.axis_index("energy")
    core = lax.rem(energy, 2)
    sources = [lax.bitwise_xor(energy, 2 * mask) for mask in range(chips)]
    for mask in range(chips):
        for side, target in enumerate((sources[mask], sources[mask] + 1 - 2 * core)):
            for index in range(chips):
                weight = weights[target, sources[index]]
                tiles[side, mask, index] = jnp.full(tiles.shape[3:], weight, F32)


def mix_kernel(chips, tiles, *refs):
    parcels, outs = dict(zip(far_first(chips), refs[:chips])), refs[chips:]
    rows, columns = parcels[0].shape
    step, width = tiles.shape[3:]
    for row in range(0, rows, step):
        where = slice(row, row + step)
        values = [parcels[mask][where] for mask in range(chips)]
        for side, out in enumerate(outs):
            for mask in range(chips):
                total = None
                for index in range(chips):
                    weight = jnp.concatenate([tiles[side, mask, index]] * (columns // width), axis=1)
                    term = weight * values[index]
                    total = term if total is None else total + term
                out[mask, where] = total


def sum_kernel(chips, mine, other, *outs):
    for mask in range(chips):
        outs[mask][...] = mine[mask] + other[mask]


def place_kernel(chips, slab, *refs):
    parcels, scattering, sems = refs[:chips], refs[-2], refs[-1]
    size = scattering.shape[-1]
    copies = []
    for index, (mask, parcel) in enumerate(zip(far_first(chips), parcels)):
        for part in range(2):
            copies.append(
                pltpu.make_async_copy(
                    parcel.at[:, pl.ds(part * size, size)],
                    scattering.at[slab, part, share(mask, parcel.shape[0]), :],
                    sems.at[index, part],
                )
            )
            copies[-1].start()
    for copy in copies:
        copy.wait()


def mode_weights(targets, sources, offsets, emission, absorption):
    spacing = sources[None, :, None] - targets[:, None, None]
    emitted = jnp.where(
        spacing == -offsets[None, None, :],
        emission[None, None, :],
        jnp.zeros_like(emission)[None, None, :],
    )
    absorbed = jnp.where(
        spacing == offsets[None, None, :],
        absorption[None, None, :],
        jnp.zeros_like(absorption)[None, None, :],
    )
    return jnp.sum(emitted + absorbed, axis=-1)


def relay_pairs(step, energies, count):
    pairs = []
    for energy in range(energies):
        turn = step - (energy + LEADING) % 2
        if turn < 0:
            pairs += [(energy * count + i, energy * count + i - 1) for i in range(1, count)]
        if 0 <= turn <= count - 2:
            ends = (turn, turn + 1)
        elif count - 1 <= turn <= 2 * count - 3:
            ends = (2 * count - 2 - turn, 2 * count - 3 - turn)
        else:
            continue
        pairs.append(tuple(energy * count + end for end in ends))
    return pairs


def shards(energies, count, free_green, self_energy, coupling, pattern, offsets, emission, absorption):
    size, blocks = free_green.shape[-1], pattern.shape[-1]
    args = (free_green[0], self_energy[0], coupling, pattern)
    row = shape(size, 2 * size)
    factor = shape(2 * size, size, HALF, 3)
    row_v = pltpu.VMEM(row.shape, F32)
    product = 24 * size**3
    loading = load_scratch(size, blocks) + matrices(3, size)

    def relay(step, value):
        return lax.ppermute(value, ("energy", "slab"), relay_pairs(step, energies, count))

    begun = call(
        source_kernel,
        [row],
        loading,
        args,
        [HBM] * 4,
        flops=6 * product,
        name="source",
        limit=53,
    )
    arrived, outs, ends = [relay(0, begun[0])], [], []
    whole, source, coupler, opening, left_lead, left_tail, forward, backward = call(
        map_kernel,
        [row] * 4 + [factor, factor, row, row],
        loading,
        args,
        [HBM] * 4,
        flops=12 * product,
        name="left_maps",
        limit=48.6,
    )
    left_map = [left_lead, left_tail, whole]
    chips = energies // 2
    everyone = jnp.arange(energies, dtype=jnp.int32)
    weights = mode_weights(everyone, everyone, offsets, emission, absorption)
    (tiles,) = call(
        functools.partial(weight_kernel, chips),
        [shape(8, 128, F32, 2, chips, chips)],
        [],
        [weights],
        [SMEM],
        name="weights",
    )
    right_map = None
    for step in range(2 * count - 2):
        lefts, rights = step <= count - 1, step >= count - 1
        closing = lefts and step >= count - 2
        args = [arrived[step]]
        if lefts:
            args += left_map
        if rights:
            args += right_map[:3]
        if closing:
            args += [forward, backward, source, coupler]
        made = call(
            functools.partial(relay_kernel, step, count, lefts, rights),
            [row] * (2 if closing else 1),
            matrices(4 if closing else 1, size),
            args,
            flops=2 * product,
            name="relay",
        )
        outs.append(made[0])
        ends += made[1:]
        arrived.append(relay(step + 1, made[0]))
        if step == 0:
            down = [
                (energy * count + i, energy * count + i - 1)
                for energy in range(energies)
                for i in range(1, count)
                if (energy + LEADING) % 2 == 0
            ]
            following = lax.ppermute(opening, ("energy", "slab"), down)
        if step == count - 2:
            args = arrived[: count - 1] + outs[: count - 1]
            args += [whole, source, forward, backward, coupler, following, arrived[0], tiles]
            right_map = call(
                functools.partial(prepare_kernel, count),
                [factor, factor, row, factor, factor],
                [row_v] * 2 + matrices(4, size),
                args,
                flops=10 * product,
                name="right_maps",
            )
    parcel = shape(size // chips, 2 * size)
    blocks, parcels = [None, None], [None, None]
    args = arrived[count - 1 :] + ends + right_map[3:] + [whole] + outs[: count - 1]
    blocks[1], *parcels[1] = call(
        functools.partial(last_kernel, count),
        [row] + [parcel] * chips,
        matrices(1, size),
        args,
        flops=2 * product,
        name="second_slab",
    )
    args = arrived[-2:] + outs[count - 2 :] + right_map[:3] + blocks[1:]
    blocks[0], *parcels[0] = call(
        functools.partial(first_kernel, count),
        [row] + [parcel] * chips,
        matrices(1, size),
        args,
        flops=2 * product,
        name="first_slab",
    )
    (retarded,) = call(
        unpack_kernel, [shape(size, size, F32, 2, 2)], [], blocks, name="retarded"
    )

    masks = far_first(chips)

    def exchange(values):
        sent = list(values)
        for mask in masks[:-1]:
            pairs = [(i, i ^ (2 * mask)) for i in range(energies)]
            sent[mask] = lax.ppermute(values[mask], "energy", pairs)
        return [sent[mask] for mask in masks]

    partial = shape(size // chips, 2 * size, F32, chips)
    sums = [None, None]
    received = exchange(parcels[1])
    for slab in (1, 0):
        if slab == 0 and chips > 1:
            last = masks[-2]
            parcels[0][last], _ = lax.optimization_barrier((parcels[0][last], received[0]))
            received = exchange(parcels[0])
        mine, other = call(
            functools.partial(mix_kernel, chips),
            [partial] * 2,
            [],
            [tiles] + received,
            flops=product // 8,
            name="mix",
        )
        other = lax.ppermute(other, "energy", [(i, i ^ 1) for i in range(energies)])
        sums[slab] = call(
            functools.partial(sum_kernel, chips), [parcel] * chips, [], [mine, other], name="sum"
        )
    returned = [exchange(sums[slab]) for slab in (1, 0)][::-1]
    scattering = []
    for slab in (1, 0):
        scattering = call(
            functools.partial(place_kernel, chips, slab),
            [shape(size, size, F32, 2, 2)],
            [pltpu.SemaphoreType.DMA((chips, 2))],
            returned[slab] + scattering,
            [VMEM] * chips + [HBM] * len(scattering),
            [HBM],
            aliases={chips: 0} if scattering else {},
            name="scattering",
        )
    (scattering,) = scattering
    return (retarded[None], scattering[None])


def solution(mesh):
    blocks = P("energy", "slab", None, None, None)
    in_specs = (blocks, blocks, P("slab", None, None, None), P("slab", None, None), P(), P(), P())
    body = functools.partial(shards, mesh.shape["energy"], mesh.shape["slab"])
    return jax.shard_map(
        body, mesh=mesh, in_specs=in_specs, out_specs=(blocks, blocks), check_vma=False
    )
```
